32 devices in a mesh: section: 2 (over core), expert: 4 (over z), dp: 4 (over y, x).
Axes of the slice: x: 2, y: 2, z: 4, core: 2. Of those that a mesh axis runs over, the one named last changes fastest.
Arguments:
- x_in: bfloat16 [2, 16, 64, 3584], P(None, ('expert', 'dp')), may hold values from -6 to 6
- dy_out: bfloat16 [2, 16, 64, 3584], P(None, ('expert', 'dp')), may hold values from -6 to 6
- routes: int32 [2, 2, 16, 64, 1], P('section', None, ('expert', 'dp')), may hold values from 0 to 3; in each aligned block of 64 rows (0 to 63, 64 to 127, ..., all dimensions but the last counted through in order) at most 24 rows name the same one
- gates: float32 [2, 2, 16, 64, 1], P('section', None, ('expert', 'dp')), may hold values from 0.2 to 1
- w_down: bfloat16 [2, 3584, 256], P('section'), may hold values from -0.09375 to 0.09375
- w_qk: bfloat16 [2, 256, 256], P('section'), may hold values from -0.375 to 0.375
- w_up: bfloat16 [2, 256, 3584], P('section'), may hold values from -0.375 to 0.375
- e_gate: bfloat16 [2, 4, 3584, 1024], P('section', 'expert', None, 'dp'), may hold values from -0.09375 to 0.09375
- e_up: bfloat16 [2, 4, 3584, 1024], P('section', 'expert', None, 'dp'), may hold values from -0.09375 to 0.09375
- e_down: bfloat16 [2, 4, 1024, 3584], P('section', 'expert', 'dp'), may hold values from -0.1875 to 0.1875
Outputs:
- activations: bfloat16 [2, 2, 16, 64, 3584], P('section', None, ('expert', 'dp'))
- grads_in: bfloat16 [2, 2, 16, 64, 3584], P('section', None, ('expert', 'dp'))
- g_down: float32 [2, 3584, 256], P('section', ('expert', 'dp'))
- g_qk: float32 [2, 256, 256], P('section', ('expert', 'dp'))
- g_up_t: float32 [2, 3584, 256], P('section', ('expert', 'dp'))
The draws below stay inside these ranges and needn't reach their ends.
Inputs may be any that keep to these rules, and one draw needn't show every extreme that they name: `routes`: within each sequence of one micro-batch and layer, every expert is named by at most 24 tokens, a bound that some block reaches.
All inputs are finite; a program needn't handle non-finite values.
Results may differ from the reference program's by a relative error of at most 0.035.
Values may be sent and summed in bfloat16 or wider, within the bound.
No kernel may reach another device: no remote copies, remote signals or barrier semaphores. Data moves between devices by JAX's collectives and lax.ppermute only.
A program may use at most 128 MiB of HBM per device.

```python
import math
import jax
import jax.numpy as jnp
import numpy as np
from jax import lax

D = 3584
LAT = 256
FF = 1024
SEQ = 64
MICRO = 2
TOPK = 1
EXPERTS = 4
BATCH = 16
CAP = 24
N_SECTION = 2
N_DP = 4


def shard_levels(own_key, extent, pieces, least, largest):
    def one(dim, blocks):
        heights = jax.random.uniform(jax.random.fold_in(jax.random.fold_in(own_key, 6), dim), (blocks,), jnp.float32, least / len(pieces), largest / len(pieces))
        return jnp.repeat(jnp.exp(heights), extent[dim] // blocks).reshape((-1,) + (1,) * (len(extent) - dim - 1))

    factor_of = one(*pieces[0])
    for cut in pieces[1:]:
        factor_of = factor_of * one(*cut)
    return factor_of


def shared_out(rng, own, number, rows, count, top, reach, skew):
    ranking = jax.random.permutation(rng, count)
    crowded, usual = shares(count, rows * top, reach, skew, True), shares(count, rows * top, reach, skew, False)
    places = jnp.arange(count)

    def named(sizes, rotation):
        used = int((sizes > 0).sum())
        fixed = max(1, used // 4)
        shifted = fixed + (places - fixed + rotation * (used - fixed)) % max(1, count - fixed)
        return jnp.zeros((count,), jnp.int32).at[ranking[jnp.where(places < fixed, places, shifted)]].set(jnp.asarray(sizes, jnp.int32))

    sizes = jnp.where(number % 4 == 0, named(crowded, number // 4), named(usual, number - number // 4 - 1))
    mixed = jax.random.permutation(jax.random.fold_in(own, 3), count)
    giver, taker = mixed[0:count // 2 * 2:2], mixed[1:count // 2 * 2:2]
    slack = jnp.minimum(sizes[giver] - 1, reach - sizes[taker]) // 2
    slack = jnp.where((giver == ranking[0]) | (taker == ranking[0]) | (sizes[taker] == 0), 0, jnp.maximum(slack, 0))
    shifted = jax.random.randint(jax.random.fold_in(own, 4), (count // 2,), 0, 1 << 20) % (slack + 1)
    sizes = sizes.at[giver].add(-shifted).at[taker].add(shifted)
    items = jnp.searchsorted(jnp.cumsum(sizes), jnp.arange(rows * top), side="right").astype(jnp.int32)
    listing = items.reshape(top, rows).T
    listing = listing[jax.random.permutation(jax.random.fold_in(own, 1), rows)]
    rotation = jax.random.randint(jax.random.fold_in(own, 2), (rows, 1), 0, top)
    return jnp.take_along_axis(listing, (jnp.arange(top)[None, :] + rotation) % top, axis=1)


def shares(count, total, limit, skew, full):
    loads = [(1 << 20) // math.isqrt(rank ** skew) + 1 for rank in range(1, count + 1)]
    largest = limit if full else min(limit, max(-(-total // count), total * loads[0] // sum(loads)))
    least = 1 if total - largest >= count - 1 else 0
    given, spare = [largest] + [least] * (count - 1), total - largest - least * (count - 1)
    while spare > 0:
        free = [i for i in range(1, count) if given[i] < largest] or [i for i in range(1, count) if given[i] < limit]
        pool, left = sum([loads[i] for i in free]), spare
        for i in free:
            more = min(limit - given[i], max(1, left * loads[i] // pool), spare)
            given[i] = given[i] + more
            spare = spare - more
    return np.array(given)


def scatter_about(rng, shape, width, reach, pieces=(), held_as=jnp.bfloat16):
    array = width * jax.random.normal(rng, shape, jnp.float32)
    if pieces:
        array = array * shard_levels(rng, shape, pieces, -0.22, 0.18)
    return jnp.clip(array, -reach, reach).astype(held_as)


def setup_inputs(seed: int = 0) -> dict:
    keys = jax.random.split(jax.random.key(seed), 11)
    x_in = scatter_about(keys[0], (MICRO, BATCH, SEQ, D), 1.0, 6.0, ((1, 16),))
    dy_out = scatter_about(keys[1], (MICRO, BATCH, SEQ, D), 1.0, 6.0, ((1, 16),))
    routes_keys = jax.random.split(jax.random.fold_in(keys[2], 1), N_SECTION * MICRO * BATCH * SEQ // SEQ)
    routes_turns = jax.random.permutation(jax.random.fold_in(keys[2], 3), N_SECTION * MICRO * BATCH * SEQ // SEQ)
    routes = jax.vmap(lambda own, number: shared_out(jax.random.fold_in(keys[2], 2), own, number, SEQ, EXPERTS, TOPK, CAP, 2))(routes_keys, routes_turns).reshape((N_SECTION, MICRO, BATCH, SEQ, TOPK))
    gates = jnp.clip(0.2 + 0.8 * jax.random.uniform(keys[3], (N_SECTION, MICRO, BATCH, SEQ, TOPK), jnp.float32) ** shard_levels(keys[3], (N_SECTION, MICRO, BATCH, SEQ, TOPK), ((0, 2), (2, 16)), -0.2, 0.2), 0.2, 1.0)
    w_down = scatter_about(keys[4], (N_SECTION, D, LAT), D ** -0.5, 0.09375, ((0, 2),))
    w_qk = scatter_about(keys[5], (N_SECTION, LAT, LAT), LAT ** -0.5, 0.375, ((0, 2),))
    w_up = scatter_about(keys[6], (N_SECTION, LAT, D), LAT ** -0.5, 0.375, ((0, 2),))
    e_gate = scatter_about(keys[7], (N_SECTION, EXPERTS, D, FF), D ** -0.5, 0.09375, ((0, 2), (1, 4), (3, 4)))
    e_up = scatter_about(keys[8], (N_SECTION, EXPERTS, D, FF), D ** -0.5, 0.09375, ((0, 2), (1, 4), (3, 4)))
    e_down = scatter_about(keys[9], (N_SECTION, EXPERTS, FF, D), FF ** -0.5, 0.1875, ((0, 2), (1, 4), (2, 4)))
    return dict(x_in=x_in, dy_out=dy_out, routes=routes, gates=gates, w_down=w_down, w_qk=w_qk, w_up=w_up, e_gate=e_gate, e_up=e_up, e_down=e_down)


epsilon = 1e-06

def times_t(left, right):
    return lax.dot_general(left, right, (((left.ndim - 1,), (right.ndim - 1,)), ((), ())), preferred_element_type=jnp.float32)

def t_times(left, right):
    return lax.dot_general(left, right, (((0,), (0,)), ((), ())), preferred_element_type=jnp.float32)

def rms_norm(values):
    inv_rms = lax.rsqrt(lax.optimization_barrier(jnp.mean(values * values, axis=-1, keepdims=True)) + epsilon)
    return (values * inv_rms, inv_rms)

def rms_back(normed, inv_rms, upstream):
    return inv_rms * (upstream - normed * lax.optimization_barrier(jnp.mean(upstream * normed, axis=-1, keepdims=True)))

def silu_parts(gate_pre):
    sigmoid = jax.nn.sigmoid(gate_pre)
    return (gate_pre * sigmoid, sigmoid * (1.0 + gate_pre * (1.0 - sigmoid)))

def attend_forward(inputs, w_down, w_qk, w_up):
    normed, inv_rms = rms_norm(inputs.astype(jnp.float32))
    normed_b = normed.astype(jnp.bfloat16)
    latent = jnp.dot(normed_b, w_down, preferred_element_type=jnp.float32).astype(jnp.bfloat16)
    queries = jnp.dot(latent, w_qk, preferred_element_type=jnp.float32).astype(jnp.bfloat16)
    length = inputs.shape[0]
    scale_qk = latent.shape[1] ** (-0.5)
    scores = times_t(queries, latent) * scale_qk
    causal = lax.broadcasted_iota(jnp.int32, (length, length), 0) >= lax.broadcasted_iota(jnp.int32, (length, length), 1)
    scores = jnp.where(causal, scores, -1e+30)
    row_max = lax.optimization_barrier(jnp.max(scores, axis=-1, keepdims=True))
    exponent = jnp.exp(scores - row_max)
    attn_probs = exponent / lax.optimization_barrier(jnp.sum(exponent, axis=-1, keepdims=True))
    probs_b = attn_probs.astype(jnp.bfloat16)
    mixed_rows = jnp.dot(probs_b, latent, preferred_element_type=jnp.float32).astype(jnp.bfloat16)
    residual = (inputs.astype(jnp.float32) + jnp.dot(mixed_rows, w_up, preferred_element_type=jnp.float32)).astype(jnp.bfloat16)
    return (residual, (normed, inv_rms, normed_b, latent, queries, attn_probs, probs_b, mixed_rows))

def attend_backward(kept, upstream, w_down, w_qk, w_up):
    normed, inv_rms, normed_b, latent, queries, attn_probs, probs_b, mixed_rows = kept
    scale_qk = latent.shape[1] ** (-0.5)
    upstream_b = upstream.astype(jnp.bfloat16)
    d_mixed = times_t(upstream_b, w_up).astype(jnp.bfloat16)
    g_up_t = t_times(upstream_b, mixed_rows)
    d_probs = times_t(d_mixed, latent)
    d_scores = (attn_probs * (d_probs - lax.optimization_barrier(jnp.sum(d_probs * attn_probs, axis=-1, keepdims=True))) * scale_qk).astype(jnp.bfloat16)
    d_queries = jnp.dot(d_scores, latent, preferred_element_type=jnp.float32).astype(jnp.bfloat16)
    g_qk = t_times(latent, d_queries)
    d_latent = (t_times(probs_b, d_mixed) + t_times(d_scores, queries) + times_t(d_queries, w_qk)).astype(jnp.bfloat16)
    g_down = t_times(normed_b, d_latent)
    d_normed = times_t(d_latent, w_down)
    return (upstream + rms_back(normed, inv_rms, d_normed), g_down, g_qk, g_up_t)

def slot_table(route_ids, experts, capacity):
    one_hot = (route_ids[:, None] == jnp.arange(experts, dtype=jnp.int32)[None, :]).astype(jnp.int32)
    order_rank = lax.optimization_barrier(jnp.sum((jnp.cumsum(one_hot, axis=0) - one_hot) * one_hot, axis=1))
    return (route_ids * capacity + order_rank).astype(jnp.int32)

def pick_rows(table, slot_index):
    return table[slot_index]

def to_sequences(by_expert, batch_size, experts, model_width):
    return by_expert.reshape(experts, batch_size, CAP, model_width).transpose(1, 0, 2, 3).reshape(batch_size, experts * CAP, model_width)

def layer_forward(inputs, route_ids, gate_vals, w_down, w_qk, w_up, e_gate, e_up, e_down):
    batch_size, length, model_width = inputs.shape
    top_count = route_ids.shape[2]
    experts = e_gate.shape[0]
    hidden = e_gate.shape[2]
    quarters = N_DP
    split = hidden // quarters
    residual, kept_attn = jax.vmap(attend_forward, in_axes=(0, None, None, None))(inputs, w_down, w_qk, w_up)
    normed, inv_rms = rms_norm(residual.astype(jnp.float32))
    normed_b = normed.astype(jnp.bfloat16)
    slot_index = jax.vmap(slot_table, in_axes=(0, None, None))(route_ids.reshape(batch_size, length * top_count), experts, CAP)
    placement = (slot_index[:, None, :] == jnp.arange(experts * CAP, dtype=jnp.int32)[None, :, None]).astype(jnp.float32)
    rows_k = jnp.repeat(normed_b, top_count, axis=1).astype(jnp.float32)
    sent = jnp.einsum('bcs,bsd->bcd', placement, rows_k).astype(jnp.bfloat16)
    by_expert = sent.reshape(batch_size, experts, CAP, model_width).transpose(1, 0, 2, 3).reshape(experts, batch_size * CAP, model_width)

    def expert_forward(operands):
        expert_rows, gate_w, up_w, down_w = operands
        gate_pre = jnp.dot(expert_rows, gate_w, preferred_element_type=jnp.float32)
        up_pre = jnp.dot(expert_rows, up_w, preferred_element_type=jnp.float32)
        hidden_b = (silu_parts(gate_pre)[0] * up_pre).astype(jnp.bfloat16)
        row_count = expert_rows.shape[0]
        partial_value = jnp.einsum('rqf,qfd->rqd', hidden_b.reshape(row_count, quarters, split).astype(jnp.float32), down_w.reshape(quarters, split, model_width).astype(jnp.float32))
        partial_value = lax.optimization_barrier(partial_value.astype(jnp.bfloat16)).astype(jnp.float32)
        return (lax.optimization_barrier(jnp.sum(partial_value, axis=1)), gate_pre, up_pre)
    summed, gate_pre, up_pre = lax.map(expert_forward, (by_expert, e_gate, e_up, e_down))
    summed = to_sequences(summed, batch_size, experts, model_width)
    picked = jax.vmap(pick_rows)(summed, slot_index)
    mixture = lax.optimization_barrier(jnp.sum(picked.reshape(batch_size, length, top_count, model_width) * gate_vals[..., None], axis=2))
    output = (residual.astype(jnp.float32) + mixture).astype(jnp.bfloat16)
    return (output, (kept_attn, normed, inv_rms, slot_index, placement, gate_pre, up_pre))

def layer_backward(kept, upstream, gate_vals, w_down, w_qk, w_up, e_gate, e_up, e_down):
    kept_attn, normed, inv_rms, slot_index, placement, gate_pre, up_pre = kept
    batch_size, length, model_width = upstream.shape
    top_count = gate_vals.shape[2]
    experts = e_gate.shape[0]
    hidden = e_gate.shape[2]
    quarters = N_DP
    split = hidden // quarters
    scaled = (upstream[:, :, None, :] * gate_vals[..., None]).reshape(batch_size, length * top_count, model_width).astype(jnp.bfloat16)
    sent = jnp.einsum('bcs,bsd->bcd', placement, scaled.astype(jnp.float32)).astype(jnp.bfloat16)
    by_expert = sent.reshape(batch_size, experts, CAP, model_width).transpose(1, 0, 2, 3).reshape(experts, batch_size * CAP, model_width)

    def expert_backward(operands):
        expert_rows, gate_in, up_in, gate_w, up_w, down_w = operands
        d_hidden = times_t(expert_rows, down_w)
        activated, slope = silu_parts(gate_in)
        d_gate = (d_hidden * up_in * slope).astype(jnp.bfloat16)
        d_up = (d_hidden * activated).astype(jnp.bfloat16)
        row_count = expert_rows.shape[0]
        returned = jnp.einsum('rqf,dqf->rqd', d_gate.reshape(row_count, quarters, split).astype(jnp.float32), gate_w.reshape(model_width, quarters, split).astype(jnp.float32))
        returned = returned + jnp.einsum('rqf,dqf->rqd', d_up.reshape(row_count, quarters, split).astype(jnp.float32), up_w.reshape(model_width, quarters, split).astype(jnp.float32))
        returned = lax.optimization_barrier(returned.astype(jnp.bfloat16)).astype(jnp.float32)
        return lax.optimization_barrier(jnp.sum(returned, axis=1))
    summed = lax.map(expert_backward, (by_expert, gate_pre, up_pre, e_gate, e_up, e_down))
    summed = to_sequences(summed, batch_size, experts, model_width)
    picked = jax.vmap(pick_rows)(summed, slot_index)
    d_normed = lax.optimization_barrier(jnp.sum(picked.reshape(batch_size, length, top_count, model_width), axis=2))
    d_resid = upstream + rms_back(normed, inv_rms, d_normed)
    d_input, g_down, g_qk, g_up_t = jax.vmap(attend_backward, in_axes=(0, 0, None, None, None))(kept_attn, d_resid, w_down, w_qk, w_up)
    return (d_input, lax.optimization_barrier(jnp.sum(g_down, axis=0)), lax.optimization_barrier(jnp.sum(g_qk, axis=0)), lax.optimization_barrier(jnp.sum(g_up_t, axis=0)))

def reference(x_in, dy_out, routes, gates, w_down, w_qk, w_up, e_gate, e_up, e_down):
    layer_in = x_in
    activations = []
    kept_all = []
    for section_index in range(N_SECTION):
        outputs = []
        kept_section = []
        for micro_idx in range(MICRO):
            output, kept = layer_forward(layer_in[micro_idx], routes[section_index, micro_idx], gates[section_index, micro_idx], w_down[section_index], w_qk[section_index], w_up[section_index], e_gate[section_index], e_up[section_index], e_down[section_index])
            outputs.append(output)
            kept_section.append(kept)
        layer_in = jnp.stack(outputs)
        activations.append(layer_in)
        kept_all.append(kept_section)
    upstream_all = dy_out.astype(jnp.float32)
    grads_in = [None] * N_SECTION
    downs = [None] * N_SECTION
    querys = [None] * N_SECTION
    uppers = [None] * N_SECTION
    for section_index in reversed(range(N_SECTION)):
        d_list = []
        total_down = jnp.zeros((D, LAT), jnp.float32)
        total_qk = jnp.zeros((LAT, LAT), jnp.float32)
        total_up = jnp.zeros((D, LAT), jnp.float32)
        for micro_idx in range(MICRO):
            d_input, g_down, g_qk, g_up_t = layer_backward(kept_all[section_index][micro_idx], upstream_all[micro_idx], gates[section_index, micro_idx], w_down[section_index], w_qk[section_index], w_up[section_index], e_gate[section_index], e_up[section_index], e_down[section_index])
            d_list.append(d_input.astype(jnp.bfloat16))
            total_down = total_down + g_down
            total_qk = total_qk + g_qk
            total_up = total_up + g_up_t
        grads_in[section_index] = jnp.stack(d_list)
        downs[section_index] = total_down
        querys[section_index] = total_qk
        uppers[section_index] = total_up
        upstream_all = grads_in[section_index].astype(jnp.float32)
    return (jnp.stack(activations), jnp.stack(grads_in), jnp.stack(downs), jnp.stack(querys), jnp.stack(uppers))
```

```python
import jax
import jax.numpy as jnp
from jax import lax
from jax.sharding import PartitionSpec as P

epsilon = 1e-06
AXES = ("section", "expert", "dp")


def dot_f32(left, right):
    return jnp.dot(left, right, preferred_element_type=jnp.float32)


def times_t(left, right):
    return lax.dot_general(
        left,
        right,
        (((left.ndim - 1,), (right.ndim - 1,)), ((), ())),
        preferred_element_type=jnp.float32,
    )


def t_times(left, right):
    return lax.dot_general(
        left, right, (((0,), (0,)), ((), ())), preferred_element_type=jnp.float32
    )


def batched(spec, left, right):
    return jnp.einsum(spec, left, right, preferred_element_type=jnp.float32)


def rms_norm(values):
    inv_rms = lax.rsqrt(jnp.mean(values * values, axis=-1, keepdims=True) + epsilon)
    return (values * inv_rms, inv_rms)


def rms_back(normed, inv_rms, upstream):
    return inv_rms * (upstream - normed * jnp.mean(upstream * normed, axis=-1, keepdims=True))


def silu_parts(gate_pre):
    sigmoid = jax.nn.sigmoid(gate_pre)
    return (gate_pre * sigmoid, sigmoid * (1.0 + gate_pre * (1.0 - sigmoid)))


def after(values, *first):
    return lax.optimization_barrier((values, first))[0]


class Links:
    def __init__(self):
        self.sections, self.experts, self.quarters = [lax.axis_size(a) for a in AXES]
        self.section, self.expert, self.quarter = [lax.axis_index(a) for a in AXES]
        self.pairwise = self.experts <= 8

    def move(self, x, sections, section_bit=0, expert_bits=0, quarter_bits=0):
        def number(s, e, d):
            return (s * self.experts + e) * self.quarters + d

        pairs = [
            (number(s, e, d), number(s ^ section_bit, e ^ expert_bits, d ^ quarter_bits))
            for s in sections
            for e in range(self.experts)
            for d in range(self.quarters)
        ]
        return lax.ppermute(x, AXES, pairs)

    def relative(self, expert):
        return expert ^ self.expert if self.pairwise else expert

    def exchange(self, blocks, section):
        if not self.pairwise:
            out = lax.all_to_all(jnp.stack(blocks), "expert", split_axis=0, concat_axis=0, tiled=True)
            return [out[k] for k in range(self.experts)]
        return [blocks[0]] + [
            self.move(blocks[k], (section,), expert_bits=k) for k in range(1, self.experts)
        ]

    def gather_quarters(self, shard, section):
        if self.quarters != 4:
            return [shard] + [
                self.move(shard, (section,), quarter_bits=k) for k in range(1, self.quarters)
            ]
        half = shard.shape[0] // 2
        one = self.move(shard, (section,), quarter_bits=1)
        two = self.move(shard, (section,), quarter_bits=2)
        upper = self.move(one[:half], (section,), quarter_bits=2)
        lower = self.move(two[half:], (section,), quarter_bits=1)
        return [shard, one, two, jnp.concatenate([upper, lower], axis=0)]

    def gather_rows(self, rows):
        every = tuple(range(self.sections))
        if not self.pairwise:
            return lax.all_gather(rows, ("expert", "dp"), axis=0, tiled=True)
        plane = jnp.concatenate(
            [rows] + [self.move(rows, every, quarter_bits=k) for k in range(1, self.quarters)], axis=0
        )
        return jnp.concatenate(
            [plane] + [self.move(plane, every, expert_bits=k) for k in range(1, self.experts)], axis=0
        )

    def spread(self, rows):
        length, width = rows.shape
        count = self.experts * self.quarters
        by_owner = rows.reshape(length, count, width // count).transpose(1, 0, 2)
        got = lax.all_to_all(by_owner, ("expert", "dp"), split_axis=0, concat_axis=0, tiled=True)
        got = got.reshape(self.experts, self.quarters, length, width // count)
        if self.pairwise:
            for axis, size, place in ((0, self.experts, self.expert), (1, self.quarters, self.quarter)):
                bit = 1
                while bit < size:
                    order = [k ^ bit for k in range(size)]
                    swapped = jnp.concatenate(
                        [lax.slice_in_dim(got, k, k + 1, axis=axis) for k in order], axis=axis
                    )
                    got = jnp.where((place & bit) != 0, swapped, got)
                    bit *= 2
        return got.reshape(count * length, width // count)


def attend_forward(inputs, micro, w_down, w_qk, w_up):
    normed, inv_rms = rms_norm(inputs.astype(jnp.float32))
    normed_b = normed.astype(jnp.bfloat16)
    latent = dot_f32(normed_b, w_down).astype(jnp.bfloat16)
    queries = dot_f32(latent, w_qk).astype(jnp.bfloat16)
    length = inputs.shape[0] // micro
    latent_s = latent.reshape(micro, length, -1)
    queries_s = queries.reshape(micro, length, -1)
    scores = batched("mqc,mkc->mqk", queries_s, latent_s) * latent.shape[1] ** (-0.5)
    causal = lax.broadcasted_iota(jnp.int32, (length, length), 0) >= lax.broadcasted_iota(
        jnp.int32, (length, length), 1
    )
    scores = jnp.where(causal, scores, -1e30)
    exponent = jnp.exp(scores - jnp.max(scores, axis=-1, keepdims=True))
    probs = exponent / jnp.sum(exponent, axis=-1, keepdims=True)
    probs_b = probs.astype(jnp.bfloat16)
    mixed = batched("mqk,mkc->mqc", probs_b, latent_s).astype(jnp.bfloat16)
    mixed = mixed.reshape(micro * length, -1)
    residual = (inputs.astype(jnp.float32) + dot_f32(mixed, w_up)).astype(jnp.bfloat16)
    return residual, (inputs, inv_rms, normed_b, latent, queries, probs, mixed)


def attend_backward(kept, micro, upstream, w_down, w_qk, w_up):
    inputs, inv_rms, normed_b, latent, queries, probs, mixed = kept
    rows = latent.shape[0]

    def by_sequence(values):
        return values.reshape(micro, rows // micro, -1)

    upstream_b = upstream.astype(jnp.bfloat16)
    d_mixed = by_sequence(times_t(upstream_b, w_up).astype(jnp.bfloat16))
    latent_s, queries_s = by_sequence(latent), by_sequence(queries)
    d_probs = batched("mqc,mkc->mqk", d_mixed, latent_s)
    d_scores = (
        probs
        * (d_probs - jnp.sum(d_probs * probs, axis=-1, keepdims=True))
        * latent.shape[1] ** (-0.5)
    ).astype(jnp.bfloat16)
    d_queries = batched("mqk,mkc->mqc", d_scores, latent_s).astype(jnp.bfloat16)
    d_queries = d_queries.reshape(rows, -1)
    d_latent = (
        batched("mqk,mqc->mkc", probs.astype(jnp.bfloat16), d_mixed)
        + batched("mqk,mqc->mkc", d_scores, queries_s)
    ).reshape(rows, -1) + times_t(d_queries, w_qk)
    d_latent = d_latent.astype(jnp.bfloat16)
    d_normed = times_t(d_latent, w_down)
    normed = inputs.astype(jnp.float32) * inv_rms
    d_input = (upstream + rms_back(normed, inv_rms, d_normed)).astype(jnp.bfloat16)
    return d_input, (upstream_b, d_latent, d_queries)


def placements(links, routes, capacity):
    micro, length = routes.shape
    earlier = lax.broadcasted_iota(jnp.int32, (length, length), 0) > lax.broadcasted_iota(
        jnp.int32, (length, length), 1
    )
    same = routes[:, :, None] == routes[:, None, :]
    rank = jnp.sum((same & earlier).astype(jnp.int32), axis=2)
    slot = jnp.arange(micro, dtype=jnp.int32)[:, None] * capacity + rank
    slot = slot.reshape(-1)
    away = links.relative(routes).reshape(-1)
    slots = jnp.arange(micro * capacity, dtype=jnp.int32)
    return [
        ((slot[None, :] == slots[:, None]) & (away == k)[None, :]).astype(jnp.bfloat16)
        for k in range(links.experts)
    ]


def dispatch(links, placed, rows, section):
    blocks = [dot_f32(p, rows).astype(jnp.bfloat16) for p in placed]
    return jnp.concatenate(links.exchange(blocks, section), axis=0)


def collect(links, placed, values, section):
    size = placed[0].shape[0]
    blocks = [values[k * size : (k + 1) * size] for k in range(links.experts)]
    back = links.exchange(blocks, section)
    return sum(t_times(p, b) for p, b in zip(placed, back))


def rounded_sum(parts):
    parts = [lax.optimization_barrier(p.astype(jnp.bfloat16)).astype(jnp.float32) for p in parts]
    return sum(parts).astype(jnp.bfloat16)


def expert_in(rows, gates_w, ups_w):
    return [(dot_f32(rows, g), dot_f32(rows, u)) for g, u in zip(gates_w, ups_w)]


def expert_out(pre, downs_w):
    hidden = [(silu_parts(g)[0] * u).astype(jnp.bfloat16) for g, u in pre]
    return rounded_sum([dot_f32(h, w) for h, w in zip(hidden, downs_w)])


def expert_back(rows, pre, gates_w, ups_w, downs_w):
    parts = []
    for (gate_pre, up_pre), g, u, w in zip(pre, gates_w, ups_w, downs_w):
        d_hidden = times_t(rows, w)
        activated, slope = silu_parts(gate_pre)
        d_gate = (d_hidden * up_pre * slope).astype(jnp.bfloat16)
        d_up = (d_hidden * activated).astype(jnp.bfloat16)
        parts.append(times_t(d_gate, g) + times_t(d_up, u))
    return rounded_sum(parts)


def body(x_in, dy_out, routes, gates, w_down, w_qk, w_up, e_gate, e_up, e_down):
    links = Links()
    micro, _, length, width = x_in.shape
    capacity = max(2, (3 * length + 2 * links.experts - 1) // (2 * links.experts))
    attn_w = (w_down[0], w_qk[0], w_up[0])
    placed = placements(links, routes[0, :, 0, :, 0], capacity)
    gate_vals = gates[0, :, 0].reshape(micro * length, 1)
    first = links.section == 0

    own = (e_gate[0, 0], e_up[0, 0], e_down[0, 0])
    set_0 = [links.gather_quarters(w, 0) for w in own]
    there = links.move(set_0[2][3][:8, :128], (0,), section_bit=1)
    own_1 = after(own, there)
    set_1 = [links.gather_quarters(w, 1) for w in own_1]

    dy = dy_out.reshape(micro * length, width).astype(jnp.float32)
    dm_1 = dispatch(links, placed, (dy * gate_vals).astype(jnp.bfloat16), 1)

    def to_moe(inputs, section):
        residual, kept = attend_forward(inputs, micro, *attn_w)
        normed, inv_rms = rms_norm(residual.astype(jnp.float32))
        rows = dispatch(links, placed, normed.astype(jnp.bfloat16), section)
        return residual, inv_rms, rows, kept

    def from_moe(residual, values, section):
        picked = collect(links, placed, values, section)
        return (residual.astype(jnp.float32) + picked * gate_vals).astype(jnp.bfloat16)

    def back_from_moe(upstream, residual, inv_rms, values, section):
        d_normed = collect(links, placed, values, section)
        normed = residual.astype(jnp.float32) * inv_rms
        return upstream + rms_back(normed, inv_rms, d_normed)

    res_0, inv_0, rows_0, kept_0 = to_moe(x_in.reshape(micro * length, width), 0)
    pre_0 = expert_in(rows_0, set_0[0], set_0[1])
    out_0 = from_moe(res_0, expert_out(pre_0, set_0[2]), 0)
    res_1, inv_1, rows_1, kept_1 = to_moe(links.move(out_0, (0,), section_bit=1), 1)
    pre_1 = expert_in(rows_1, set_1[0], set_1[1])
    back_1 = expert_back(dm_1, pre_1, *set_1)
    d_res_1 = back_from_moe(dy, res_1, inv_1, back_1, 1)
    d_in_1, late_1 = attend_backward(kept_1, micro, d_res_1, *attn_w)
    u_0 = links.move(d_in_1, (1,), section_bit=1).astype(jnp.float32)
    dm_0 = dispatch(links, placed, (u_0 * gate_vals).astype(jnp.bfloat16), 0)
    back_0 = expert_back(dm_0, pre_0, *set_0)
    d_res_0 = back_from_moe(u_0, res_0, inv_0, back_0, 0)
    d_in_0, late_0 = attend_backward(kept_0, micro, d_res_0, *attn_w)
    out_1 = from_moe(res_1, expert_out(pre_1, set_1[2]), 1)

    def pick(upper, lower):
        return jnp.where(first, upper, lower)

    activations = pick(out_0, out_1).reshape(1, micro, 1, length, width)
    grads_in = pick(d_in_0, d_in_1).reshape(1, micro, 1, length, width)

    normed_cols = links.spread(pick(kept_0[2], kept_1[2]))
    latent_cols = links.spread(pick(kept_0[3], kept_1[3]))
    mixed_all = links.gather_rows(pick(kept_0[6], kept_1[6]))
    res_cols = links.spread(pick(late_0[0], late_1[0]))
    late = links.gather_rows(
        jnp.concatenate([pick(late_0[1], late_1[1]), pick(late_0[2], late_1[2])], axis=1)
    )
    latent_width = w_qk.shape[2]
    g_down = t_times(normed_cols, late[:, :latent_width])
    g_qk = t_times(latent_cols, late[:, latent_width:])
    g_up_t = t_times(res_cols, mixed_all)
    return (activations, grads_in, g_down[None], g_qk[None], g_up_t[None])


def solution(mesh):
    by_sequence = P(None, ("expert", "dp"), None, None)
    by_layer = P("section", None, ("expert", "dp"), None, None)
    shared = P("section", None, None)
    placed = (
        by_sequence,
        by_sequence,
        by_layer,
        by_layer,
        shared,
        shared,
        shared,
        P("section", "expert", None, "dp"),
        P("section", "expert", None, "dp"),
        P("section", "expert", "dp", None),
    )
    by_rows = P("section", ("expert", "dp"), None)
    return jax.shard_map(
        body,
        mesh=mesh,
        in_specs=placed,
        out_specs=(by_layer, by_layer, by_rows, by_rows, by_rows),
        check_vma=False,
    )
```

```python
import jax
import jax.numpy as jnp
from jax import lax
from jax.experimental import pallas as pl
from jax.experimental.pallas import tpu as pltpu
from jax.sharding import PartitionSpec as P

epsilon = 1e-06
AXES = ("section", "expert", "dp")
BF16, F32 = jnp.bfloat16, jnp.float32


def dot_f32(left, right):
    return jnp.dot(left, right, preferred_element_type=F32)


def times_t(left, right):
    return lax.dot_general(left, right, (((1,), (1,)), ((), ())), preferred_element_type=F32)


def t_times(left, right):
    return lax.dot_general(left, right, (((0,), (0,)), ((), ())), preferred_element_type=F32)


def inverse_rms(values):
    return lax.rsqrt(jnp.mean(values * values, axis=-1, keepdims=True) + epsilon)


def rms_back(normed, inv_rms, upstream):
    return inv_rms * (upstream - normed * jnp.mean(upstream * normed, axis=-1, keepdims=True))


def silu_parts(gate_pre):
    sigmoid = jax.nn.sigmoid(gate_pre)
    return (gate_pre * sigmoid, sigmoid * (1.0 + gate_pre * (1.0 - sigmoid)))


def run(name, kernel, ins, outs, scratch=None, hbm=(), smem=(), mib=32, flops=0, out_hbm=False):
    scratch = scratch or {}
    names = [*ins, *outs, *scratch]

    def body(*refs):
        kernel(dict(zip(names, refs)))

    def place(n):
        space = pl.ANY if n in hbm else pltpu.SMEM if n in smem else pltpu.VMEM
        return pl.BlockSpec(memory_space=space)

    moved = sum(x.size * x.dtype.itemsize for x in ins.values())
    got = pl.pallas_call(
        body,
        name=name,
        in_specs=[place(n) for n in ins],
        out_specs=[pl.BlockSpec(memory_space=pl.ANY if out_hbm else pltpu.VMEM) for _ in outs],
        out_shape=[jax.ShapeDtypeStruct(*o) for o in outs.values()],
        scratch_shapes=list(scratch.values()),
        compiler_params=pltpu.CompilerParams(vmem_limit_bytes=mib << 20),
        cost_estimate=pl.CostEstimate(flops=flops, bytes_accessed=moved, transcendentals=0),
    )(*ins.values())
    return dict(zip(outs, got))


class Links:
    def __init__(self):
        self.sections, self.experts, self.quarters = [lax.axis_size(a) for a in AXES]
        self.section, self.expert, self.quarter = [lax.axis_index(a) for a in AXES]
        self.pairwise = self.experts <= 8
        self.every = tuple(range(self.sections))

    def move(self, x, sections, section_bit=0, expert_bits=0, quarter_bits=0):
        def number(s, e, d):
            return (s * self.experts + e) * self.quarters + d

        pairs = [
            (number(s, e, d), number(s ^ section_bit, e ^ expert_bits, d ^ quarter_bits))
            for s in sections
            for e in range(self.experts)
            for d in range(self.quarters)
        ]
        return lax.ppermute(x, AXES, pairs)

    def relative(self, expert):
        return expert ^ self.expert if self.pairwise else expert

    def exchange(self, blocks, section):
        if not self.pairwise:
            sent = blocks[0].reshape(self.experts, -1, blocks[0].shape[1])
            out = lax.all_to_all(sent, "expert", split_axis=0, concat_axis=0, tiled=True)
            return [out.reshape(blocks[0].shape)]
        got = {k: self.move(blocks[k], (section,), expert_bits=k) for k in range(self.experts - 1, 0, -1)}
        return [blocks[0]] + [got[k] for k in range(1, self.experts)]

    def gather_quarters(self, weights, section):
        if self.quarters != 4:
            return [
                [w] + [self.move(w, (section,), quarter_bits=k) for k in range(1, self.quarters)]
                for w in weights
            ]
        near = [[self.move(w, (section,), quarter_bits=k) for k in (1, 2)] for w in weights]
        out = []
        for w, (one, two) in zip(weights, near):
            half = w.shape[0] // 2
            upper = self.move(one[:half], (section,), quarter_bits=2)
            lower = self.move(two[half:], (section,), quarter_bits=1)
            out.append([w, one, two, (upper, lower)])
        return out


def attend_forward(links, inputs, micro, attn_w, pos_row, blocks):
    rows, width = inputs.shape
    length = rows // micro
    latent_width = attn_w[0].shape[1]
    slots, block_rows = blocks
    count = links.experts * links.quarters

    def kernel(r):
        h = r["h"][...].astype(F32)
        normed_b = (h * inverse_rms(h)).astype(BF16)
        latent = dot_f32(normed_b, r["w_down"][...]).astype(BF16)
        queries = dot_f32(latent, r["w_qk"][...]).astype(BF16)
        r["latent"][...] = latent
        r["queries"][...] = queries
        causal = lax.broadcasted_iota(jnp.int32, (length, length), 0) >= lax.broadcasted_iota(
            jnp.int32, (length, length), 1
        )
        mixed = []
        for m in range(micro):
            part = slice(m * length, (m + 1) * length)
            scores = times_t(queries[part], latent[part]) * latent_width ** (-0.5)
            scores = jnp.where(causal, scores, -1e30)
            exponent = jnp.exp(scores - jnp.max(scores, axis=-1, keepdims=True))
            probs = exponent / jnp.sum(exponent, axis=-1, keepdims=True)
            r["probs"][m] = probs
            mixed.append(dot_f32(probs.astype(BF16), latent[part]).astype(BF16))
        mixed = jnp.concatenate(mixed, axis=0)
        residual = (h + dot_f32(mixed, r["w_up"][...])).astype(BF16)
        r["residual"][...] = residual
        wide = residual.astype(F32)
        second_b = (wide * inverse_rms(wide)).astype(BF16)
        place = (r["pos_row"][...] == lax.broadcasted_iota(jnp.int32, (slots, rows), 0)).astype(BF16)
        for k in range(slots // block_rows):
            part = slice(k * block_rows, (k + 1) * block_rows)
            r[f"sent{k}"][...] = dot_f32(place[part], second_b).astype(BF16)
        if links.pairwise:
            pack_factors(links, r, normed_b, [mixed, latent])
        else:
            r["normed"][...] = normed_b
            r["mixed"][...] = mixed

    ins = dict(h=inputs, w_down=attn_w[0], w_qk=attn_w[1], w_up=attn_w[2], pos_row=pos_row)
    outs = dict(
        residual=((rows, width), BF16),
        latent=((rows, latent_width), BF16),
        queries=((rows, latent_width), BF16),
        probs=((micro, length, length), F32),
    )
    for k in range(slots // block_rows):
        outs[f"sent{k}"] = ((block_rows, width), BF16)
    scratch = {}
    smem = ()
    if links.pairwise:
        ins["place"] = jnp.stack([links.expert, links.quarter])
        smem = ("place",)
        outs.update(pack_shapes(links, rows, latent_width))
        scratch = {"cols": pltpu.VMEM((count, rows, latent_width), BF16)}
    else:
        outs.update(normed=((rows, width), BF16), mixed=((rows, latent_width), BF16))
    got = run("attend_forward", kernel, ins, outs, scratch, smem=smem)
    got["inputs"] = inputs
    got["sent"] = [got[f"sent{k}"] for k in range(slots // block_rows)]
    return got


def pack_shapes(links, rows, latent_width):
    return {
        f"pack{k}": (((links.experts + 2) * rows, latent_width), BF16) for k in range(links.quarters)
    }


def pack_factors(links, r, wide, narrow):
    rows, width = wide.shape
    experts, quarters = links.experts, links.quarters
    share = width // (experts * quarters)
    for i in range(experts * quarters):
        r["cols"][i, :, :share] = wide[:, i * share : (i + 1) * share]
    expert, quarter = r["place"][0], r["place"][1]
    for k in range(quarters):
        out = r[f"pack{k}"]
        for e in range(experts):
            out[e * rows : (e + 1) * rows, :share] = r["cols"][
                (expert ^ e) * quarters + (quarter ^ k), :, :share
            ]
        for n, values in enumerate(narrow):
            out[(experts + n) * rows : (experts + n + 1) * rows] = values


def picked_rows(r, count, rows):
    values = [r[f"back{k}"][...] for k in range(count)]
    values = values[0] if count == 1 else jnp.concatenate(values, axis=0)
    slots = values.shape[0]
    place = (r["pos_col"][...] == lax.broadcasted_iota(jnp.int32, (rows, slots), 1)).astype(BF16)
    return dot_f32(place, values)


def attend_backward(links, kept, micro, upstream, back, attn_w, pos_col):
    inputs = kept["inputs"]
    rows, width = inputs.shape
    length = rows // micro
    latent_width = attn_w[0].shape[1]
    count = links.experts * links.quarters

    def kernel(r):
        u = r["u"][...].astype(F32)
        d_second = picked_rows(r, len(back), rows)
        wide = r["residual"][...].astype(F32)
        inv = inverse_rms(wide)
        d_res = u + rms_back(wide * inv, inv, d_second)
        d_res_b = d_res.astype(BF16)
        d_mixed = times_t(d_res_b, r["w_up"][...]).astype(BF16)
        latent, queries = r["latent"][...], r["queries"][...]
        d_latent, d_queries = [], []
        for m in range(micro):
            part = slice(m * length, (m + 1) * length)
            probs = r["probs"][m]
            d_probs = times_t(d_mixed[part], latent[part])
            d_scores = (
                probs
                * (d_probs - jnp.sum(d_probs * probs, axis=-1, keepdims=True))
                * latent_width ** (-0.5)
            ).astype(BF16)
            d_queries.append(dot_f32(d_scores, latent[part]).astype(BF16))
            d_latent.append(
                t_times(probs.astype(BF16), d_mixed[part]) + t_times(d_scores, queries[part])
            )
        d_queries = jnp.concatenate(d_queries, axis=0)
        d_latent = jnp.concatenate(d_latent, axis=0) + times_t(d_queries, r["w_qk"][...])
        d_latent = d_latent.astype(BF16)
        if links.pairwise:
            pack_factors(links, r, d_res_b, [d_latent, d_queries])
        else:
            r["d_res"][...] = d_res_b
            r["d_latent"][...] = d_latent
            r["d_queries"][...] = d_queries
        d_normed = times_t(d_latent, r["w_down"][...])
        h = r["h"][...].astype(F32)
        inv = inverse_rms(h)
        r["d_input"][...] = (d_res + rms_back(h * inv, inv, d_normed)).astype(BF16)

    ins = dict(
        u=upstream,
        h=inputs,
        w_down=attn_w[0],
        w_qk=attn_w[1],
        w_up=attn_w[2],
        pos_col=pos_col,
        **{n: kept[n] for n in ("residual", "latent", "queries", "probs")},
        **{f"back{k}": b for k, b in enumerate(back)},
    )
    outs = dict(d_input=((rows, width), BF16))
    scratch = {}
    smem = ()
    if links.pairwise:
        ins["place"] = jnp.stack([links.expert, links.quarter])
        smem = ("place",)
        outs.update(pack_shapes(links, rows, latent_width))
        scratch = {"cols": pltpu.VMEM((count, rows, latent_width), BF16)}
    else:
        outs.update(
            d_res=((rows, width), BF16),
            d_latent=((rows, latent_width), BF16),
            d_queries=((rows, latent_width), BF16),
        )
    return run("attend_backward", kernel, ins, outs, scratch, smem=smem)


def scatter(upstream, gate_col, pos_row, blocks):
    rows, width = upstream.shape
    slots, block_rows = blocks

    def kernel(r):
        scaled = (r["u"][...].astype(F32) * r["gate"][...]).astype(BF16)
        place = (r["pos_row"][...] == lax.broadcasted_iota(jnp.int32, (slots, rows), 0)).astype(BF16)
        for k in range(slots // block_rows):
            part = slice(k * block_rows, (k + 1) * block_rows)
            r[f"sent{k}"][...] = dot_f32(place[part], scaled).astype(BF16)

    got = run(
        "scatter",
        kernel,
        dict(u=upstream, gate=gate_col, pos_row=pos_row),
        {f"sent{k}": ((block_rows, width), BF16) for k in range(slots // block_rows)},
    )
    return list(got.values())


def combine(residual, back, gate_col, pos_col):
    rows, width = residual.shape

    def kernel(r):
        mixture = picked_rows(r, len(back), rows) * r["gate"][...]
        r["out"][...] = (r["residual"][...].astype(F32) + mixture).astype(BF16)

    ins = dict(residual=residual, gate=gate_col, pos_col=pos_col)
    ins.update({f"back{k}": b for k, b in enumerate(back)})
    return run("combine", kernel, ins, dict(out=((rows, width), BF16)))["out"]


def experts_call(weights, rows=None, pre=None, hidden=None, d_rows=None, forward=False):
    sources = rows if rows is not None else d_rows
    quarters = len(weights[0])
    width, split = weights[0][0].shape
    if hidden is not None:
        slots, block_rows, count = hidden.shape[1], d_rows, hidden.shape[1] // d_rows
    else:
        block_rows, count = sources[0].shape[0], len(sources)
        slots = block_rows * count
    backward = d_rows is not None and hidden is None
    used = []
    if rows is not None or backward:
        used += [0, 1]
    if forward or backward:
        used += [2]
    step = 512 if width % 512 == 0 else width
    steps = [slice(c, c + step) for c in range(0, width, step)]

    def kernel(r):
        def copies(q, source):
            for n in used:
                for half, ref in enumerate(source[n]):
                    size = ref.shape[0]
                    yield pltpu.make_async_copy(
                        ref, r[f"all{n}"].at[q, pl.ds(half * size, size)], r["sem"].at[n, q, half]
                    )

        for q in range(quarters):
            for copy in copies(q, [r[f"w{n}_{q}"] for n in range(3)]):
                copy.start()
        r["acc"][...] = jnp.zeros_like(r["acc"])
        for kind in ("rows", "d_rows"):
            if kind in r and count > 1:
                for k in range(count):
                    r[kind][k * block_rows : (k + 1) * block_rows] = r[f"{kind}{k}"][...]

        def quarter(q, gate_pre=None, up_pre=None):
            for copy in copies(q, [r[f"w{n}_{min(q, quarters - 1)}"] for n in range(3)]):
                copy.wait()
            if rows is not None:
                held = r["rows"][...]
                gate_pre = dot_f32(held, r["all0"][q])
                up_pre = dot_f32(held, r["all1"][q])
            elif pre is not None:
                gate_pre, up_pre = r["gate_pre"][q], r["up_pre"][q]
            if hidden is not None:
                hidden_q = r["hidden"][q]
            else:
                activated, slope = silu_parts(gate_pre)
            if rows is not None:
                hidden_q = (activated * up_pre).astype(BF16)
                if backward:
                    r["hidden_out"][q] = hidden_q
                else:
                    r["gate_out"][q] = gate_pre
                    r["up_out"][q] = up_pre
            if forward:
                for c in steps:
                    part = dot_f32(hidden_q, r["all2"][q, :, c])
                    r["acc"][:, c] += part.astype(BF16).astype(F32)
            if backward:
                d_hidden = times_t(r["d_rows"][...], r["all2"][q])
                d_gate = (d_hidden * up_pre * slope).astype(BF16)
                d_up = (d_hidden * activated).astype(BF16)
                for c in steps:
                    part = times_t(d_gate, r["all0"][q, c]) + times_t(d_up, r["all1"][q, c])
                    r["acc"][:, c] += part.astype(BF16).astype(F32)

        for q in range(quarters):
            quarter(q)
        for k in range(count):
            r[f"value{k}"][...] = r["acc"][k * block_rows : (k + 1) * block_rows].astype(BF16)

    ins, hbm = {}, []
    names = {}
    for n in used:
        for q in range(quarters):
            parts = weights[n][q] if isinstance(weights[n][q], tuple) else (weights[n][q],)
            names[n, q] = []
            for i, part in enumerate(parts):
                ins[f"w{n}_{q}_{i}"] = part
                hbm.append(f"w{n}_{q}_{i}")
                names[n, q].append(f"w{n}_{q}_{i}")
    outs, scratch = {}, {}
    for kind, values in (("rows", rows), ("d_rows", d_rows if backward else None)):
        if values is not None:
            if count == 1:
                ins[kind] = values[0]
            else:
                ins.update({f"{kind}{k}": v for k, v in enumerate(values)})
                scratch[kind] = pltpu.VMEM((slots, width), BF16)
    shape = (quarters, slots, split)
    if pre is not None:
        ins.update(gate_pre=pre[0], up_pre=pre[1])
    if hidden is not None:
        ins["hidden"] = hidden
    if rows is not None and backward:
        outs["hidden_out"] = (shape, BF16)
    elif rows is not None:
        outs.update(gate_out=(shape, F32), up_out=(shape, F32))
    for k in range(count):
        outs[f"value{k}"] = ((block_rows, width), BF16)
    for n in used:
        scratch[f"all{n}"] = pltpu.VMEM((quarters,) + ((width, split) if n < 2 else (split, width)), BF16)
    scratch["acc"] = pltpu.VMEM((slots, width), F32)
    scratch["sem"] = pltpu.SemaphoreType.DMA((3, quarters, 2))

    def with_lists(r):
        r = dict(r)
        for n in range(3):
            for q in range(quarters):
                r[f"w{n}_{q}"] = [r[name] for name in names.get((n, q), ())]
        kernel(r)

    flops = 2 * slots * width * split * quarters * (len(used) + (0 if rows is None or not backward else 2))
    got = run("experts", with_lists, ins, outs, scratch, hbm=hbm, mib=48, flops=flops)
    return [got[f"value{k}"] for k in range(count)], got


def held_back(token, weights, section):
    count = len(weights)

    def kernel(r):
        @pl.when(r["section"][0] == 1)
        def _():
            copies = [
                pltpu.make_async_copy(r[f"w{i}"], r[f"out{i}"], r["sem"].at[i]) for i in range(count)
            ]
            for copy in copies:
                copy.start()
            for copy in copies:
                copy.wait()

    ins = {f"w{i}": w for i, w in enumerate(weights)}
    hbm = tuple(ins)
    ins.update(token=token, section=section.reshape(1))
    got = run(
        "held_back",
        kernel,
        ins,
        {f"out{i}": (w.shape, w.dtype) for i, w in enumerate(weights)},
        {"sem": pltpu.SemaphoreType.DMA((count,))},
        hbm=hbm,
        smem=("section",),
        out_hbm=True,
    )
    return list(got.values())


def weight_gradients(links, early, late, width):
    experts, quarters = links.experts, links.quarters
    rows = early[0].shape[0] // (experts + 2)
    latent_width = early[0].shape[1]
    share, share_qk = width // (experts * quarters), latent_width // (experts * quarters)
    total = 2 * share + share_qk

    def plane_sums(r):
        def part(ref, i, columns=latent_width):
            return ref[i * rows : (i + 1) * rows, :columns]

        sum_qk = jnp.zeros((latent_width, latent_width), F32)
        for k in range(quarters):
            sum_qk += t_times(part(r[f"early{k}"], experts + 1), part(r[f"late{k}"], experts + 1))
        r["qk"][...] = sum_qk
        for e in range(experts):
            down = jnp.zeros((share, latent_width), F32)
            up = jnp.zeros((share, latent_width), F32)
            for k in range(quarters):
                first, last = r[f"early{k}"], r[f"late{k}"]
                down += t_times(part(first, e, share), part(last, experts))
                up += t_times(part(last, e, share), part(first, experts))
            at = pl.multiple_of(((r["place"][0] ^ e) * quarters + r["place"][1]) * share_qk, share_qk)
            out = r[f"sum{e}"]
            out[:share] = down.astype(out.dtype)
            out[share : 2 * share] = up.astype(out.dtype)
            out[2 * share :] = r["qk"][pl.ds(at, share_qk)].astype(out.dtype)

    ins = {f"early{k}": v for k, v in enumerate(early)}
    ins.update({f"late{k}": v for k, v in enumerate(late)})
    ins["place"] = jnp.stack([links.expert, links.quarter])
    outs = {f"sum{e}": ((total, latent_width), BF16 if e else F32) for e in range(experts)}
    sums = run(
        "plane_sums", plane_sums, ins, outs, {"qk": pltpu.VMEM((latent_width, latent_width), F32)}, smem=("place",)
    )
    got = [links.move(sums[f"sum{e}"], links.every, expert_bits=e) for e in range(experts - 1, 0, -1)]

    def add(r):
        value = r["own"][...]
        for i in range(experts - 1):
            value = value + r[f"got{i}"][...].astype(F32)
        r["down"][...] = value[:share]
        r["up"][...] = value[share : 2 * share]
        r["qk"][...] = value[2 * share :]

    ins = {"own": sums["sum0"], **{f"got{i}": g for i, g in enumerate(got)}}
    done = run(
        "add_planes",
        add,
        ins,
        dict(
            down=((share, latent_width), F32),
            qk=((share_qk, latent_width), F32),
            up=((share, latent_width), F32),
        ),
    )
    return done["down"], done["qk"], done["up"]


def spread(links, rows):
    length, width = rows.shape
    count = links.experts * links.quarters
    by_owner = rows.reshape(length, count, width // count).transpose(1, 0, 2)
    got = lax.all_to_all(by_owner, ("expert", "dp"), split_axis=0, concat_axis=0, tiled=True)
    return got.reshape(count * length, width // count)


def body(x_in, dy_out, routes, gates, w_down, w_qk, w_up, e_gate, e_up, e_down):
    links = Links()
    micro, _, length, width = x_in.shape
    rows = micro * length
    capacity = max(2, (3 * length + 2 * links.experts - 1) // (2 * links.experts))
    attn_w = (w_down[0], w_qk[0], w_up[0])
    first = links.section == 0

    route = routes[0, :, 0, :, 0]
    earlier = lax.broadcasted_iota(jnp.int32, (length, length), 0) > lax.broadcasted_iota(
        jnp.int32, (length, length), 1
    )
    same = route[:, :, None] == route[:, None, :]
    rank = jnp.sum((same & earlier).astype(jnp.int32), axis=2)
    slot = jnp.arange(micro, dtype=jnp.int32)[:, None] * capacity + rank
    position = (links.relative(route) * (micro * capacity) + slot).reshape(rows)
    pos_row, pos_col = position.reshape(1, rows), position.reshape(rows, 1)
    gate_col = gates[0, :, 0].reshape(rows, 1)
    slots = links.experts * micro * capacity
    blocks = (slots, micro * capacity if links.pairwise else slots)

    own = (e_gate[0, 0], e_up[0, 0], e_down[0, 0])
    set_0 = links.gather_quarters(own, 0)
    last = set_0[2][3]
    last = last[1] if isinstance(last, tuple) else last
    there = links.move(last[:8, :128], (0,), section_bit=1)
    set_1 = links.gather_quarters(held_back(there, own, links.section), 1)
    set_1 = [[w] + got[1:] for w, got in zip(own, set_1)]

    dy = dy_out.reshape(rows, width)
    dm_1 = links.exchange(scatter(dy, gate_col, pos_row, blocks), 1)

    kept_0 = attend_forward(links, x_in.reshape(rows, width), micro, attn_w, pos_row, blocks)
    rows_0 = links.exchange(kept_0["sent"], 0)
    value_0, pre_0 = experts_call(set_0, rows=rows_0, forward=True)
    out_0 = combine(kept_0["residual"], links.exchange(value_0, 0), gate_col, pos_col)
    kept_1 = attend_forward(
        links, links.move(out_0, (0,), section_bit=1), micro, attn_w, pos_row, blocks
    )
    rows_1 = links.exchange(kept_1["sent"], 1)
    back_1, made_1 = experts_call(set_1, rows=rows_1, d_rows=dm_1)
    back_1 = links.exchange(back_1, 1)
    late_1 = attend_backward(links, kept_1, micro, dy, back_1, attn_w, pos_col)
    u_0 = links.move(late_1["d_input"], (1,), section_bit=1)
    dm_0 = links.exchange(scatter(u_0, gate_col, pos_row, blocks), 0)
    back_0, _ = experts_call(set_0, pre=(pre_0["gate_out"], pre_0["up_out"]), d_rows=dm_0)
    back_0 = links.exchange(back_0, 0)
    late_0 = attend_backward(links, kept_0, micro, u_0, back_0, attn_w, pos_col)
    value_1, _ = experts_call(set_1, hidden=made_1["hidden_out"], d_rows=blocks[1], forward=True)
    out_1 = combine(kept_1["residual"], links.exchange(value_1, 1), gate_col, pos_col)

    def pick(upper, lower):
        return jnp.where(first, upper, lower)

    activations = pick(out_0, out_1).reshape(1, micro, 1, length, width)
    grads_in = pick(late_0["d_input"], late_1["d_input"]).reshape(1, micro, 1, length, width)

    if links.pairwise:
        def plane(upper, lower):
            packs = [pick(upper[f"pack{k}"], lower[f"pack{k}"]) for k in range(links.quarters)]
            return packs[:1] + [
                links.move(packs[k], links.every, quarter_bits=k) for k in range(1, links.quarters)
            ]

        g_down, g_qk, g_up_t = weight_gradients(links, plane(kept_0, kept_1), plane(late_0, late_1), width)
    else:
        def gathered(upper, lower):
            return lax.all_gather(pick(upper, lower), ("expert", "dp"), axis=0, tiled=True)

        g_down = t_times(
            spread(links, pick(kept_0["normed"], kept_1["normed"])),
            gathered(late_0["d_latent"], late_1["d_latent"]),
        )
        g_qk = t_times(
            spread(links, pick(kept_0["latent"], kept_1["latent"])),
            gathered(late_0["d_queries"], late_1["d_queries"]),
        )
        g_up_t = t_times(
            spread(links, pick(late_0["d_res"], late_1["d_res"])),
            gathered(kept_0["mixed"], kept_1["mixed"]),
        )
    return (activations, grads_in, g_down[None], g_qk[None], g_up_t[None])


def solution(mesh):
    by_sequence = P(None, ("expert", "dp"), None, None)
    by_layer = P("section", None, ("expert", "dp"), None, None)
    shared = P("section", None, None)
    placed = (
        by_sequence,
        by_sequence,
        by_layer,
        by_layer,
        shared,
        shared,
        shared,
        P("section", "expert", None, "dp"),
        P("section", "expert", None, "dp"),
        P("section", "expert", "dp", None),
    )
    by_rows = P("section", ("expert", "dp"), None)
    return jax.shard_map(
        body,
        mesh=mesh,
        in_specs=placed,
        out_specs=(by_layer, by_layer, by_rows, by_rows, by_rows),
        check_vma=False,
    )
```

```python
from types import SimpleNamespace

import jax
import jax.numpy as jnp
from jax import lax
from jax.experimental import pallas as pl
from jax.experimental.pallas import tpu as pltpu
from jax.sharding import PartitionSpec as P

epsilon = 1e-06
AXES = ("section", "expert", "dp")
BF16, F32 = jnp.bfloat16, jnp.float32


def dot_f32(left, right):
    return jnp.dot(left, right, preferred_element_type=F32)


def times_t(left, right):
    return lax.dot_general(left, right, (((1,), (1,)), ((), ())), preferred_element_type=F32)


def t_times(left, right):
    return lax.dot_general(left, right, (((0,), (0,)), ((), ())), preferred_element_type=F32)


def inverse_rms(values):
    return lax.rsqrt(jnp.mean(values * values, axis=-1, keepdims=True) + epsilon)


def rms_back(normed, inv_rms, upstream):
    return inv_rms * (upstream - normed * jnp.mean(upstream * normed, axis=-1, keepdims=True))


def silu_parts(gate_pre):
    sigmoid = jax.nn.sigmoid(gate_pre)
    return (gate_pre * sigmoid, sigmoid * (1.0 + gate_pre * (1.0 - sigmoid)))


class Held:
    def __init__(self, refs, held, sems):
        self.held, self.parts, self.seen = held, [], set()
        start = 0
        for i, ref in enumerate(refs):
            target = held
            if len(refs) > 1:
                target = held.at[pl.ds(start, ref.shape[0])]
                start += ref.shape[0]
            self.parts.append((pltpu.make_async_copy(ref, target, sems.at[i]), target))

    def start(self, i):
        if i < len(self.parts):
            self.parts[i][0].start()

    def block(self, i):
        if i not in self.seen:
            self.seen.add(i)
            self.parts[i][0].wait()
        return self.parts[i][1]

    def all(self):
        for i in range(len(self.parts)):
            self.block(i)
        return self.held


class Made:
    def __init__(self, refs, held, sems):
        self.held, self.parts, self.sent = held, [], set()
        start = 0
        for i, ref in enumerate(refs):
            source = held
            if len(refs) > 1:
                source = held.at[pl.ds(start, ref.shape[0])]
                start += ref.shape[0]
            self.parts.append((pltpu.make_async_copy(source, ref, sems.at[i]), source))

    def send(self, i=0):
        if i not in self.sent:
            self.sent.add(i)
            self.parts[i][0].start()

    def finish(self):
        for i, (copy, _) in enumerate(self.parts):
            self.send(i)
        for copy, _ in self.parts:
            copy.wait()


def as_list(value):
    return list(value) if isinstance(value, (list, tuple)) else [value]


def stage_shape(arrays):
    if len(arrays) == 1:
        return pltpu.VMEM(arrays[0].shape, arrays[0].dtype)
    return pltpu.VMEM((sum(a.shape[0] for a in arrays), *arrays[0].shape[1:]), arrays[0].dtype)


def run(name, kernel, ins, outs, scratch=None, smem=None, raw=None, later=(), mib=32, flops=0):
    scratch, smem, raw = scratch or {}, smem or {}, raw or {}
    ins = {k: as_list(v) for k, v in ins.items()}
    outs = {k: v if isinstance(v, list) else [v] for k, v in outs.items()}
    flat_in = [a for v in ins.values() for a in v]
    flat_out = [a for v in outs.values() for a in v]
    stages = [stage_shape(v) for v in [*ins.values(), *outs.values()]]
    sems = [pltpu.SemaphoreType.DMA((len(v),)) for v in [*ins.values(), *outs.values()]]

    def body(*refs):
        refs = list(refs)

        def take(count):
            got = refs[:count]
            del refs[:count]
            return got

        smem_refs, raw_refs = take(len(smem)), take(len(raw))
        in_refs = [take(len(v)) for v in ins.values()]
        take(len(later))
        out_refs = [take(len(v)) for v in outs.values()]
        staged, signals = take(len(stages)), take(len(sems))
        r = SimpleNamespace(**dict(zip(smem, smem_refs)), **dict(zip(raw, raw_refs)))
        held = [Held(a, b, c) for a, b, c in zip(in_refs, staged, signals)]
        made = [Made(a, b, c) for a, b, c in zip(out_refs, staged[len(ins):], signals[len(ins):])]
        for i in range(max([len(v) for v in ins.values()], default=0)):
            for h in held:
                h.start(i)
        r.__dict__.update(zip(ins, held))
        r.__dict__.update(zip(outs, made))
        r.__dict__.update(zip(scratch, refs))
        kernel(r)
        for h in held:
            h.all()
        for m in made:
            m.finish()

    everything = [*smem.values(), *raw.values(), *flat_in, *later]
    spaces = [pltpu.SMEM] * len(smem) + [pl.ANY] * (len(raw) + len(flat_in) + len(later))
    got = pl.pallas_call(
        body,
        name=name,
        in_specs=[pl.BlockSpec(memory_space=s) for s in spaces],
        out_specs=[pl.BlockSpec(memory_space=pl.ANY) for _ in flat_out],
        out_shape=flat_out,
        scratch_shapes=[*stages, *sems, *scratch.values()],
        compiler_params=pltpu.CompilerParams(vmem_limit_bytes=mib << 20),
        cost_estimate=pl.CostEstimate(
            flops=flops,
            bytes_accessed=sum(a.size * a.dtype.itemsize for a in flat_in),
            transcendentals=0,
        ),
    )(*everything)
    got, result = list(got), SimpleNamespace()
    for k, v in outs.items():
        part, got = got[: len(v)], got[len(v) :]
        setattr(result, k, part if len(part) > 1 else part[0])
    return result


def like(*shape, dtype=BF16):
    return jax.ShapeDtypeStruct(shape, dtype)


class Links:
    def __init__(self):
        self.sections, self.experts, self.quarters = [lax.axis_size(a) for a in AXES]
        self.section, self.expert, self.quarter = [lax.axis_index(a) for a in AXES]
        self.pairwise = self.experts <= 8
        self.every = tuple(range(self.sections))
        self.place = jnp.stack([self.expert, self.quarter, self.section])

    def move(self, x, sections, section_bit=0, expert_bits=0, quarter_bits=0):
        def number(s, e, d):
            return (s * self.experts + e) * self.quarters + d

        pairs = [
            (number(s, e, d), number(s ^ section_bit, e ^ expert_bits, d ^ quarter_bits))
            for s in sections
            for e in range(self.experts)
            for d in range(self.quarters)
        ]
        return lax.ppermute(x, AXES, pairs)

    def relative(self, expert):
        return expert ^ self.expert if self.pairwise else expert

    def exchange(self, blocks, section):
        if not self.pairwise:
            sent = blocks.reshape(self.experts, -1, blocks.shape[1])
            out = lax.all_to_all(sent, "expert", split_axis=0, concat_axis=0, tiled=True)
            return out.reshape(blocks.shape)
        got = {k: self.move(blocks[k], (section,), expert_bits=k) for k in range(self.experts - 1, 0, -1)}
        return [blocks[0]] + [got[k] for k in range(1, self.experts)]

    def gather_quarters(self, packs, section):
        if self.quarters != 4:
            return [
                [p] + [self.move(p, (section,), quarter_bits=k) for k in range(1, self.quarters)]
                for p in packs
            ]
        one = [self.move(p, (section,), quarter_bits=1) for p in packs]
        two = [self.move(p, (section,), quarter_bits=2) for p in packs]
        three = [
            self.move(one[0], (section,), quarter_bits=2),
            self.move(two[1], (section,), quarter_bits=1),
        ]
        return [list(quarters) for quarters in zip(packs, one, two, three)]


def attend_forward(links, inputs, micro, attn_w, pos_row, blocks, later=()):
    rows, width = inputs.shape
    length = rows // micro
    latent_width = attn_w[0].shape[1]
    slots, block_rows = blocks

    def kernel(r):
        h = r.h.all()[...].astype(F32)
        normed_b = (h * inverse_rms(h)).astype(BF16)
        latent = dot_f32(normed_b, r.w_down.all()[...]).astype(BF16)
        queries = dot_f32(latent, r.w_qk.all()[...]).astype(BF16)
        r.latent.held[...] = latent
        r.queries.held[...] = queries
        causal = lax.broadcasted_iota(jnp.int32, (length, length), 0) >= lax.broadcasted_iota(
            jnp.int32, (length, length), 1
        )
        mixed = []
        for m in range(micro):
            part = slice(m * length, (m + 1) * length)
            scores = times_t(queries[part], latent[part]) * latent_width ** (-0.5)
            scores = jnp.where(causal, scores, -1e30)
            exponent = jnp.exp(scores - jnp.max(scores, axis=-1, keepdims=True))
            probs = exponent / jnp.sum(exponent, axis=-1, keepdims=True)
            r.probs.held[m] = probs
            mixed.append(dot_f32(probs.astype(BF16), latent[part]).astype(BF16))
        mixed = jnp.concatenate(mixed, axis=0)
        residual = (h + dot_f32(mixed, r.w_up.all()[...])).astype(BF16)
        r.residual.held[...] = residual
        r.residual.send()
        wide = residual.astype(F32)
        second_b = (wide * inverse_rms(wide)).astype(BF16)
        place_rows(r, r.pos_row.all()[...], second_b, slots, block_rows)
        if links.pairwise:
            pack_factors(links, r, normed_b, [mixed, latent])
        else:
            r.normed.held[...] = normed_b
            r.mixed.held[...] = mixed

    outs = dict(
        sent=[like(block_rows, width)] * (slots // block_rows),
        residual=like(rows, width),
        latent=like(rows, latent_width),
        queries=like(rows, latent_width),
        probs=like(micro, length, length, dtype=F32),
    )
    if links.pairwise:
        outs.update(packs=pack_shapes(links, rows, latent_width))
    else:
        outs.update(normed=like(rows, width), mixed=like(rows, latent_width))
    got = run(
        "attend_forward",
        kernel,
        dict(h=inputs, w_down=attn_w[0], w_qk=attn_w[1], w_up=attn_w[2], pos_row=pos_row),
        outs,
        pack_scratch(links, rows, latent_width),
        dict(place=links.place),
        later=later,
    )
    got.inputs = inputs
    return got


def place_rows(r, pos_row, values, slots, block_rows):
    shape = (slots, pos_row.shape[1])
    place = (pos_row == lax.broadcasted_iota(jnp.int32, shape, 0)).astype(BF16)
    for k in range(slots // block_rows):
        part = slice(k * block_rows, (k + 1) * block_rows)
        r.sent.held[part] = dot_f32(place[part], values).astype(BF16)
        r.sent.send(k)


def pack_shapes(links, rows, latent_width):
    return [like((links.experts + 2) * rows, latent_width)] * links.quarters


def pack_scratch(links, rows, latent_width):
    if not links.pairwise:
        return {}
    return dict(cols=pltpu.VMEM((links.experts * links.quarters, rows, latent_width), BF16))


def pack_factors(links, r, wide, narrow):
    rows, width = wide.shape
    experts, quarters = links.experts, links.quarters
    share = width // (experts * quarters)
    for i in range(experts * quarters):
        r.cols[i, :, :share] = wide[:, i * share : (i + 1) * share]
    expert, quarter = r.place[0], r.place[1]
    for k in range(quarters):
        out = r.packs.parts[k][1]
        for e in range(experts):
            out[e * rows : (e + 1) * rows] = r.cols[(expert ^ e) * quarters + (quarter ^ k)]
        for n, values in enumerate(narrow):
            out[(experts + n) * rows : (experts + n + 1) * rows] = values
        r.packs.send(k)


def picked_rows(r, rows):
    values = r.back.all()
    place = (
        r.pos_col.all()[...] == lax.broadcasted_iota(jnp.int32, (rows, values.shape[0]), 1)
    ).astype(BF16)
    return dot_f32(place, values[...])


def attend_backward(links, kept, micro, upstream, back, attn_w, pos_col, later=()):
    inputs = kept.inputs
    rows, width = inputs.shape
    length = rows // micro
    latent_width = attn_w[0].shape[1]

    def kernel(r):
        u = r.u.all()[...].astype(F32)
        d_second = picked_rows(r, rows)
        wide = r.residual.all()[...].astype(F32)
        inv = inverse_rms(wide)
        d_res = u + rms_back(wide * inv, inv, d_second)
        d_res_b = d_res.astype(BF16)
        d_mixed = times_t(d_res_b, r.w_up.all()[...]).astype(BF16)
        latent, queries, all_probs = r.latent.all()[...], r.queries.all()[...], r.probs.all()
        d_latent, d_queries = [], []
        for m in range(micro):
            part = slice(m * length, (m + 1) * length)
            probs = all_probs[m]
            d_probs = times_t(d_mixed[part], latent[part])
            d_scores = (
                probs
                * (d_probs - jnp.sum(d_probs * probs, axis=-1, keepdims=True))
                * latent_width ** (-0.5)
            ).astype(BF16)
            d_queries.append(dot_f32(d_scores, latent[part]).astype(BF16))
            d_latent.append(
                t_times(probs.astype(BF16), d_mixed[part]) + t_times(d_scores, queries[part])
            )
        d_queries = jnp.concatenate(d_queries, axis=0)
        d_latent = jnp.concatenate(d_latent, axis=0) + times_t(d_queries, r.w_qk.all()[...])
        d_latent = d_latent.astype(BF16)
        if links.pairwise:
            pack_factors(links, r, d_res_b, [d_latent, d_queries])
        else:
            r.d_res.held[...] = d_res_b
            r.d_latent.held[...] = d_latent
            r.d_queries.held[...] = d_queries
        d_normed = times_t(d_latent, r.w_down.all()[...])
        h = r.h.all()[...].astype(F32)
        inv = inverse_rms(h)
        r.d_input.held[...] = (d_res + rms_back(h * inv, inv, d_normed)).astype(BF16)

    outs = dict(d_input=like(rows, width))
    if links.pairwise:
        outs.update(packs=pack_shapes(links, rows, latent_width))
    else:
        outs.update(
            d_res=like(rows, width),
            d_latent=like(rows, latent_width),
            d_queries=like(rows, latent_width),
        )
    return run(
        "attend_backward",
        kernel,
        dict(
            back=back,
            pos_col=pos_col,
            u=upstream,
            residual=kept.residual,
            w_up=attn_w[2],
            latent=kept.latent,
            queries=kept.queries,
            probs=kept.probs,
            w_qk=attn_w[1],
            w_down=attn_w[0],
            h=inputs,
        ),
        outs,
        pack_scratch(links, rows, latent_width),
        dict(place=links.place),
        later=later,
    )


def scatter(upstream, gate_col, pos_row, blocks):
    width = upstream.shape[1]
    slots, block_rows = blocks

    def kernel(r):
        scaled = (r.u.all()[...].astype(F32) * r.gate.all()[...]).astype(BF16)
        place_rows(r, r.pos_row.all()[...], scaled, slots, block_rows)

    ins = dict(u=upstream, gate=gate_col, pos_row=pos_row)
    return run("scatter", kernel, ins, dict(sent=[like(block_rows, width)] * (slots // block_rows))).sent


def combine(residual, back, gate_col, pos_col):
    rows, width = residual.shape

    def kernel(r):
        mixture = picked_rows(r, rows) * r.gate.all()[...]
        r.out.held[...] = (r.residual.all()[...].astype(F32) + mixture).astype(BF16)

    ins = dict(back=back, pos_col=pos_col, gate=gate_col, residual=residual)
    return run("combine", kernel, ins, dict(out=like(rows, width))).out


def pack_weights(weights, later=(), only=None, section=None):
    gate_w, up_w, down_w = weights
    width, split = gate_w.shape
    count = width // split
    half = count // 2
    shape = like(width + half * split, split)

    def kernel(r):
        def copy_all():
            copies = []
            for source, target in ((r.gate, r.out0), (r.up, r.out1)):
                copies.append((source, target.at[pl.ds(0, width)]))
            for j in range(count):
                target = r.out0 if j < half else r.out1
                at = pl.ds(width + (j % half) * split, split)
                copies.append((r.down.at[:, pl.ds(j * split, split)], target.at[at]))
            copies = [
                pltpu.make_async_copy(a, b, r.sem.at[i]) for i, (a, b) in enumerate(copies)
            ]
            for copy in copies:
                copy.start()
            for copy in copies:
                copy.wait()

        if only is None:
            copy_all()
        else:
            pl.when(r.place[2] == only)(copy_all)

    def body(place, gate, up, down, *refs):
        out0, out1, sem = refs[len(later):]
        kernel(SimpleNamespace(place=place, gate=gate, up=up, down=down, out0=out0, out1=out1, sem=sem))

    spaces = [pltpu.SMEM] + [pl.ANY] * (3 + len(later))
    return list(
        pl.pallas_call(
            body,
            name="pack_weights",
            in_specs=[pl.BlockSpec(memory_space=s) for s in spaces],
            out_specs=[pl.BlockSpec(memory_space=pl.ANY)] * 2,
            out_shape=[shape, shape],
            scratch_shapes=[pltpu.SemaphoreType.DMA((count + 2,))],
            cost_estimate=pl.CostEstimate(flops=0, bytes_accessed=0, transcendentals=0),
        )(section, gate_w, up_w, down_w, *later)
    )


def experts_call(packs, rows=None, pre=None, hidden=None, d_rows=None, forward=False, block_rows=None):
    quarters = len(packs[0])
    split = packs[0][0].shape[1]
    backward = d_rows is not None
    sources = as_list(rows if rows is not None else d_rows) if hidden is None else []
    if hidden is None:
        block_rows, count = sources[0].shape[0], len(sources)
        width = sources[0].shape[1]
        slots = block_rows * count
    else:
        slots = hidden.shape[1]
        count = slots // block_rows
        width = 2 * packs[0][0].shape[0] // 3
    blocks = width // split
    half = blocks // 2

    def kernel(r):
        def down_block(q, j):
            pack = (r.pack0 if j < half else r.pack1).block(q)
            return pack[width + (j % half) * split : width + (j % half + 1) * split]

        gate_pre, up_pre, hiddens, d_gates, d_ups = [], [], [], [], []
        for q in range(quarters):
            if rows is not None:
                held = r.rows.all()[...]
                gate_pre = dot_f32(held, r.pack0.block(q)[:width])
                up_pre = dot_f32(held, r.pack1.block(q)[:width])
                if not backward:
                    r.gate_out.held[q] = gate_pre
                    r.up_out.held[q] = up_pre
            elif pre is not None:
                gate_pre, up_pre = r.gate_pre.all()[q], r.up_pre.all()[q]
            if hidden is not None:
                hiddens.append(r.hidden.all()[q])
                continue
            activated, slope = silu_parts(gate_pre)
            if rows is not None:
                hiddens.append((activated * up_pre).astype(BF16))
                if backward:
                    r.hidden_out.held[q] = hiddens[-1]
            if backward:
                d_held = r.d_rows.all()
                d_hidden = sum(
                    times_t(d_held[:, j * split : (j + 1) * split], down_block(q, j))
                    for j in range(blocks)
                )
                d_gates.append((d_hidden * up_pre * slope).astype(BF16))
                d_ups.append((d_hidden * activated).astype(BF16))
        for j in range(blocks):
            columns = slice(j * split, (j + 1) * split)
            total = jnp.zeros((slots, split), F32)
            for q in range(quarters):
                if forward:
                    part = dot_f32(hiddens[q], down_block(q, j))
                else:
                    part = times_t(d_gates[q], r.pack0.block(q)[columns]) + times_t(
                        d_ups[q], r.pack1.block(q)[columns]
                    )
                total += part.astype(BF16).astype(F32)
            r.value.held[:, columns] = total.astype(BF16)

    ins = {}
    if rows is not None:
        ins.update(rows=rows)
    if backward:
        ins.update(d_rows=d_rows)
    if pre is not None:
        ins.update(gate_pre=pre[0], up_pre=pre[1])
    if hidden is not None:
        ins.update(hidden=hidden)
    ins.update(pack0=packs[0], pack1=packs[1])
    outs = dict(value=[like(block_rows, width)] * count)
    if rows is not None and backward:
        outs.update(hidden_out=like(quarters, slots, split))
    elif rows is not None:
        made = like(quarters, slots, split, dtype=F32)
        outs.update(gate_out=made, up_out=made)
    flops = 2 * slots * width * split * quarters * 3
    return run("experts", kernel, ins, outs, mib=52, flops=flops)


def weight_gradients(links, early, late, width):
    experts, quarters = links.experts, links.quarters
    rows = early[0].shape[0] // (experts + 2)
    latent_width = early[0].shape[1]
    share, share_qk = width // (experts * quarters), latent_width // (experts * quarters)
    total = 2 * share + share_qk

    def plane_sums(r):
        def part(held, k, i, columns=latent_width):
            return held.block(k)[i * rows : (i + 1) * rows, :columns]

        sum_qk = jnp.zeros((latent_width, latent_width), F32)
        for k in range(quarters):
            sum_qk += t_times(part(r.early, k, experts + 1), part(r.late, k, experts + 1))
        r.qk[...] = sum_qk
        for e in range(experts):
            down = jnp.zeros((share, latent_width), F32)
            up = jnp.zeros((share, latent_width), F32)
            for k in range(quarters):
                down += t_times(part(r.early, k, e, share), part(r.late, k, experts))
                up += t_times(part(r.late, k, e, share), part(r.early, k, experts))
            at = pl.multiple_of(((r.place[0] ^ e) * quarters + r.place[1]) * share_qk, share_qk)
            made = r.away if e else r.own
            out = made.parts[max(e - 1, 0)][1]
            out[:share] = down.astype(out.dtype)
            out[share : 2 * share] = up.astype(out.dtype)
            out[2 * share :] = r.qk[pl.ds(at, share_qk)].astype(out.dtype)
            made.send(max(e - 1, 0))

    sums = run(
        "plane_sums",
        plane_sums,
        dict(early=early, late=late),
        dict(
            own=like(total, latent_width, dtype=F32),
            away=[like(total, latent_width)] * (experts - 1),
        ),
        dict(qk=pltpu.VMEM((latent_width, latent_width), F32)),
        dict(place=links.place),
    )
    away = as_list(sums.away)
    got = [links.move(away[e - 1], links.every, expert_bits=e) for e in range(experts - 1, 0, -1)]

    def add(r):
        value = r.own.all()[...]
        for i in range(experts - 1):
            value = value + r.got.block(i)[...].astype(F32)
        r.down.held[...] = value[:share]
        r.up.held[...] = value[share : 2 * share]
        r.qk.held[...] = value[2 * share :]

    done = run(
        "add_planes",
        add,
        dict(own=sums.own, got=got),
        dict(
            down=like(share, latent_width, dtype=F32),
            qk=like(share_qk, latent_width, dtype=F32),
            up=like(share, latent_width, dtype=F32),
        ),
    )
    return done.down, done.qk, done.up


def spread(links, rows):
    length, width = rows.shape
    count = links.experts * links.quarters
    by_owner = rows.reshape(length, count, width // count).transpose(1, 0, 2)
    got = lax.all_to_all(by_owner, ("expert", "dp"), split_axis=0, concat_axis=0, tiled=True)
    return got.reshape(count * length, width // count)


def body(x_in, dy_out, routes, gates, w_down, w_qk, w_up, e_gate, e_up, e_down):
    links = Links()
    micro, _, length, width = x_in.shape
    rows = micro * length
    capacity = max(2, (3 * length + 2 * links.experts - 1) // (2 * links.experts))
    attn_w = (w_down[0], w_qk[0], w_up[0])
    first = links.section == 0

    route = routes[0, :, 0, :, 0]
    earlier = lax.broadcasted_iota(jnp.int32, (length, length), 0) > lax.broadcasted_iota(
        jnp.int32, (length, length), 1
    )
    same = route[:, :, None] == route[:, None, :]
    rank = jnp.sum((same & earlier).astype(jnp.int32), axis=2)
    slot = jnp.arange(micro, dtype=jnp.int32)[:, None] * capacity + rank
    position = (links.relative(route) * (micro * capacity) + slot).reshape(rows)
    pos_row, pos_col = position.reshape(1, rows), position.reshape(rows, 1)
    gate_col = gates[0, :, 0].reshape(rows, 1)
    slots = links.experts * micro * capacity
    blocks = (slots, micro * capacity if links.pairwise else slots)

    own = (e_gate[0, 0], e_up[0, 0], e_down[0, 0])
    packed = pack_weights(own, section=links.place)
    set_0 = links.gather_quarters(packed, 0)
    there = [links.move(pack[3][:16, :128], (0,), section_bit=1) for pack in set_0]
    set_1 = links.gather_quarters(pack_weights(own, there, 1, links.place), 1)
    set_1 = [[mine] + got[1:] for mine, got in zip(packed, set_1)]

    dy = dy_out.reshape(rows, width)
    dm_1 = links.exchange(scatter(dy, gate_col, pos_row, blocks), 1)

    kept_0 = attend_forward(
        links, x_in.reshape(rows, width), micro, attn_w, pos_row, blocks, as_list(dm_1)
    )
    made_0 = experts_call(set_0, rows=links.exchange(kept_0.sent, 0), forward=True)
    out_0 = combine(kept_0.residual, links.exchange(made_0.value, 0), gate_col, pos_col)
    kept_1 = attend_forward(
        links, links.move(out_0, (0,), section_bit=1), micro, attn_w, pos_row, blocks
    )
    made_1 = experts_call(set_1, rows=links.exchange(kept_1.sent, 1), d_rows=dm_1)
    back_1 = links.exchange(made_1.value, 1)
    value_1 = experts_call(set_1, hidden=made_1.hidden_out, forward=True, block_rows=blocks[1]).value
    late_1 = attend_backward(
        links, kept_1, micro, dy, back_1, attn_w, pos_col, as_list(value_1)[:1]
    )
    u_0 = links.move(late_1.d_input, (1,), section_bit=1)
    dm_0 = links.exchange(scatter(u_0, gate_col, pos_row, blocks), 0)
    back_0 = experts_call(set_0, pre=(made_0.gate_out, made_0.up_out), d_rows=dm_0).value
    late_0 = attend_backward(links, kept_0, micro, u_0, links.exchange(back_0, 0), attn_w, pos_col)
    out_1 = combine(kept_1.residual, links.exchange(value_1, 1), gate_col, pos_col)

    def pick(upper, lower):
        return jnp.where(first, upper, lower)

    activations = pick(out_0, out_1).reshape(1, micro, 1, length, width)
    grads_in = pick(late_0.d_input, late_1.d_input).reshape(1, micro, 1, length, width)

    if links.pairwise:
        def plane(upper, lower):
            packs = [pick(a, b) for a, b in zip(upper.packs, lower.packs)]
            return packs[:1] + [
                links.move(packs[k], links.every, quarter_bits=k) for k in range(1, links.quarters)
            ]

        g_down, g_qk, g_up_t = weight_gradients(links, plane(kept_0, kept_1), plane(late_0, late_1), width)
    else:
        def gathered(upper, lower):
            return lax.all_gather(pick(upper, lower), ("expert", "dp"), axis=0, tiled=True)

        g_down = t_times(
            spread(links, pick(kept_0.normed, kept_1.normed)),
            gathered(late_0.d_latent, late_1.d_latent),
        )
        g_qk = t_times(
            spread(links, pick(kept_0.latent, kept_1.latent)),
            gathered(late_0.d_queries, late_1.d_queries),
        )
        g_up_t = t_times(
            spread(links, pick(late_0.d_res, late_1.d_res)),
            gathered(kept_0.mixed, kept_1.mixed),
        )
    return (activations, grads_in, g_down[None], g_qk[None], g_up_t[None])


def solution(mesh):
    by_sequence = P(None, ("expert", "dp"), None, None)
    by_layer = P("section", None, ("expert", "dp"), None, None)
    shared = P("section", None, None)
    placed = (
        by_sequence,
        by_sequence,
        by_layer,
        by_layer,
        shared,
        shared,
        shared,
        P("section", "expert", None, "dp"),
        P("section", "expert", None, "dp"),
        P("section", "expert", "dp", None),
    )
    by_rows = P("section", ("expert", "dp"), None)
    return jax.shard_map(
        body,
        mesh=mesh,
        in_specs=placed,
        out_specs=(by_layer, by_layer, by_rows, by_rows, by_rows),
        check_vma=False,
    )
```

```python
from types import SimpleNamespace

import jax
import jax.numpy as jnp
from jax import lax
from jax.experimental import pallas as pl
from jax.experimental.pallas import tpu as pltpu
from jax.sharding import PartitionSpec as P

epsilon = 1e-06
AXES = ("section", "expert", "dp")
GRANT = 62 << 20
ATTENTION = ("w_down", "w_qk", "w_up")
BF16, F32 = jnp.bfloat16, jnp.float32


def dot_f32(left, right):
    return jnp.dot(left, right, preferred_element_type=F32)


def times_t(left, right):
    return lax.dot_general(left, right, (((1,), (1,)), ((), ())), preferred_element_type=F32)


def t_times(left, right):
    return lax.dot_general(left, right, (((0,), (0,)), ((), ())), preferred_element_type=F32)


def inverse_rms(values):
    return lax.rsqrt(jnp.mean(values * values, axis=-1, keepdims=True) + epsilon)


def rms_back(normed, inv_rms, upstream):
    return inv_rms * (upstream - normed * jnp.mean(upstream * normed, axis=-1, keepdims=True))


def silu_parts(gate_pre):
    sigmoid = jax.nn.sigmoid(gate_pre)
    return (gate_pre * sigmoid, sigmoid * (1.0 + gate_pre * (1.0 - sigmoid)))


class Held:
    def __init__(self, refs, held, sems):
        self.held, self.parts, self.seen = held, [], set()
        start = 0
        for i, ref in enumerate(refs):
            target = held
            if len(refs) > 1:
                target = held.at[pl.ds(start, ref.shape[0])]
                start += ref.shape[0]
            self.parts.append((pltpu.make_async_copy(ref, target, sems.at[i]), target))

    def start(self, i):
        if i < len(self.parts):
            self.parts[i][0].start()

    def block(self, i):
        if i not in self.seen:
            self.seen.add(i)
            self.parts[i][0].wait()
        return self.parts[i][1]

    def all(self):
        for i in range(len(self.parts)):
            self.block(i)
        return self.held


class Made:
    def __init__(self, refs, held, sems):
        self.held, self.parts, self.sent = held, [], set()
        start = 0
        for i, ref in enumerate(refs):
            source = held
            if len(refs) > 1:
                source = held.at[pl.ds(start, ref.shape[0])]
                start += ref.shape[0]
            self.parts.append((pltpu.make_async_copy(source, ref, sems.at[i]), source))

    def send(self, i=0):
        if i not in self.sent:
            self.sent.add(i)
            self.parts[i][0].start()

    def finish(self):
        for i, (copy, _) in enumerate(self.parts):
            self.send(i)
        for copy, _ in self.parts:
            copy.wait()


def as_list(value):
    return list(value) if isinstance(value, (list, tuple)) else [value]


def stage_shape(arrays):
    if len(arrays) == 1:
        return pltpu.VMEM(arrays[0].shape, arrays[0].dtype)
    rows = sum(a.shape[0] for a in arrays)
    return pltpu.VMEM((rows, *arrays[0].shape[1:]), arrays[0].dtype)


def run(name, kernel, ins, outs, scratch=None, vmem=None, later=(), merge=None, only=None, place=None, raw=None, first=99, flops=0):
    scratch, vmem, merge, raw = scratch or {}, vmem or {}, merge or {}, raw or {}
    ins = {k: as_list(v) for k, v in ins.items()}
    outs = {k: as_list(v) for k, v in outs.items()}
    merge = {k: as_list(v) for k, v in merge.items()}
    flat_in = [a for v in ins.values() for a in v]
    flat_out = [a for v in outs.values() for a in v]
    flat_merge = [a for v in merge.values() for a in v]
    stages = [stage_shape(v) for v in [*ins.values(), *outs.values()]]
    sems = [pltpu.SemaphoreType.DMA((len(v),)) for v in [*ins.values(), *outs.values()]]
    smem = [] if place is None else [place]

    def body(*refs):
        refs = list(refs)

        def take(count):
            got = refs[:count]
            del refs[:count]
            return got

        place_refs, vmem_refs = take(len(smem)), take(len(vmem))
        in_refs = [take(len(v)) for v in ins.values()]
        instead = {k: take(len(v)) for k, v in merge.items()}
        raw_refs = {k: take(len(v)) for k, v in raw.items()}
        take(len(later))
        out_refs = [take(len(v)) for v in outs.values()]
        staged, signals = take(len(stages)), take(len(sems))
        r = SimpleNamespace(**dict(zip(vmem, vmem_refs)))
        if smem:
            r.place = place_refs[0]
        held = [Held(a, b, c) for a, b, c in zip(in_refs, staged, signals)]
        made = [Made(a, b, c) for a, b, c in zip(out_refs, staged[len(ins) :], signals[len(ins) :])]
        r.__dict__.update(zip(ins, held))
        r.__dict__.update(zip(outs, made))
        r.__dict__.update(zip(scratch, refs))

        r.__dict__.update(raw_refs)

        def open_all(part):
            for i in range(max([len(h.parts) for h in part], default=0)):
                for h in part:
                    h.start(i)

        r.open_rest = lambda: open_all(held[first:])

        def work():
            open_all(held[:first])
            kernel(r)
            for h in held:
                h.all()
            for m in made:
                m.finish()

        def passed_on():
            for k, m, sem in zip(outs, made, signals[len(ins) :]):
                parts = list(zip(instead.get(k, ()), m.parts))
                loads = [
                    pltpu.make_async_copy(ref, part[1], sem.at[i]) for i, (ref, part) in enumerate(parts)
                ]
                for load in loads:
                    load.start()
                for load, (_, part) in zip(loads, parts):
                    load.wait()
                    part[0].start()
                for _, part in parts:
                    part[0].wait()

        if only is None:
            work()
        else:
            pl.when(r.place[2] == only)(work)
            if merge:
                pl.when(r.place[2] != only)(passed_on)

    flat_raw = [a for v in raw.values() for a in v]
    everything = [*smem, *vmem.values(), *flat_in, *flat_merge, *flat_raw, *later]
    spaces = [pltpu.SMEM] * len(smem) + [pltpu.VMEM] * len(vmem)
    spaces += [pltpu.HBM] * (len(everything) - len(spaces))
    got = pl.pallas_call(
        body,
        name=name,
        in_specs=[pl.BlockSpec(memory_space=s) for s in spaces],
        out_specs=[pl.BlockSpec(memory_space=pltpu.HBM) for _ in flat_out],
        out_shape=flat_out,
        scratch_shapes=[*stages, *sems, *scratch.values()],
        compiler_params=pltpu.CompilerParams(vmem_limit_bytes=GRANT),
        cost_estimate=pl.CostEstimate(
            flops=flops,
            bytes_accessed=sum(a.size * a.dtype.itemsize for a in flat_in),
            transcendentals=0,
        ),
    )(*everything)
    got, result = list(got), SimpleNamespace()
    for k, v in outs.items():
        part, got = got[: len(v)], got[len(v) :]
        setattr(result, k, part if len(part) > 1 else part[0])
    return result


def like(*shape, dtype=BF16):
    return jax.ShapeDtypeStruct(shape, dtype)


class Links:
    def __init__(self):
        self.sections, self.experts, self.quarters = [lax.axis_size(a) for a in AXES]
        self.section, self.expert, self.quarter = [lax.axis_index(a) for a in AXES]
        self.pairwise = self.experts <= 8
        self.every = tuple(range(self.sections))
        self.place = jnp.stack([self.expert, self.quarter, self.section])

    def move(self, x, sections, section_bit=0, expert_bits=0, quarter_bits=0):
        def number(s, e, d):
            return (s * self.experts + e) * self.quarters + d

        pairs = [
            (number(s, e, d), number(s ^ section_bit, e ^ expert_bits, d ^ quarter_bits))
            for s in sections
            for e in range(self.experts)
            for d in range(self.quarters)
        ]
        return lax.ppermute(x, AXES, pairs)

    def relative(self, expert):
        return expert ^ self.expert if self.pairwise else expert

    def exchange(self, blocks, section):
        if not self.pairwise:
            sent = blocks.reshape(self.experts, -1, blocks.shape[1])
            out = lax.all_to_all(sent, "expert", split_axis=0, concat_axis=0, tiled=True)
            return out.reshape(blocks.shape)
        got = {k: self.move(blocks[k], (section,), expert_bits=k) for k in range(self.experts - 1, 0, -1)}
        return [blocks[0]] + [got[k] for k in range(1, self.experts)]

    def gather_quarters(self, packs, section, before=(), between=()):
        if self.quarters != 4:
            return [
                [p] + [self.move(p, (section,), quarter_bits=k) for k in range(1, self.quarters)]
                for p in packs[:2]
            ]

        def across(one, two):
            return [
                self.move(one, (section,), quarter_bits=1),
                self.move(two, (section,), quarter_bits=2),
            ]

        step = across(packs[0], packs[1])
        again = tied(packs[2:], between) if between else packs
        other = across(again[1], again[0])
        step = tied(step, [*other, *before])
        third = across(step[1], step[0])
        return [[packs[0], step[0], other[1], third[1]], [packs[1], other[0], step[1], third[0]]]


def tied(arrays, first):
    count = len(arrays)
    hbm = pl.BlockSpec(memory_space=pltpu.HBM)
    return list(
        pl.pallas_call(
            lambda *refs: None,
            name="tied",
            in_specs=[hbm] * (count + len(first)),
            out_specs=[hbm] * count,
            out_shape=[like(*a.shape, dtype=a.dtype) for a in arrays],
            input_output_aliases={i: i for i in range(count)},
            compiler_params=pltpu.CompilerParams(vmem_limit_bytes=GRANT),
        )(*arrays, *first)
    )


def attend_forward(links, inputs, micro, attn_w, pos_row, blocks, only, later=()):
    rows, width = inputs.shape
    length = rows // micro
    latent_width = attn_w[0].shape[1]
    slots, block_rows = blocks

    def kernel(r):
        h = r.h.all()[...].astype(F32)
        normed_b = (h * inverse_rms(h)).astype(BF16)
        latent = dot_f32(normed_b, r.w_down.all()[...]).astype(BF16)
        queries = dot_f32(latent, r.w_qk.all()[...]).astype(BF16)
        r.latent.held[...] = latent
        r.queries.held[...] = queries
        causal = lax.broadcasted_iota(jnp.int32, (length, length), 0) >= lax.broadcasted_iota(
            jnp.int32, (length, length), 1
        )
        mixed = []
        for m in range(micro):
            part = slice(m * length, (m + 1) * length)
            scores = times_t(queries[part], latent[part]) * latent_width ** (-0.5)
            scores = jnp.where(causal, scores, -1e30)
            exponent = jnp.exp(scores - jnp.max(scores, axis=-1, keepdims=True))
            probs = exponent / jnp.sum(exponent, axis=-1, keepdims=True)
            r.probs.held[m] = probs
            mixed.append(dot_f32(probs.astype(BF16), latent[part]).astype(BF16))
        mixed = jnp.concatenate(mixed, axis=0)
        residual = (h + dot_f32(mixed, r.w_up.all()[...])).astype(BF16)
        r.residual.held[...] = residual
        r.residual.send()
        wide = residual.astype(F32)
        second_b = (wide * inverse_rms(wide)).astype(BF16)
        place_rows(r, r.pos_row.all()[...], second_b, slots, block_rows)
        r.mixed.held[...] = mixed
        if not links.pairwise:
            r.normed.held[...] = normed_b

    outs = dict(
        sent=[like(block_rows, width)] * (slots // block_rows),
        residual=like(rows, width),
        latent=like(rows, latent_width),
        queries=like(rows, latent_width),
        mixed=like(rows, latent_width),
        probs=like(micro, length, length, dtype=F32),
    )
    if not links.pairwise:
        outs.update(normed=like(rows, width))
    got = run(
        "attend_forward",
        kernel,
        dict(h=inputs, **dict(zip(ATTENTION, attn_w)), pos_row=pos_row),
        outs,
        later=later,
        only=only,
        place=links.place,
    )
    got.inputs = inputs
    return got


def early_factors(links, kept, only, merge=None, later=()):
    rows = kept.inputs.shape[0]
    latent_width = kept.latent.shape[1]

    def kernel(r):
        h = r.h.all()[...].astype(F32)
        normed_b = (h * inverse_rms(h)).astype(BF16)
        pack_factors(links, r, normed_b, [r.mixed.all()[...], r.latent.all()[...]])

    return as_list(
        run(
            "early_factors",
            kernel,
            dict(h=kept.inputs, mixed=kept.mixed, latent=kept.latent),
            dict(packs=pack_shapes(links, rows, latent_width)),
            pack_scratch(links, rows, latent_width),
            later=later,
            merge=merge,
            only=only,
            place=links.place,
        ).packs
    )


def place_rows(r, pos_row, values, slots, block_rows):
    shape = (slots, pos_row.shape[1])
    place = (pos_row == lax.broadcasted_iota(jnp.int32, shape, 0)).astype(BF16)
    for k in range(slots // block_rows):
        part = slice(k * block_rows, (k + 1) * block_rows)
        r.sent.held[part] = dot_f32(place[part], values).astype(BF16)
        r.sent.send(k)


def pack_shapes(links, rows, latent_width):
    return [like((links.experts + 2) * rows, latent_width)] * links.quarters


def pack_scratch(links, rows, latent_width):
    if not links.pairwise:
        return {}
    return dict(cols=pltpu.VMEM((links.experts * links.quarters, rows, latent_width), BF16))


def pack_factors(links, r, wide, narrow):
    rows, width = wide.shape
    experts, quarters = links.experts, links.quarters
    share = width // (experts * quarters)
    for i in range(experts * quarters):
        r.cols[i, :, :share] = wide[:, i * share : (i + 1) * share]
    expert, quarter = r.place[0], r.place[1]
    for k in range(quarters):
        out = r.packs.parts[k][1]
        for e in range(experts):
            out[e * rows : (e + 1) * rows] = r.cols[(expert ^ e) * quarters + (quarter ^ k)]
        for n, values in enumerate(narrow):
            out[(experts + n) * rows : (experts + n + 1) * rows] = values
        r.packs.send(k)


def picked_rows(r, rows):
    values = r.back.all()
    place = (
        r.pos_col.all()[...] == lax.broadcasted_iota(jnp.int32, (rows, values.shape[0]), 1)
    ).astype(BF16)
    return dot_f32(place, values[...])


def attend_backward(links, kept, micro, upstream, back, attn_w, pos_col, only, later=(), merge=None):
    inputs = kept.inputs
    rows, width = inputs.shape
    length = rows // micro
    latent_width = attn_w[0].shape[1]

    def kernel(r):
        u = r.u.all()[...].astype(F32)
        d_second = picked_rows(r, rows)
        wide = r.residual.all()[...].astype(F32)
        inv = inverse_rms(wide)
        d_res = u + rms_back(wide * inv, inv, d_second)
        d_res_b = d_res.astype(BF16)
        d_mixed = times_t(d_res_b, r.w_up.all()[...]).astype(BF16)
        latent, queries, all_probs = r.latent.all()[...], r.queries.all()[...], r.probs.all()
        d_latent, d_queries = [], []
        for m in range(micro):
            part = slice(m * length, (m + 1) * length)
            probs = all_probs[m]
            d_probs = times_t(d_mixed[part], latent[part])
            d_scores = (
                probs
                * (d_probs - jnp.sum(d_probs * probs, axis=-1, keepdims=True))
                * latent_width ** (-0.5)
            ).astype(BF16)
            d_queries.append(dot_f32(d_scores, latent[part]).astype(BF16))
            d_latent.append(
                t_times(probs.astype(BF16), d_mixed[part]) + t_times(d_scores, queries[part])
            )
        d_queries = jnp.concatenate(d_queries, axis=0)
        d_latent = jnp.concatenate(d_latent, axis=0) + times_t(d_queries, r.w_qk.all()[...])
        d_latent = d_latent.astype(BF16)
        if links.pairwise:
            pack_factors(links, r, d_res_b, [d_latent, d_queries])
        else:
            r.d_res.held[...] = d_res_b
            r.d_latent.held[...] = d_latent
            r.d_queries.held[...] = d_queries
        d_normed = times_t(d_latent, r.w_down.all()[...])
        h = r.h.all()[...].astype(F32)
        inv = inverse_rms(h)
        r.d_input.held[...] = (d_res + rms_back(h * inv, inv, d_normed)).astype(BF16)

    outs = dict(d_input=like(rows, width))
    if links.pairwise:
        outs.update(packs=pack_shapes(links, rows, latent_width))
    else:
        outs.update(
            d_res=like(rows, width),
            d_latent=like(rows, latent_width),
            d_queries=like(rows, latent_width),
        )
    return run(
        "attend_backward",
        kernel,
        dict(
            back=back,
            pos_col=pos_col,
            u=upstream,
            residual=kept.residual,
            latent=kept.latent,
            queries=kept.queries,
            probs=kept.probs,
            h=inputs,
            **dict(zip(ATTENTION, attn_w)),
        ),
        outs,
        pack_scratch(links, rows, latent_width),
        later=later,
        merge=merge,
        only=only,
        place=links.place,
    )


def scatter(links, upstream, gate_col, pos_row, blocks, only, later=()):
    width = upstream.shape[1]
    slots, block_rows = blocks

    def kernel(r):
        scaled = (r.u.all()[...].astype(F32) * r.gate.all()[...]).astype(BF16)
        place_rows(r, r.pos_row.all()[...], scaled, slots, block_rows)

    ins = dict(u=upstream, gate=gate_col, pos_row=pos_row)
    outs = dict(sent=[like(block_rows, width)] * (slots // block_rows))
    return run("scatter", kernel, ins, outs, later=later, only=only, place=links.place).sent


def combine(links, residual, back, gate_col, pos_col, only, merge=None):
    rows, width = residual.shape

    def kernel(r):
        mixture = picked_rows(r, rows) * r.gate.all()[...]
        r.out.held[...] = (r.residual.all()[...].astype(F32) + mixture).astype(BF16)

    ins = dict(back=back, pos_col=pos_col, gate=gate_col, residual=residual)
    outs = dict(out=like(rows, width))
    return run("combine", kernel, ins, outs, merge=merge, only=only, place=links.place).out


def pack_weights(links, weights, copies, later=(), only=None):
    gate_w, up_w, down_w = weights
    width, split = gate_w.shape
    count = width // split
    half = count // 2
    shape = (width + half * split, split)

    def body(place, gate, up, down, *refs):
        *outs, held0, held1, sems, out_sems = refs[len(later) :]

        def copy_all():
            moves = []
            for source, held, first in ((gate, held0, 0), (up, held1, half)):
                part = [(source, held.at[pl.ds(0, width)])]
                for j in range(half):
                    columns = pl.ds((first + j) * split, split)
                    part.append((down.at[:, columns], held.at[pl.ds(width + j * split, split)]))
                moves.append(part)
            loads = [
                [pltpu.make_async_copy(a, b, sems.at[i, j]) for j, (a, b) in enumerate(part)]
                for i, part in enumerate(moves)
            ]
            for load in loads[0] + loads[1]:
                load.start()
            stores = []
            for i, held in enumerate((held0, held1)):
                for load in loads[i]:
                    load.wait()
                for k in range(i, 2 * copies, 2):
                    stores.append(pltpu.make_async_copy(held, outs[k], out_sems.at[k]))
                    stores[-1].start()
            for store in stores:
                store.wait()

        if only is None:
            copy_all()
        else:
            pl.when(place[2] == only)(copy_all)

    hbm = pl.BlockSpec(memory_space=pltpu.HBM)
    return list(
        pl.pallas_call(
            body,
            name="pack_weights",
            in_specs=[pl.BlockSpec(memory_space=pltpu.SMEM)] + [hbm] * (3 + len(later)),
            out_specs=[hbm] * (2 * copies),
            out_shape=[like(*shape)] * (2 * copies),
            scratch_shapes=[
                pltpu.VMEM(shape, BF16),
                pltpu.VMEM(shape, BF16),
                pltpu.SemaphoreType.DMA((2, half + 1)),
                pltpu.SemaphoreType.DMA((2 * copies,)),
            ],
            compiler_params=pltpu.CompilerParams(vmem_limit_bytes=GRANT),
        )(links.place, gate_w, up_w, down_w, *later)
    )


def experts_call(links, packs, only, rows=None, pre=None, hidden=None, d_rows=None, forward=False, block_rows=None, before=None, last=True, later=()):
    quarters = len(packs[0])
    split = packs[0][0].shape[1]
    backward = d_rows is not None
    sources = as_list(rows if rows is not None else d_rows) if hidden is None else []
    if hidden is None:
        block_rows, count = sources[0].shape[0], len(sources)
        width = sources[0].shape[1]
        slots = block_rows * count
    else:
        slots = hidden[0].shape[0]
        count = slots // block_rows
        width = 2 * packs[0][0].shape[0] // 3
    blocks = width // split
    half = blocks // 2

    step = 2 * split if width % (2 * split) == 0 else split
    steps = [slice(c, c + step) for c in range(0, width, step)]

    def kernel(r):
        def copies(q):
            found = []
            for n, pack in enumerate((r.pack0[q], r.pack1[q])):
                if hidden is None:
                    found.append((pack.at[pl.ds(0, width)], (r.all0, r.all1)[n].at[q]))
                for j in range(half):
                    target = r.all2.at[q, :, pl.ds((n * half + j) * split, split)]
                    found.append((pack.at[pl.ds(width + j * split, split)], target))
            return [pltpu.make_async_copy(a, b, r.sems.at[q, i]) for i, (a, b) in enumerate(found)]

        loads = [copies(q) for q in range(quarters)]
        for copy in loads[0]:
            copy.start()
        r.open_rest()
        running = r.running if last else r.total.held

        def add(q, columns, part):
            part = part.astype(BF16).astype(F32)
            if q:
                part = part + running[:, columns]
            elif before is not None:
                part = part + r.before.all()[:, columns]
            if q == quarters - 1 and last:
                r.value.held[:, columns] = part.astype(BF16)
            else:
                running[:, columns] = part

        for q in range(quarters):
            for copy in loads[q]:
                copy.wait()
            if q + 1 < quarters:
                for copy in loads[q + 1]:
                    copy.start()
            if rows is not None:
                held = r.rows.all()[...]
                gate_pre, up_pre = dot_f32(held, r.all0[q]), dot_f32(held, r.all1[q])
                if not backward:
                    r.gate_out.parts[q][1][...] = gate_pre
                    r.gate_out.send(q)
                    r.up_out.parts[q][1][...] = up_pre
                    r.up_out.send(q)
            elif pre is not None:
                gate_pre, up_pre = r.gate_pre.block(q)[...], r.up_pre.block(q)[...]
            if hidden is not None:
                hidden_q = r.hidden.block(q)[...]
            else:
                activated, slope = silu_parts(gate_pre)
            if rows is not None:
                hidden_q = (activated * up_pre).astype(BF16)
                if backward:
                    r.hidden_out.parts[q][1][...] = hidden_q
                    r.hidden_out.send(q)
            if forward:
                for c in steps:
                    add(q, c, dot_f32(hidden_q, r.all2[q, :, c]))
            if backward:
                d_hidden = times_t(r.d_rows.all()[...], r.all2[q])
                d_gate = (d_hidden * up_pre * slope).astype(BF16)
                d_up = (d_hidden * activated).astype(BF16)
                for c in steps:
                    add(q, c, times_t(d_gate, r.all0[q, c]) + times_t(d_up, r.all1[q, c]))

    ins = {}
    if rows is not None:
        ins.update(rows=rows)
    if backward:
        ins.update(d_rows=d_rows)
    if pre is not None:
        ins.update(gate_pre=pre[0], up_pre=pre[1])
    if hidden is not None:
        ins.update(hidden=hidden)
    if before is not None:
        ins.update(before=before)
    if last:
        outs = dict(value=[like(block_rows, width)] * count)
    else:
        outs = dict(total=like(slots, width, dtype=F32))
    if rows is not None and backward:
        outs.update(hidden_out=[like(slots, split)] * quarters)
    elif rows is not None:
        made = [like(slots, split, dtype=F32)] * quarters
        outs.update(gate_out=made, up_out=made)
    flops = 2 * slots * width * split * quarters * 3
    scratch = dict(
        all2=pltpu.VMEM((quarters, split, width), BF16),
        sems=pltpu.SemaphoreType.DMA((quarters, blocks + 2)),
    )
    if hidden is None:
        weights = pltpu.VMEM((quarters, width, split), BF16)
        scratch.update(all0=weights, all1=weights)
    if last:
        scratch.update(running=pltpu.VMEM((slots, width), F32))
    return run(
        "experts",
        kernel,
        ins,
        outs,
        scratch,
        raw=dict(pack0=packs[0], pack1=packs[1]),
        first=2,
        later=later,
        flops=flops,
        only=only,
        place=links.place,
    )


def weight_gradients(links, early, late, width):
    experts, quarters = links.experts, links.quarters
    rows = early[0].shape[0] // (experts + 2)
    latent_width = early[0].shape[1]
    share, share_qk = width // (experts * quarters), latent_width // (experts * quarters)
    total = 2 * share + share_qk

    def plane_sums(r):
        def part(held, k, i, columns=latent_width):
            return held.block(k)[i * rows : (i + 1) * rows, :columns]

        sum_qk = jnp.zeros((latent_width, latent_width), F32)
        for k in range(quarters):
            sum_qk += t_times(part(r.early, k, experts + 1), part(r.late, k, experts + 1))
        r.qk[...] = sum_qk
        for e in range(experts):
            down = jnp.zeros((share, latent_width), F32)
            up = jnp.zeros((share, latent_width), F32)
            for k in range(quarters):
                down += t_times(part(r.early, k, e, share), part(r.late, k, experts))
                up += t_times(part(r.late, k, e, share), part(r.early, k, experts))
            at = pl.multiple_of(((r.place[0] ^ e) * quarters + r.place[1]) * share_qk, share_qk)
            made = r.away if e else r.own
            out = made.parts[max(e - 1, 0)][1]
            out[:share] = down.astype(out.dtype)
            out[share : 2 * share] = up.astype(out.dtype)
            out[2 * share :] = r.qk[pl.ds(at, share_qk)].astype(out.dtype)
            made.send(max(e - 1, 0))

    sums = run(
        "plane_sums",
        plane_sums,
        dict(early=early, late=late),
        dict(
            own=like(total, latent_width, dtype=F32),
            away=[like(total, latent_width)] * (experts - 1),
        ),
        dict(qk=pltpu.VMEM((latent_width, latent_width), F32)),
        place=links.place,
    )
    away = as_list(sums.away)
    got = [links.move(away[e - 1], links.every, expert_bits=e) for e in range(experts - 1, 0, -1)]

    def add(r):
        value = r.own.all()[...]
        for i in range(experts - 1):
            value = value + r.got.block(i)[...].astype(F32)
        r.down.held[...] = value[:share]
        r.up.held[...] = value[share : 2 * share]
        r.qk.held[...] = value[2 * share :]

    done = run(
        "add_planes",
        add,
        dict(own=sums.own, got=got),
        dict(
            down=like(share, latent_width, dtype=F32),
            qk=like(share_qk, latent_width, dtype=F32),
            up=like(share, latent_width, dtype=F32),
        ),
    )
    return done.down, done.qk, done.up


def spread(links, rows):
    length, width = rows.shape
    count = links.experts * links.quarters
    by_owner = rows.reshape(length, count, width // count).transpose(1, 0, 2)
    got = lax.all_to_all(by_owner, ("expert", "dp"), split_axis=0, concat_axis=0, tiled=True)
    return got.reshape(count * length, width // count)


def nearer(packs):
    return [pack[:-1] for pack in packs]


def farthest(packs):
    return [pack[-1:] for pack in packs]


def body(x_in, dy_out, routes, gates, w_down, w_qk, w_up, e_gate, e_up, e_down):
    links = Links()
    micro, _, length, width = x_in.shape
    rows = micro * length
    capacity = max(2, (3 * length + 2 * links.experts - 1) // (2 * links.experts))
    attn_w = (w_down[0], w_qk[0], w_up[0])
    first = links.section == 0

    route = routes[0, :, 0, :, 0]
    earlier = lax.broadcasted_iota(jnp.int32, (length, length), 0) > lax.broadcasted_iota(
        jnp.int32, (length, length), 1
    )
    same = route[:, :, None] == route[:, None, :]
    rank = jnp.sum((same & earlier).astype(jnp.int32), axis=2)
    slot = jnp.arange(micro, dtype=jnp.int32)[:, None] * capacity + rank
    position = (links.relative(route) * (micro * capacity) + slot).reshape(rows)
    pos_row, pos_col = position.reshape(1, rows), position.reshape(rows, 1)
    gate_col = gates[0, :, 0].reshape(rows, 1)
    slots = links.experts * micro * capacity
    blocks = (slots, micro * capacity if links.pairwise else slots)

    own = (e_gate[0, 0], e_up[0, 0], e_down[0, 0])
    packed = pack_weights(links, own, 1)
    dy = dy_out.reshape(rows, width)
    sent_1 = scatter(links, dy, gate_col, pos_row, blocks, 1)
    kept_0 = attend_forward(
        links, x_in.reshape(rows, width), micro, attn_w, pos_row, blocks, 0, as_list(sent_1)[:1]
    )
    dm_1 = links.exchange(sent_1, 1)
    rows_0 = links.exchange(kept_0.sent, 0)
    set_0 = links.gather_quarters(packed, 0, as_list(rows_0))
    near_0 = experts_call(links, nearer(set_0), 0, rows=rows_0, forward=True, last=False)
    there = tied(
        [kept_0.latent[:16, :128]], [*set_0[0][1:], *set_0[1][1:], near_0.total]
    )
    there = links.move(there[0], (0,), section_bit=1)
    packed_1 = pack_weights(links, own, 2, [there, *as_list(dm_1)], 1)
    made_0 = experts_call(links, farthest(set_0), 0, rows=rows_0, forward=True, before=near_0.total, later=[there])
    pre_0 = [
        as_list(near_0.gate_out) + as_list(made_0.gate_out),
        as_list(near_0.up_out) + as_list(made_0.up_out),
    ]
    returned_0 = links.exchange(made_0.value, 0)
    out_0 = combine(links, kept_0.residual, returned_0, gate_col, pos_col, 0)
    h_1 = links.move(out_0, (0,), section_bit=1)
    kept_1 = attend_forward(links, h_1, micro, attn_w, pos_row, blocks, 1)
    sent = as_list(kept_1.sent)
    set_1 = links.gather_quarters(packed_1, 1, sent[:1], as_list(returned_0))
    if links.pairwise:
        sent = [sent[0], *tied(sent[1:], [set_1[0][1]])]
        rows_1 = links.exchange(sent, 1)
        early = early_factors(links, kept_0, 0)
        early = early_factors(links, kept_1, 1, dict(packs=early), rows_1)
    else:
        rows_1 = links.exchange(kept_1.sent, 1)
    set_1 = [[mine] + got[1:] for mine, got in zip(packed, set_1)]
    near_1 = experts_call(links, nearer(set_1), 1, rows=rows_1, d_rows=dm_1, last=False)
    made_1 = experts_call(links, farthest(set_1), 1, rows=rows_1, d_rows=dm_1, before=near_1.total)
    hidden_1 = as_list(near_1.hidden_out) + as_list(made_1.hidden_out)
    back_1 = links.exchange(made_1.value, 1)
    value_1 = experts_call(
        links, set_1, 1, hidden=hidden_1, forward=True, block_rows=blocks[1]
    ).value
    returned_1 = links.exchange(value_1, 1)
    late_1 = attend_backward(
        links, kept_1, micro, dy, back_1, attn_w, pos_col, 1, as_list(value_1)[:1]
    )
    u_0 = links.move(late_1.d_input, (1,), section_bit=1)
    sent_0 = scatter(links, u_0, gate_col, pos_row, blocks, 0, as_list(returned_1))
    dm_0 = links.exchange(sent_0, 0)
    back_0 = experts_call(links, set_0, 0, pre=pre_0, d_rows=dm_0).value
    merge = dict(d_input=late_1.d_input)
    if links.pairwise:
        merge.update(packs=late_1.packs)
    late_0 = attend_backward(
        links, kept_0, micro, u_0, links.exchange(back_0, 0), attn_w, pos_col, 0, merge=merge
    )
    grads_in = late_0.d_input.reshape(1, micro, 1, length, width)
    activations = combine(
        links, kept_1.residual, returned_1, gate_col, pos_col, 1, dict(out=out_0)
    ).reshape(1, micro, 1, length, width)

    if links.pairwise:
        def plane(packs):
            return packs[:1] + [
                links.move(packs[k], links.every, quarter_bits=k) for k in range(1, links.quarters)
            ]

        g_down, g_qk, g_up_t = weight_gradients(links, plane(early), plane(late_0.packs), width)
    else:
        def pick(upper, lower):
            return jnp.where(first, upper, lower)

        def gathered(upper, lower):
            return lax.all_gather(pick(upper, lower), ("expert", "dp"), axis=0, tiled=True)

        g_down = t_times(
            spread(links, pick(kept_0.normed, kept_1.normed)),
            gathered(late_0.d_latent, late_1.d_latent),
        )
        g_qk = t_times(
            spread(links, pick(kept_0.latent, kept_1.latent)),
            gathered(late_0.d_queries, late_1.d_queries),
        )
        g_up_t = t_times(
            spread(links, pick(late_0.d_res, late_1.d_res)),
            gathered(kept_0.mixed, kept_1.mixed),
        )
    return (activations, grads_in, g_down[None], g_qk[None], g_up_t[None])


def solution(mesh):
    by_sequence = P(None, ("expert", "dp"), None, None)
    by_layer = P("section", None, ("expert", "dp"), None, None)
    shared = P("section", None, None)
    placed = (
        by_sequence,
        by_sequence,
        by_layer,
        by_layer,
        shared,
        shared,
        shared,
        P("section", "expert", None, "dp"),
        P("section", "expert", None, "dp"),
        P("section", "expert", "dp", None),
    )
    by_rows = P("section", ("expert", "dp"), None)
    return jax.shard_map(
        body,
        mesh=mesh,
        in_specs=placed,
        out_specs=(by_layer, by_layer, by_rows, by_rows, by_rows),
        check_vma=False,
    )
```

```python
from types import SimpleNamespace

import jax
import jax.numpy as jnp
from jax import lax
from jax.experimental import pallas as pl
from jax.experimental.pallas import tpu as pltpu
from jax.sharding import PartitionSpec as P

epsilon = 1e-06
AXES = ("section", "expert", "dp")
GRANT = 62 << 20
ATTENTION = ("w_down", "w_qk", "w_up")
BF16, F32 = jnp.bfloat16, jnp.float32


def dot_f32(left, right):
    return jnp.dot(left, right, preferred_element_type=F32)


def times_t(left, right):
    return lax.dot_general(left, right, (((1,), (1,)), ((), ())), preferred_element_type=F32)


def t_times(left, right):
    return lax.dot_general(left, right, (((0,), (0,)), ((), ())), preferred_element_type=F32)


def inverse_rms(values):
    return lax.rsqrt(jnp.mean(values * values, axis=-1, keepdims=True) + epsilon)


def rms_back(normed, inv_rms, upstream):
    return inv_rms * (upstream - normed * jnp.mean(upstream * normed, axis=-1, keepdims=True))


def silu_parts(gate_pre):
    sigmoid = jax.nn.sigmoid(gate_pre)
    return (gate_pre * sigmoid, sigmoid * (1.0 + gate_pre * (1.0 - sigmoid)))


class Held:
    def __init__(self, refs, held, sems):
        self.held, self.parts, self.seen = held, [], set()
        start = 0
        for i, ref in enumerate(refs):
            target = held
            if len(refs) > 1:
                target = held.at[pl.ds(start, ref.shape[0])]
                start += ref.shape[0]
            self.parts.append((pltpu.make_async_copy(ref, target, sems.at[i]), target))

    def start(self, i):
        if i < len(self.parts):
            self.parts[i][0].start()

    def block(self, i):
        if i not in self.seen:
            self.seen.add(i)
            self.parts[i][0].wait()
        return self.parts[i][1]

    def all(self):
        for i in range(len(self.parts)):
            self.block(i)
        return self.held


class Made:
    def __init__(self, refs, held, sems):
        self.held, self.parts, self.sent = held, [], set()
        start = 0
        for i, ref in enumerate(refs):
            source = held
            if len(refs) > 1:
                source = held.at[pl.ds(start, ref.shape[0])]
                start += ref.shape[0]
            self.parts.append((pltpu.make_async_copy(source, ref, sems.at[i]), source))

    def send(self, i=0):
        if i not in self.sent:
            self.sent.add(i)
            self.parts[i][0].start()

    def finish(self):
        for i, (copy, _) in enumerate(self.parts):
            self.send(i)
        for copy, _ in self.parts:
            copy.wait()


def as_list(value):
    return list(value) if isinstance(value, (list, tuple)) else [value]


def stage_shape(arrays):
    if len(arrays) == 1:
        return pltpu.VMEM(arrays[0].shape, arrays[0].dtype)
    rows = sum(a.shape[0] for a in arrays)
    return pltpu.VMEM((rows, *arrays[0].shape[1:]), arrays[0].dtype)


def run(name, kernel, ins, outs, scratch=None, vmem=None, later=(), merge=None, only=None, place=None, raw=None, first=99, flops=0):
    scratch, vmem, merge, raw = scratch or {}, vmem or {}, merge or {}, raw or {}
    ins = {k: as_list(v) for k, v in ins.items()}
    outs = {k: as_list(v) for k, v in outs.items()}
    merge = {k: as_list(v) for k, v in merge.items()}
    flat_in = [a for v in ins.values() for a in v]
    flat_out = [a for v in outs.values() for a in v]
    flat_merge = [a for v in merge.values() for a in v]
    stages = [stage_shape(v) for v in [*ins.values(), *outs.values()]]
    sems = [pltpu.SemaphoreType.DMA((len(v),)) for v in [*ins.values(), *outs.values()]]
    smem = [] if place is None else [place]

    def body(*refs):
        refs = list(refs)

        def take(count):
            got = refs[:count]
            del refs[:count]
            return got

        place_refs, vmem_refs = take(len(smem)), take(len(vmem))
        in_refs = [take(len(v)) for v in ins.values()]
        instead = {k: take(len(v)) for k, v in merge.items()}
        raw_refs = {k: take(len(v)) for k, v in raw.items()}
        take(len(later))
        out_refs = [take(len(v)) for v in outs.values()]
        staged, signals = take(len(stages)), take(len(sems))
        r = SimpleNamespace(**dict(zip(vmem, vmem_refs)))
        if smem:
            r.place = place_refs[0]
        held = [Held(a, b, c) for a, b, c in zip(in_refs, staged, signals)]
        made = [Made(a, b, c) for a, b, c in zip(out_refs, staged[len(ins) :], signals[len(ins) :])]
        r.__dict__.update(zip(ins, held))
        r.__dict__.update(zip(outs, made))
        r.__dict__.update(zip(scratch, refs))

        r.__dict__.update(raw_refs)

        def open_all(part):
            for i in range(max([len(h.parts) for h in part], default=0)):
                for h in part:
                    h.start(i)

        r.open_rest = lambda: open_all(held[first:])

        def work():
            open_all(held[:first])
            if first >= len(held):
                r.open_rest()
            kernel(r)
            for h in held:
                h.all()
            for m in made:
                m.finish()

        def passed_on():
            for k, m, sem in zip(outs, made, signals[len(ins) :]):
                parts = list(zip(instead.get(k, ()), m.parts))
                loads = [
                    pltpu.make_async_copy(ref, part[1], sem.at[i]) for i, (ref, part) in enumerate(parts)
                ]
                for load in loads:
                    load.start()
                for load, (_, part) in zip(loads, parts):
                    load.wait()
                    part[0].start()
                for _, part in parts:
                    part[0].wait()

        if only is None:
            work()
        else:
            pl.when(r.place[2] == only)(work)
            if merge:
                pl.when(r.place[2] != only)(passed_on)

    flat_raw = [a for v in raw.values() for a in v]
    everything = [*smem, *vmem.values(), *flat_in, *flat_merge, *flat_raw, *later]
    spaces = [pltpu.SMEM] * len(smem) + [pltpu.VMEM] * len(vmem)
    spaces += [pltpu.HBM] * (len(everything) - len(spaces))
    got = pl.pallas_call(
        body,
        name=name,
        in_specs=[pl.BlockSpec(memory_space=s) for s in spaces],
        out_specs=[pl.BlockSpec(memory_space=pltpu.HBM) for _ in flat_out],
        out_shape=flat_out,
        scratch_shapes=[*stages, *sems, *scratch.values()],
        compiler_params=pltpu.CompilerParams(vmem_limit_bytes=GRANT),
        cost_estimate=pl.CostEstimate(
            flops=flops,
            bytes_accessed=sum(a.size * a.dtype.itemsize for a in flat_in),
            transcendentals=0,
        ),
    )(*everything)
    got, result = list(got), SimpleNamespace()
    for k, v in outs.items():
        part, got = got[: len(v)], got[len(v) :]
        setattr(result, k, part if len(part) > 1 else part[0])
    return result


def like(*shape, dtype=BF16):
    return jax.ShapeDtypeStruct(shape, dtype)


class Links:
    def __init__(self):
        self.sections, self.experts, self.quarters = [lax.axis_size(a) for a in AXES]
        self.section, self.expert, self.quarter = [lax.axis_index(a) for a in AXES]
        self.pairwise = self.experts <= 8
        self.every = tuple(range(self.sections))
        self.place = jnp.stack([self.expert, self.quarter, self.section])

    def move(self, x, sections, section_bit=0, expert_bits=0, quarter_bits=0):
        def number(s, e, d):
            return (s * self.experts + e) * self.quarters + d

        pairs = [
            (number(s, e, d), number(s ^ section_bit, e ^ expert_bits, d ^ quarter_bits))
            for s in sections
            for e in range(self.experts)
            for d in range(self.quarters)
        ]
        return lax.ppermute(x, AXES, pairs)

    def relative(self, expert):
        return expert ^ self.expert if self.pairwise else expert

    def exchange_over(self, blocks, section):
        got = {
            k: self.move(blocks[k], (section,), section_bit=1, expert_bits=k)
            for k in range(self.experts - 1, -1, -1)
        }
        return [got[k] for k in range(self.experts)]

    def exchange(self, blocks, section):
        if not self.pairwise:
            sent = blocks.reshape(self.experts, -1, blocks.shape[1])
            out = lax.all_to_all(sent, "expert", split_axis=0, concat_axis=0, tiled=True)
            return out.reshape(blocks.shape)
        got = {k: self.move(blocks[k], (section,), expert_bits=k) for k in range(self.experts - 1, 0, -1)}
        return [blocks[0]] + [got[k] for k in range(1, self.experts)]

    def gather_quarters(self, packs, section, before=(), between=()):
        if self.quarters != 4:
            return [
                [p] + [self.move(p, (section,), quarter_bits=k) for k in range(1, self.quarters)]
                for p in packs[:2]
            ]

        def across(one, two):
            return [
                self.move(one, (section,), quarter_bits=1),
                self.move(two, (section,), quarter_bits=2),
            ]

        step = across(packs[0], packs[1])
        again = tied(packs[2:], between) if between else packs
        other = across(again[1], again[0])
        step = tied(step, [*other, *before])
        third = across(step[1], step[0])
        return [[packs[0], step[0], other[1], third[1]], [packs[1], other[0], step[1], third[0]]]


def tied(arrays, first):
    count = len(arrays)
    hbm = pl.BlockSpec(memory_space=pltpu.HBM)
    return list(
        pl.pallas_call(
            lambda *refs: None,
            name="tied",
            in_specs=[hbm] * (count + len(first)),
            out_specs=[hbm] * count,
            out_shape=[like(*a.shape, dtype=a.dtype) for a in arrays],
            input_output_aliases={i: i for i in range(count)},
            compiler_params=pltpu.CompilerParams(vmem_limit_bytes=GRANT),
        )(*arrays, *first)
    )


def attend_forward(links, inputs, micro, attn_w, pos_row, blocks, only, later=()):
    rows, width = inputs.shape
    length = rows // micro
    latent_width = attn_w[0].shape[1]
    slots, block_rows = blocks

    def kernel(r):
        h = r.h.all()[...].astype(F32)
        r.open_rest()
        normed_b = (h * inverse_rms(h)).astype(BF16)
        latent = dot_f32(normed_b, r.w_down.all()[...]).astype(BF16)
        queries = dot_f32(latent, r.w_qk.all()[...]).astype(BF16)
        r.latent.held[...] = latent
        r.queries.held[...] = queries
        causal = lax.broadcasted_iota(jnp.int32, (length, length), 0) >= lax.broadcasted_iota(
            jnp.int32, (length, length), 1
        )
        mixed = []
        for m in range(micro):
            part = slice(m * length, (m + 1) * length)
            scores = times_t(queries[part], latent[part]) * latent_width ** (-0.5)
            scores = jnp.where(causal, scores, -1e30)
            exponent = jnp.exp(scores - jnp.max(scores, axis=-1, keepdims=True))
            probs = exponent / jnp.sum(exponent, axis=-1, keepdims=True)
            r.probs.held[m] = probs
            mixed.append(dot_f32(probs.astype(BF16), latent[part]).astype(BF16))
        mixed = jnp.concatenate(mixed, axis=0)
        residual = (h + dot_f32(mixed, r.w_up.all()[...])).astype(BF16)
        r.residual.held[...] = residual
        r.residual.send()
        wide = residual.astype(F32)
        second_b = (wide * inverse_rms(wide)).astype(BF16)
        place_rows(r, r.pos_row.all()[...], second_b, slots, block_rows)
        r.mixed.held[...] = mixed
        if not links.pairwise:
            r.normed.held[...] = normed_b

    outs = dict(
        sent=[like(block_rows, width)] * (slots // block_rows),
        residual=like(rows, width),
        latent=like(rows, latent_width),
        queries=like(rows, latent_width),
        mixed=like(rows, latent_width),
        probs=like(micro, length, length, dtype=F32),
    )
    if not links.pairwise:
        outs.update(normed=like(rows, width))
    got = run(
        "attend_forward",
        kernel,
        dict(h=inputs, **dict(zip(ATTENTION, attn_w)), pos_row=pos_row),
        outs,
        first=2,
        later=later,
        only=only,
        place=links.place,
    )
    got.inputs = inputs
    return got


def factors(links, wide, narrow, only, normalize, merge=None, later=()):
    rows = wide.shape[0]
    latent_width = narrow[0].shape[1]

    def kernel(r):
        values = r.wide.all()[...]
        if normalize:
            h = values.astype(F32)
            values = (h * inverse_rms(h)).astype(BF16)
        pack_factors(links, r, values, [r.narrow.block(0)[...], r.narrow.block(1)[...]])

    return as_list(
        run(
            "factors",
            kernel,
            dict(wide=wide, narrow=narrow),
            dict(packs=pack_shapes(links, rows, latent_width)),
            pack_scratch(links, rows, latent_width),
            later=later,
            merge=merge,
            only=only,
            place=links.place,
        ).packs
    )


def place_rows(r, pos_row, values, slots, block_rows):
    shape = (slots, pos_row.shape[1])
    place = (pos_row == lax.broadcasted_iota(jnp.int32, shape, 0)).astype(BF16)
    for k in range(slots // block_rows):
        part = slice(k * block_rows, (k + 1) * block_rows)
        r.sent.held[part] = dot_f32(place[part], values).astype(BF16)
        r.sent.send(k)


def pack_shapes(links, rows, latent_width):
    return [like((links.experts + 2) * rows, latent_width)] * links.quarters


def pack_scratch(links, rows, latent_width):
    if not links.pairwise:
        return {}
    return dict(cols=pltpu.VMEM((links.experts * links.quarters, rows, latent_width), BF16))


def pack_factors(links, r, wide, narrow):
    rows, width = wide.shape
    experts, quarters = links.experts, links.quarters
    share = width // (experts * quarters)
    for i in range(experts * quarters):
        r.cols[i, :, :share] = wide[:, i * share : (i + 1) * share]
    expert, quarter = r.place[0], r.place[1]
    for k in range(quarters):
        out = r.packs.parts[k][1]
        for e in range(experts):
            out[e * rows : (e + 1) * rows] = r.cols[(expert ^ e) * quarters + (quarter ^ k)]
        for n, values in enumerate(narrow):
            out[(experts + n) * rows : (experts + n + 1) * rows] = values
        r.packs.send(k)


def picked_rows(r, rows):
    values = r.back.all()
    place = (
        r.pos_col.all()[...] == lax.broadcasted_iota(jnp.int32, (rows, values.shape[0]), 1)
    ).astype(BF16)
    return dot_f32(place, values[...])


def attend_backward(links, kept, micro, upstream, back, attn_w, pos_col, only, later=(), merge=None, onward=None):
    inputs = kept.inputs
    rows, width = inputs.shape
    length = rows // micro
    latent_width = attn_w[0].shape[1]
    packed = links.pairwise and not onward

    def kernel(r):
        r.back.all()
        r.open_rest()
        d_second = picked_rows(r, rows)
        u = r.u.all()[...].astype(F32)
        wide = r.residual.all()[...].astype(F32)
        inv = inverse_rms(wide)
        d_res = u + rms_back(wide * inv, inv, d_second)
        d_res_b = d_res.astype(BF16)
        d_mixed = times_t(d_res_b, r.w_up.all()[...]).astype(BF16)
        latent, queries, all_probs = r.latent.all()[...], r.queries.all()[...], r.probs.all()
        d_latent, d_queries = [], []
        for m in range(micro):
            part = slice(m * length, (m + 1) * length)
            probs = all_probs[m]
            d_probs = times_t(d_mixed[part], latent[part])
            d_scores = (
                probs
                * (d_probs - jnp.sum(d_probs * probs, axis=-1, keepdims=True))
                * latent_width ** (-0.5)
            ).astype(BF16)
            d_queries.append(dot_f32(d_scores, latent[part]).astype(BF16))
            d_latent.append(
                t_times(probs.astype(BF16), d_mixed[part]) + t_times(d_scores, queries[part])
            )
        d_queries = jnp.concatenate(d_queries, axis=0)
        d_latent = jnp.concatenate(d_latent, axis=0) + times_t(d_queries, r.w_qk.all()[...])
        d_latent = d_latent.astype(BF16)
        if packed:
            pack_factors(links, r, d_res_b, [d_latent, d_queries])
        else:
            r.d_res.held[...] = d_res_b
            r.d_latent.held[...] = d_latent
            r.d_queries.held[...] = d_queries
        d_normed = times_t(d_latent, r.w_down.all()[...])
        h = r.h.all()[...].astype(F32)
        inv = inverse_rms(h)
        d_input = (d_res + rms_back(h * inv, inv, d_normed)).astype(BF16)
        if onward:
            scaled = (d_input.astype(F32) * r.gate.all()[...]).astype(BF16)
            place_rows(r, r.pos_row.all()[...], scaled, slots, block_rows)
        r.d_input.held[...] = d_input

    outs = dict(d_input=like(rows, width))
    ins = {}
    if onward:
        ins, (slots, block_rows) = dict(pos_row=onward[0], gate=onward[1]), onward[2]
        outs.update(sent=[like(block_rows, width)] * (slots // block_rows))
    if packed:
        outs.update(packs=pack_shapes(links, rows, latent_width))
    else:
        outs.update(
            d_res=like(rows, width),
            d_latent=like(rows, latent_width),
            d_queries=like(rows, latent_width),
        )
    return run(
        "attend_backward",
        kernel,
        dict(
            back=back,
            pos_col=pos_col,
            u=upstream,
            residual=kept.residual,
            w_up=attn_w[2],
            latent=kept.latent,
            queries=kept.queries,
            probs=kept.probs,
            w_qk=attn_w[1],
            w_down=attn_w[0],
            h=inputs,
            **ins,
        ),
        outs,
        pack_scratch(links, rows, latent_width) if packed else None,
        first=4,
        later=later,
        merge=merge,
        only=only,
        place=links.place,
    )


def scatter(links, upstream, gate_col, pos_row, blocks, only, later=()):
    width = upstream.shape[1]
    slots, block_rows = blocks

    def kernel(r):
        scaled = (r.u.all()[...].astype(F32) * r.gate.all()[...]).astype(BF16)
        place_rows(r, r.pos_row.all()[...], scaled, slots, block_rows)

    ins = dict(u=upstream, gate=gate_col, pos_row=pos_row)
    outs = dict(sent=[like(block_rows, width)] * (slots // block_rows))
    return run("scatter", kernel, ins, outs, later=later, only=only, place=links.place).sent


def combine(links, residual, back, gate_col, pos_col, only, merge=None):
    rows, width = residual.shape

    def kernel(r):
        mixture = picked_rows(r, rows) * r.gate.all()[...]
        r.out.held[...] = (r.residual.all()[...].astype(F32) + mixture).astype(BF16)

    ins = dict(back=back, pos_col=pos_col, gate=gate_col, residual=residual)
    outs = dict(out=like(rows, width))
    return run("combine", kernel, ins, outs, merge=merge, only=only, place=links.place).out


def pack_weights(links, weights, copies, later=(), only=None):
    gate_w, up_w, down_w = weights
    width, split = gate_w.shape
    count = width // split
    half = count // 2
    shape = (width + half * split, split)

    def body(place, gate, up, down, *refs):
        *outs, held0, held1, sems, out_sems = refs[len(later) :]

        def copy_all():
            moves = []
            for source, held, first in ((gate, held0, 0), (up, held1, half)):
                part = [(source, held.at[pl.ds(0, width)])]
                for j in range(half):
                    columns = pl.ds((first + j) * split, split)
                    part.append((down.at[:, columns], held.at[pl.ds(width + j * split, split)]))
                moves.append(part)
            loads = [
                [pltpu.make_async_copy(a, b, sems.at[i, j]) for j, (a, b) in enumerate(part)]
                for i, part in enumerate(moves)
            ]
            for load in loads[0] + loads[1]:
                load.start()
            stores = []
            for i, held in enumerate((held0, held1)):
                for load in loads[i]:
                    load.wait()
                for k in range(i, 2 * copies, 2):
                    stores.append(pltpu.make_async_copy(held, outs[k], out_sems.at[k]))
                    stores[-1].start()
            for store in stores:
                store.wait()

        if only is None:
            copy_all()
        else:
            pl.when(place[2] == only)(copy_all)

    hbm = pl.BlockSpec(memory_space=pltpu.HBM)
    return list(
        pl.pallas_call(
            body,
            name="pack_weights",
            in_specs=[pl.BlockSpec(memory_space=pltpu.SMEM)] + [hbm] * (3 + len(later)),
            out_specs=[hbm] * (2 * copies),
            out_shape=[like(*shape)] * (2 * copies),
            scratch_shapes=[
                pltpu.VMEM(shape, BF16),
                pltpu.VMEM(shape, BF16),
                pltpu.SemaphoreType.DMA((2, half + 1)),
                pltpu.SemaphoreType.DMA((2 * copies,)),
            ],
            compiler_params=pltpu.CompilerParams(vmem_limit_bytes=GRANT),
        )(links.place, gate_w, up_w, down_w, *later)
    )


def experts_call(links, packs, only, rows=None, pre=None, hidden=None, d_rows=None, forward=False, block_rows=None, before=None, last=True, later=()):
    quarters = len(packs[0])
    split = packs[0][0].shape[1]
    backward = d_rows is not None
    sources = as_list(rows if rows is not None else d_rows) if hidden is None else []
    if hidden is None:
        block_rows, count = sources[0].shape[0], len(sources)
        width = sources[0].shape[1]
        slots = block_rows * count
    else:
        slots = hidden[0].shape[0]
        count = slots // block_rows
        width = 2 * packs[0][0].shape[0] // 3
    blocks = width // split
    half = blocks // 2

    step = 2 * split if width % (2 * split) == 0 else split
    steps = [slice(c, c + step) for c in range(0, width, step)]

    def kernel(r):
        def copies(q):
            found = []
            for n, pack in enumerate((r.pack0[q], r.pack1[q])):
                if hidden is None:
                    found.append((pack.at[pl.ds(0, width)], (r.all0, r.all1)[n].at[q]))
                for j in range(half):
                    target = r.all2.at[q, :, pl.ds((n * half + j) * split, split)]
                    found.append((pack.at[pl.ds(width + j * split, split)], target))
            return [pltpu.make_async_copy(a, b, r.sems.at[q, i]) for i, (a, b) in enumerate(found)]

        loads = [copies(q) for q in range(quarters)]
        for copy in loads[0]:
            copy.start()
        r.open_rest()
        running = r.running if last else r.total.held

        def add(q, columns, part):
            part = part.astype(BF16).astype(F32)
            if q:
                part = part + running[:, columns]
            elif before is not None:
                part = part + r.before.all()[:, columns]
            if q == quarters - 1 and last:
                r.value.held[:, columns] = part.astype(BF16)
            else:
                running[:, columns] = part

        for q in range(quarters):
            for copy in loads[q]:
                copy.wait()
            if q + 1 < quarters:
                for copy in loads[q + 1]:
                    copy.start()
            if rows is not None:
                held = r.rows.all()[...]
                gate_pre, up_pre = dot_f32(held, r.all0[q]), dot_f32(held, r.all1[q])
                if not backward:
                    r.gate_out.parts[q][1][...] = gate_pre
                    r.gate_out.send(q)
                    r.up_out.parts[q][1][...] = up_pre
                    r.up_out.send(q)
            elif pre is not None:
                gate_pre, up_pre = r.gate_pre.block(q)[...], r.up_pre.block(q)[...]
            if hidden is not None:
                hidden_q = r.hidden.block(q)[...]
            else:
                activated, slope = silu_parts(gate_pre)
            if rows is not None:
                hidden_q = (activated * up_pre).astype(BF16)
                if backward:
                    r.hidden_out.parts[q][1][...] = hidden_q
                    r.hidden_out.send(q)
            if forward:
                for c in steps:
                    add(q, c, dot_f32(hidden_q, r.all2[q, :, c]))
            if backward:
                d_hidden = times_t(r.d_rows.all()[...], r.all2[q])
                d_gate = (d_hidden * up_pre * slope).astype(BF16)
                d_up = (d_hidden * activated).astype(BF16)
                for c in steps:
                    add(q, c, times_t(d_gate, r.all0[q, c]) + times_t(d_up, r.all1[q, c]))

    ins = {}
    if rows is not None:
        ins.update(rows=rows)
    if backward:
        ins.update(d_rows=d_rows)
    if pre is not None:
        ins.update(gate_pre=pre[0], up_pre=pre[1])
    if hidden is not None:
        ins.update(hidden=hidden)
    if before is not None:
        ins.update(before=before)
    if last:
        outs = dict(value=[like(block_rows, width)] * count)
    else:
        outs = dict(total=like(slots, width, dtype=F32))
    if rows is not None and backward:
        outs.update(hidden_out=[like(slots, split)] * quarters)
    elif rows is not None:
        made = [like(slots, split, dtype=F32)] * quarters
        outs.update(gate_out=made, up_out=made)
    flops = 2 * slots * width * split * quarters * 3
    scratch = dict(
        all2=pltpu.VMEM((quarters, split, width), BF16),
        sems=pltpu.SemaphoreType.DMA((quarters, blocks + 2)),
    )
    if hidden is None:
        weights = pltpu.VMEM((quarters, width, split), BF16)
        scratch.update(all0=weights, all1=weights)
    if last:
        scratch.update(running=pltpu.VMEM((slots, width), F32))
    return run(
        "experts",
        kernel,
        ins,
        outs,
        scratch,
        raw=dict(pack0=packs[0], pack1=packs[1]),
        first=2,
        later=later,
        flops=flops,
        only=only,
        place=links.place,
    )


def weight_gradients(links, early, late, width):
    experts, quarters = links.experts, links.quarters
    rows = early[0].shape[0] // (experts + 2)
    latent_width = early[0].shape[1]
    share, share_qk = width // (experts * quarters), latent_width // (experts * quarters)
    total = 2 * share + share_qk

    def plane_sums(r):
        def part(held, k, i, columns=latent_width):
            return held.block(k)[i * rows : (i + 1) * rows, :columns]

        sum_qk = jnp.zeros((latent_width, latent_width), F32)
        for k in range(quarters):
            sum_qk += t_times(part(r.early, k, experts + 1), part(r.late, k, experts + 1))
        r.qk[...] = sum_qk
        for e in range(experts):
            down = jnp.zeros((share, latent_width), F32)
            up = jnp.zeros((share, latent_width), F32)
            for k in range(quarters):
                down += t_times(part(r.early, k, e, share), part(r.late, k, experts))
                up += t_times(part(r.late, k, e, share), part(r.early, k, experts))
            at = pl.multiple_of(((r.place[0] ^ e) * quarters + r.place[1]) * share_qk, share_qk)
            made = r.away if e else r.own
            out = made.parts[max(e - 1, 0)][1]
            out[:share] = down.astype(out.dtype)
            out[share : 2 * share] = up.astype(out.dtype)
            out[2 * share :] = r.qk[pl.ds(at, share_qk)].astype(out.dtype)
            made.send(max(e - 1, 0))

    sums = run(
        "plane_sums",
        plane_sums,
        dict(early=early, late=late),
        dict(
            own=like(total, latent_width, dtype=F32),
            away=[like(total, latent_width)] * (experts - 1),
        ),
        dict(qk=pltpu.VMEM((latent_width, latent_width), F32)),
        place=links.place,
    )
    away = as_list(sums.away)
    got = [links.move(away[e - 1], links.every, expert_bits=e) for e in range(experts - 1, 0, -1)]

    value = sums.own + sum(g.astype(F32) for g in got)
    return value[:share], value[2 * share :], value[share : 2 * share]


def spread(links, rows):
    length, width = rows.shape
    count = links.experts * links.quarters
    by_owner = rows.reshape(length, count, width // count).transpose(1, 0, 2)
    got = lax.all_to_all(by_owner, ("expert", "dp"), split_axis=0, concat_axis=0, tiled=True)
    return got.reshape(count * length, width // count)


def nearer(packs):
    return [pack[:-1] for pack in packs]


def farthest(packs):
    return [pack[-1:] for pack in packs]


def body(x_in, dy_out, routes, gates, w_down, w_qk, w_up, e_gate, e_up, e_down):
    links = Links()
    micro, _, length, width = x_in.shape
    rows = micro * length
    capacity = max(2, (3 * length + 2 * links.experts - 1) // (2 * links.experts))
    attn_w = (w_down[0], w_qk[0], w_up[0])
    first = links.section == 0

    route = routes[0, :, 0, :, 0]
    earlier = lax.broadcasted_iota(jnp.int32, (length, length), 0) > lax.broadcasted_iota(
        jnp.int32, (length, length), 1
    )
    same = route[:, :, None] == route[:, None, :]
    rank = jnp.sum((same & earlier).astype(jnp.int32), axis=2)
    slot = jnp.arange(micro, dtype=jnp.int32)[:, None] * capacity + rank
    position = (links.relative(route) * (micro * capacity) + slot).reshape(rows)
    pos_row, pos_col = position.reshape(1, rows), position.reshape(rows, 1)
    gate_col = gates[0, :, 0].reshape(rows, 1)
    slots = links.experts * micro * capacity
    blocks = (slots, micro * capacity if links.pairwise else slots)

    own = (e_gate[0, 0], e_up[0, 0], e_down[0, 0])
    packed = pack_weights(links, own, 1)
    dy = dy_out.reshape(rows, width)
    sent_1 = scatter(links, dy, gate_col, pos_row, blocks, 1)
    kept_0 = attend_forward(
        links, x_in.reshape(rows, width), micro, attn_w, pos_row, blocks, 0, as_list(sent_1)[:1]
    )
    dm_1 = links.exchange(sent_1, 1)
    rows_0 = links.exchange(kept_0.sent, 0)
    set_0 = links.gather_quarters(packed, 0, as_list(rows_0))
    onward = jnp.concatenate([pos_row.astype(F32), gate_col.reshape(1, rows)], axis=0)
    onward = links.move(onward, (0,), section_bit=1)
    packed_1 = pack_weights(links, own, 2, [onward, *as_list(dm_1)], 1)
    onward = (onward[:1].astype(jnp.int32), onward[1].reshape(rows, 1), blocks)

    near_0 = experts_call(links, nearer(set_0), 0, rows=rows_0, forward=True, last=False, later=packed_1[:1])
    there = tied(
        [kept_0.latent[:16, :128]], [*set_0[0][1:], *set_0[1][1:], near_0.total]
    )
    there = links.move(there[0], (0,), section_bit=1)
    packed_1 = tied(packed_1, [there])
    made_0 = experts_call(links, farthest(set_0), 0, rows=rows_0, forward=True, before=near_0.total, later=[there])
    pre_0 = [
        as_list(near_0.gate_out) + as_list(made_0.gate_out),
        as_list(near_0.up_out) + as_list(made_0.up_out),
    ]
    returned_0 = links.exchange(made_0.value, 0)
    out_0 = combine(links, kept_0.residual, returned_0, gate_col, pos_col, 0)
    h_1 = links.move(out_0, (0,), section_bit=1)
    kept_1 = attend_forward(links, h_1, micro, attn_w, pos_row, blocks, 1)
    sent = as_list(kept_1.sent)
    set_1 = links.gather_quarters(packed_1, 1, sent[:1], as_list(returned_0))
    if links.pairwise:
        sent = [sent[0], *tied(sent[1:], [set_1[0][1]])]
        rows_1 = links.exchange(sent, 1)
        early = factors(links, kept_0.inputs, [kept_0.mixed, kept_0.latent], 0, True)
        early = factors(
            links, h_1, [kept_1.mixed, kept_1.latent], 1, True, dict(packs=early), rows_1
        )
    else:
        rows_1 = links.exchange(kept_1.sent, 1)
    set_1 = [[mine] + got[1:] for mine, got in zip(packed, set_1)]
    near_1 = experts_call(links, nearer(set_1), 1, rows=rows_1, d_rows=dm_1, last=False)
    made_1 = experts_call(links, farthest(set_1), 1, rows=rows_1, d_rows=dm_1, before=near_1.total)
    hidden_1 = as_list(near_1.hidden_out) + as_list(made_1.hidden_out)
    back_1 = links.exchange(made_1.value, 1)
    value_1 = experts_call(
        links, set_1, 1, hidden=hidden_1, forward=True, block_rows=blocks[1]
    ).value
    first_value = as_list(value_1)[:1]
    if links.pairwise:
        late_1 = attend_backward(
            links, kept_1, micro, dy, back_1, attn_w, pos_col, 1, first_value, onward=onward
        )
        dm_0 = links.exchange_over(late_1.sent, 1)
        returned_1 = links.exchange(tied(value_1, dm_0), 1)
        u_0 = links.move(late_1.d_input, (1,), section_bit=1)
    else:
        late_1 = attend_backward(links, kept_1, micro, dy, back_1, attn_w, pos_col, 1, first_value)
        u_0 = links.move(late_1.d_input, (1,), section_bit=1)
        dm_0 = links.exchange(scatter(links, u_0, gate_col, pos_row, blocks, 0), 0)
        returned_1 = links.exchange(value_1, 1)
    back_0 = experts_call(links, set_0, 0, pre=pre_0, d_rows=dm_0, later=as_list(returned_1)).value
    merge = dict(d_input=late_1.d_input)
    if links.pairwise:
        narrow = [late_1.d_latent, late_1.d_queries]
        merge.update(packs=factors(links, late_1.d_res, narrow, 1, False, later=dm_0))
    late_0 = attend_backward(
        links, kept_0, micro, u_0, links.exchange(back_0, 0), attn_w, pos_col, 0, merge=merge
    )
    grads_in = late_0.d_input.reshape(1, micro, 1, length, width)
    activations = combine(
        links, kept_1.residual, returned_1, gate_col, pos_col, 1, dict(out=out_0)
    ).reshape(1, micro, 1, length, width)

    if links.pairwise:
        def plane(packs):
            return packs[:1] + [
                links.move(packs[k], links.every, quarter_bits=k) for k in range(1, links.quarters)
            ]

        g_down, g_qk, g_up_t = weight_gradients(links, plane(early), plane(late_0.packs), width)
    else:
        def pick(upper, lower):
            return jnp.where(first, upper, lower)

        def gathered(upper, lower):
            return lax.all_gather(pick(upper, lower), ("expert", "dp"), axis=0, tiled=True)

        g_down = t_times(
            spread(links, pick(kept_0.normed, kept_1.normed)),
            gathered(late_0.d_latent, late_1.d_latent),
        )
        g_qk = t_times(
            spread(links, pick(kept_0.latent, kept_1.latent)),
            gathered(late_0.d_queries, late_1.d_queries),
        )
        g_up_t = t_times(
            spread(links, pick(late_0.d_res, late_1.d_res)),
            gathered(kept_0.mixed, kept_1.mixed),
        )
    return (activations, grads_in, g_down[None], g_qk[None], g_up_t[None])


def solution(mesh):
    by_sequence = P(None, ("expert", "dp"), None, None)
    by_layer = P("section", None, ("expert", "dp"), None, None)
    shared = P("section", None, None)
    placed = (
        by_sequence,
        by_sequence,
        by_layer,
        by_layer,
        shared,
        shared,
        shared,
        P("section", "expert", None, "dp"),
        P("section", "expert", None, "dp"),
        P("section", "expert", "dp", None),
    )
    by_rows = P("section", ("expert", "dp"), None)
    return jax.shard_map(
        body,
        mesh=mesh,
        in_specs=placed,
        out_specs=(by_layer, by_layer, by_rows, by_rows, by_rows),
        check_vma=False,
    )
```

```python
from types import SimpleNamespace

import jax
import jax.numpy as jnp
from jax import lax
from jax.experimental import pallas as pl
from jax.experimental.pallas import tpu as pltpu
from jax.sharding import PartitionSpec as P

epsilon = 1e-06
AXES = ("section", "expert", "dp")
GRANT = (64 << 20) - (256 << 10)
ATTENTION = ("w_down", "w_qk", "w_up")
BF16, F32 = jnp.bfloat16, jnp.float32


def dot_f32(left, right):
    return jnp.dot(left, right, preferred_element_type=F32)


def times_t(left, right):
    return lax.dot_general(left, right, (((1,), (1,)), ((), ())), preferred_element_type=F32)


def t_times(left, right):
    return lax.dot_general(left, right, (((0,), (0,)), ((), ())), preferred_element_type=F32)


def inverse_rms(values):
    return lax.rsqrt(jnp.mean(values * values, axis=-1, keepdims=True) + epsilon)


def rms_back(normed, inv_rms, upstream):
    return inv_rms * (upstream - normed * jnp.mean(upstream * normed, axis=-1, keepdims=True))


def silu_parts(gate_pre):
    sigmoid = jax.nn.sigmoid(gate_pre)
    return (gate_pre * sigmoid, sigmoid * (1.0 + gate_pre * (1.0 - sigmoid)))


class Held:
    def __init__(self, refs, held, sems):
        self.held, self.parts, self.seen = held, [], set()
        start = 0
        for i, ref in enumerate(refs):
            target = held
            if len(refs) > 1:
                target = held.at[pl.ds(start, ref.shape[0])]
                start += ref.shape[0]
            self.parts.append((pltpu.make_async_copy(ref, target, sems.at[i]), target))

    def start(self, i):
        if i < len(self.parts):
            self.parts[i][0].start()

    def block(self, i):
        if i not in self.seen:
            self.seen.add(i)
            self.parts[i][0].wait()
        return self.parts[i][1]

    def all(self):
        for i in range(len(self.parts)):
            self.block(i)
        return self.held


class Made:
    def __init__(self, refs, held, sems):
        self.held, self.parts, self.sent = held, [], set()
        start = 0
        for i, ref in enumerate(refs):
            source = held
            if len(refs) > 1:
                source = held.at[pl.ds(start, ref.shape[0])]
                start += ref.shape[0]
            self.parts.append((pltpu.make_async_copy(source, ref, sems.at[i]), source))

    def send(self, i=0):
        if i not in self.sent:
            self.sent.add(i)
            self.parts[i][0].start()

    def finish(self):
        for i, (copy, _) in enumerate(self.parts):
            self.send(i)
        for copy, _ in self.parts:
            copy.wait()


def as_list(value):
    return list(value) if isinstance(value, (list, tuple)) else [value]


def stage_shape(arrays):
    if len(arrays) == 1:
        return pltpu.VMEM(arrays[0].shape, arrays[0].dtype)
    rows = sum(a.shape[0] for a in arrays)
    return pltpu.VMEM((rows, *arrays[0].shape[1:]), arrays[0].dtype)


def run(name, kernel, ins, outs, scratch=None, vmem=None, later=(), merge=None, only=None, place=None, raw=None, first=99, flops=0):
    scratch, vmem, merge, raw = scratch or {}, vmem or {}, merge or {}, raw or {}
    ins = {k: as_list(v) for k, v in ins.items()}
    outs = {k: as_list(v) for k, v in outs.items()}
    merge = {k: as_list(v) for k, v in merge.items()}
    flat_in = [a for v in ins.values() for a in v]
    flat_out = [a for v in outs.values() for a in v]
    flat_merge = [a for v in merge.values() for a in v]
    stages = [stage_shape(v) for v in [*ins.values(), *outs.values()]]
    sems = [pltpu.SemaphoreType.DMA((len(v),)) for v in [*ins.values(), *outs.values()]]
    smem = [] if place is None else [place]

    def body(*refs):
        refs = list(refs)

        def take(count):
            got = refs[:count]
            del refs[:count]
            return got

        place_refs, vmem_refs = take(len(smem)), take(len(vmem))
        in_refs = [take(len(v)) for v in ins.values()]
        instead = {k: take(len(v)) for k, v in merge.items()}
        raw_refs = {k: take(len(v)) for k, v in raw.items()}
        take(len(later))
        out_refs = [take(len(v)) for v in outs.values()]
        staged, signals = take(len(stages)), take(len(sems))
        r = SimpleNamespace(**dict(zip(vmem, vmem_refs)))
        if smem:
            r.place = place_refs[0]
        held = [Held(a, b, c) for a, b, c in zip(in_refs, staged, signals)]
        made = [Made(a, b, c) for a, b, c in zip(out_refs, staged[len(ins) :], signals[len(ins) :])]
        r.__dict__.update(zip(ins, held))
        r.__dict__.update(zip(outs, made))
        r.__dict__.update(zip(scratch, refs))

        r.__dict__.update(raw_refs)

        def open_all(part):
            for i in range(max([len(h.parts) for h in part], default=0)):
                for h in part:
                    h.start(i)

        r.open_rest = lambda: open_all(held[first:])

        def work():
            open_all(held[:first])
            if first >= len(held):
                r.open_rest()
            kernel(r)
            for h in held:
                h.all()
            for m in made:
                m.finish()

        def passed_on():
            for k, m, sem in zip(outs, made, signals[len(ins) :]):
                parts = list(zip(instead.get(k, ()), m.parts))
                loads = [
                    pltpu.make_async_copy(ref, part[1], sem.at[i]) for i, (ref, part) in enumerate(parts)
                ]
                for load in loads:
                    load.start()
                for load, (_, part) in zip(loads, parts):
                    load.wait()
                    part[0].start()
                for _, part in parts:
                    part[0].wait()

        if only is None:
            work()
        else:
            pl.when(r.place[2] == only)(work)
            if merge:
                pl.when(r.place[2] != only)(passed_on)

    flat_raw = [a for v in raw.values() for a in v]
    everything = [*smem, *vmem.values(), *flat_in, *flat_merge, *flat_raw, *later]
    spaces = [pltpu.SMEM] * len(smem) + [pltpu.VMEM] * len(vmem)
    spaces += [pltpu.HBM] * (len(everything) - len(spaces))
    got = pl.pallas_call(
        body,
        name=name,
        in_specs=[pl.BlockSpec(memory_space=s) for s in spaces],
        out_specs=[pl.BlockSpec(memory_space=pltpu.HBM) for _ in flat_out],
        out_shape=flat_out,
        scratch_shapes=[*stages, *sems, *scratch.values()],
        compiler_params=pltpu.CompilerParams(vmem_limit_bytes=GRANT),
        cost_estimate=pl.CostEstimate(
            flops=flops,
            bytes_accessed=sum(a.size * a.dtype.itemsize for a in flat_in),
            transcendentals=0,
        ),
    )(*everything)
    got, result = list(got), SimpleNamespace()
    for k, v in outs.items():
        part, got = got[: len(v)], got[len(v) :]
        setattr(result, k, part if len(part) > 1 else part[0])
    return result


def like(*shape, dtype=BF16):
    return jax.ShapeDtypeStruct(shape, dtype)


class Links:
    def __init__(self):
        self.sections, self.experts, self.quarters = [lax.axis_size(a) for a in AXES]
        self.section, self.expert, self.quarter = [lax.axis_index(a) for a in AXES]
        self.pairwise = self.experts <= 8
        self.every = tuple(range(self.sections))
        self.place = jnp.stack([self.expert, self.quarter, self.section])

    def move(self, x, sections, section_bit=0, expert_bits=0, quarter_bits=0):
        def number(s, e, d):
            return (s * self.experts + e) * self.quarters + d

        pairs = [
            (number(s, e, d), number(s ^ section_bit, e ^ expert_bits, d ^ quarter_bits))
            for s in sections
            for e in range(self.experts)
            for d in range(self.quarters)
        ]
        return lax.ppermute(x, AXES, pairs)

    def relative(self, expert):
        return expert ^ self.expert if self.pairwise else expert

    def exchange_over(self, blocks, section):
        got = {
            k: self.move(blocks[k], (section,), section_bit=1, expert_bits=k)
            for k in range(self.experts - 1, -1, -1)
        }
        return [got[k] for k in range(self.experts)]

    def exchange(self, blocks, section):
        if not self.pairwise:
            sent = blocks.reshape(self.experts, -1, blocks.shape[1])
            out = lax.all_to_all(sent, "expert", split_axis=0, concat_axis=0, tiled=True)
            return out.reshape(blocks.shape)
        got = {k: self.move(blocks[k], (section,), expert_bits=k) for k in range(self.experts - 1, 0, -1)}
        return [blocks[0]] + [got[k] for k in range(1, self.experts)]

    def gather_quarters(self, packs, section, before=(), between=(), hurry=False):
        if self.quarters != 4:
            return [
                [p] + [self.move(p, (section,), quarter_bits=k) for k in range(1, self.quarters)]
                for p in packs[:2]
            ]

        def across(one, two):
            return [
                self.move(one, (section,), quarter_bits=1),
                self.move(two, (section,), quarter_bits=2),
            ]

        step = across(packs[0], packs[1])
        again = tied(packs[2:], between) if between else packs[-2:]
        other = across(again[1], again[0])
        if not hurry:
            step = tied(step, [*other, *before])
        third = across(step[1], step[0])
        return [[packs[0], step[0], other[1], third[1]], [packs[1], other[0], step[1], third[0]]]


def tied(arrays, first):
    count = len(arrays)
    hbm = pl.BlockSpec(memory_space=pltpu.HBM)
    return list(
        pl.pallas_call(
            lambda *refs: None,
            name="tied",
            in_specs=[hbm] * (count + len(first)),
            out_specs=[hbm] * count,
            out_shape=[like(*a.shape, dtype=a.dtype) for a in arrays],
            input_output_aliases={i: i for i in range(count)},
            compiler_params=pltpu.CompilerParams(vmem_limit_bytes=GRANT),
        )(*arrays, *first)
    )


def attend_forward(links, inputs, micro, attn_w, pos_row, blocks, only, later=()):
    rows, width = inputs.shape
    length = rows // micro
    latent_width = attn_w[0].shape[1]
    slots, block_rows = blocks

    def kernel(r):
        h = r.h.all()[...].astype(F32)
        r.open_rest()
        normed_b = (h * inverse_rms(h)).astype(BF16)
        latent = dot_f32(normed_b, r.w_down.all()[...]).astype(BF16)
        queries = dot_f32(latent, r.w_qk.all()[...]).astype(BF16)
        r.latent.held[...] = latent
        r.queries.held[...] = queries
        causal = lax.broadcasted_iota(jnp.int32, (length, length), 0) >= lax.broadcasted_iota(
            jnp.int32, (length, length), 1
        )
        mixed = []
        for m in range(micro):
            part = slice(m * length, (m + 1) * length)
            scores = times_t(queries[part], latent[part]) * latent_width ** (-0.5)
            scores = jnp.where(causal, scores, -1e30)
            exponent = jnp.exp(scores - jnp.max(scores, axis=-1, keepdims=True))
            probs = exponent / jnp.sum(exponent, axis=-1, keepdims=True)
            r.probs.held[m] = probs
            mixed.append(dot_f32(probs.astype(BF16), latent[part]).astype(BF16))
        mixed = jnp.concatenate(mixed, axis=0)
        residual = (h + dot_f32(mixed, r.w_up.all()[...])).astype(BF16)
        r.residual.held[...] = residual
        r.residual.send()
        wide = residual.astype(F32)
        second_b = (wide * inverse_rms(wide)).astype(BF16)
        place_rows(r, r.pos_row.all()[...], second_b, slots, block_rows)
        r.mixed.held[...] = mixed
        if not links.pairwise:
            r.normed.held[...] = normed_b

    outs = dict(
        sent=[like(block_rows, width)] * (slots // block_rows),
        residual=like(rows, width),
        latent=like(rows, latent_width),
        queries=like(rows, latent_width),
        mixed=like(rows, latent_width),
        probs=like(micro, length, length, dtype=F32),
    )
    if not links.pairwise:
        outs.update(normed=like(rows, width))
    got = run(
        "attend_forward",
        kernel,
        dict(h=inputs, **dict(zip(ATTENTION, attn_w)), pos_row=pos_row),
        outs,
        first=2,
        later=later,
        only=only,
        place=links.place,
    )
    got.inputs = inputs
    return got


def factors(links, wide, narrow, only, normalize, merge=None, later=()):
    rows = wide.shape[0]
    latent_width = narrow[0].shape[1]

    def kernel(r):
        values = r.wide.all()[...]
        if normalize:
            h = values.astype(F32)
            values = (h * inverse_rms(h)).astype(BF16)
        pack_factors(links, r, values, [r.narrow.block(0)[...], r.narrow.block(1)[...]])

    return as_list(
        run(
            "factors",
            kernel,
            dict(wide=wide, narrow=narrow),
            dict(packs=pack_shapes(links, rows, latent_width)),
            pack_scratch(links, rows, latent_width),
            later=later,
            merge=merge,
            only=only,
            place=links.place,
        ).packs
    )


def place_rows(r, pos_row, values, slots, block_rows):
    shape = (slots, pos_row.shape[1])
    place = (pos_row == lax.broadcasted_iota(jnp.int32, shape, 0)).astype(BF16)
    for k in range(slots // block_rows):
        part = slice(k * block_rows, (k + 1) * block_rows)
        r.sent.held[part] = dot_f32(place[part], values).astype(BF16)
        r.sent.send(k)


def pack_shapes(links, rows, latent_width):
    return [like((links.experts + 2) * rows, latent_width)] * links.quarters


def pack_scratch(links, rows, latent_width):
    if not links.pairwise:
        return {}
    return dict(cols=pltpu.VMEM((links.experts * links.quarters, rows, latent_width), BF16))


def pack_factors(links, r, wide, narrow):
    rows, width = wide.shape
    experts, quarters = links.experts, links.quarters
    share = width // (experts * quarters)
    for i in range(experts * quarters):
        r.cols[i, :, :share] = wide[:, i * share : (i + 1) * share]
    expert, quarter = r.place[0], r.place[1]
    for k in range(quarters):
        out = r.packs.parts[k][1]
        for e in range(experts):
            out[e * rows : (e + 1) * rows] = r.cols[(expert ^ e) * quarters + (quarter ^ k)]
        for n, values in enumerate(narrow):
            out[(experts + n) * rows : (experts + n + 1) * rows] = values
        r.packs.send(k)


def picked_rows(r, rows):
    values = r.back.all()
    place = (
        r.pos_col.all()[...] == lax.broadcasted_iota(jnp.int32, (rows, values.shape[0]), 1)
    ).astype(BF16)
    return dot_f32(place, values[...])


def attend_backward(links, kept, micro, upstream, back, attn_w, pos_col, only, later=(), merge=None, onward=None):
    inputs = kept.inputs
    rows, width = inputs.shape
    length = rows // micro
    latent_width = attn_w[0].shape[1]
    packed = links.pairwise and not onward

    def kernel(r):
        r.back.all()
        r.open_rest()
        d_second = picked_rows(r, rows)
        u = r.u.all()[...].astype(F32)
        wide = r.residual.all()[...].astype(F32)
        inv = inverse_rms(wide)
        d_res = u + rms_back(wide * inv, inv, d_second)
        d_res_b = d_res.astype(BF16)
        d_mixed = times_t(d_res_b, r.w_up.all()[...]).astype(BF16)
        latent, queries, all_probs = r.latent.all()[...], r.queries.all()[...], r.probs.all()
        d_latent, d_queries = [], []
        for m in range(micro):
            part = slice(m * length, (m + 1) * length)
            probs = all_probs[m]
            d_probs = times_t(d_mixed[part], latent[part])
            d_scores = (
                probs
                * (d_probs - jnp.sum(d_probs * probs, axis=-1, keepdims=True))
                * latent_width ** (-0.5)
            ).astype(BF16)
            d_queries.append(dot_f32(d_scores, latent[part]).astype(BF16))
            d_latent.append(
                t_times(probs.astype(BF16), d_mixed[part]) + t_times(d_scores, queries[part])
            )
        d_queries = jnp.concatenate(d_queries, axis=0)
        d_latent = jnp.concatenate(d_latent, axis=0) + times_t(d_queries, r.w_qk.all()[...])
        d_latent = d_latent.astype(BF16)
        if packed:
            pack_factors(links, r, d_res_b, [d_latent, d_queries])
        else:
            r.d_res.held[...] = d_res_b
            r.d_latent.held[...] = d_latent
            r.d_queries.held[...] = d_queries
        d_normed = times_t(d_latent, r.w_down.all()[...])
        h = r.h.all()[...].astype(F32)
        inv = inverse_rms(h)
        d_input = (d_res + rms_back(h * inv, inv, d_normed)).astype(BF16)
        if onward:
            scaled = (d_input.astype(F32) * r.gate.all()[...]).astype(BF16)
            place_rows(r, r.pos_row.all()[...], scaled, slots, block_rows)
        r.d_input.held[...] = d_input

    outs = dict(d_input=like(rows, width))
    ins = {}
    if onward:
        ins, (slots, block_rows) = dict(pos_row=onward[0], gate=onward[1]), onward[2]
        outs.update(sent=[like(block_rows, width)] * (slots // block_rows))
    if packed:
        outs.update(packs=pack_shapes(links, rows, latent_width))
    else:
        outs.update(
            d_res=like(rows, width),
            d_latent=like(rows, latent_width),
            d_queries=like(rows, latent_width),
        )
    return run(
        "attend_backward",
        kernel,
        dict(
            back=back,
            pos_col=pos_col,
            u=upstream,
            residual=kept.residual,
            w_up=attn_w[2],
            latent=kept.latent,
            queries=kept.queries,
            probs=kept.probs,
            w_qk=attn_w[1],
            w_down=attn_w[0],
            h=inputs,
            **ins,
        ),
        outs,
        pack_scratch(links, rows, latent_width) if packed else None,
        first=4,
        later=later,
        merge=merge,
        only=only,
        place=links.place,
    )


def scatter(links, upstream, gate_col, pos_row, blocks, only, later=()):
    width = upstream.shape[1]
    slots, block_rows = blocks

    def kernel(r):
        scaled = (r.u.all()[...].astype(F32) * r.gate.all()[...]).astype(BF16)
        place_rows(r, r.pos_row.all()[...], scaled, slots, block_rows)

    ins = dict(u=upstream, gate=gate_col, pos_row=pos_row)
    outs = dict(sent=[like(block_rows, width)] * (slots // block_rows))
    return run("scatter", kernel, ins, outs, later=later, only=only, place=links.place).sent


def combine(links, residual, back, gate_col, pos_col, only, merge=None):
    rows, width = residual.shape

    def kernel(r):
        mixture = picked_rows(r, rows) * r.gate.all()[...]
        r.out.held[...] = (r.residual.all()[...].astype(F32) + mixture).astype(BF16)

    ins = dict(back=back, pos_col=pos_col, gate=gate_col, residual=residual)
    outs = dict(out=like(rows, width))
    return run("combine", kernel, ins, outs, merge=merge, only=only, place=links.place).out


def pack_weights(links, weights, copies, later=(), only=None):
    gate_w, up_w, down_w = weights
    width, split = gate_w.shape
    count = width // split
    half = count // 2
    shape = (width + half * split, split)

    def body(place, gate, up, down, *refs):
        *outs, held0, held1, sems, out_sems = refs[len(later) :]

        def copy_all():
            moves = []
            for source, held, first in ((gate, held0, 0), (up, held1, half)):
                part = [(source, held.at[pl.ds(0, width)])]
                for j in range(half):
                    columns = pl.ds((first + j) * split, split)
                    part.append((down.at[:, columns], held.at[pl.ds(width + j * split, split)]))
                moves.append(part)
            loads = [
                [pltpu.make_async_copy(a, b, sems.at[i, j]) for j, (a, b) in enumerate(part)]
                for i, part in enumerate(moves)
            ]
            for load in loads[0] + loads[1]:
                load.start()
            stores = []
            for i, held in enumerate((held0, held1)):
                for load in loads[i]:
                    load.wait()
                for k in range(i, 2 * copies, 2):
                    stores.append(pltpu.make_async_copy(held, outs[k], out_sems.at[k]))
                    stores[-1].start()
            for store in stores:
                store.wait()

        if only is None:
            copy_all()
        else:
            pl.when(place[2] == only)(copy_all)

    hbm = pl.BlockSpec(memory_space=pltpu.HBM)
    return list(
        pl.pallas_call(
            body,
            name="pack_weights",
            in_specs=[pl.BlockSpec(memory_space=pltpu.SMEM)] + [hbm] * (3 + len(later)),
            out_specs=[hbm] * (2 * copies),
            out_shape=[like(*shape)] * (2 * copies),
            scratch_shapes=[
                pltpu.VMEM(shape, BF16),
                pltpu.VMEM(shape, BF16),
                pltpu.SemaphoreType.DMA((2, half + 1)),
                pltpu.SemaphoreType.DMA((2 * copies,)),
            ],
            compiler_params=pltpu.CompilerParams(vmem_limit_bytes=GRANT),
        )(links.place, gate_w, up_w, down_w, *later)
    )


def experts_call(links, packs, only, rows=None, pre=None, hidden=None, d_rows=None, forward=False, block_rows=None, before=None, last=True, later=()):
    quarters = len(packs[0])
    split = packs[0][0].shape[1]
    backward = d_rows is not None
    sources = as_list(rows if rows is not None else d_rows) if hidden is None else []
    if hidden is None:
        block_rows, count = sources[0].shape[0], len(sources)
        width = sources[0].shape[1]
        slots = block_rows * count
    else:
        slots = hidden[0].shape[0]
        count = slots // block_rows
        width = 2 * packs[0][0].shape[0] // 3
    blocks = width // split
    half = blocks // 2

    step = 2 * split if width % (2 * split) == 0 else split
    steps = [slice(c, c + step) for c in range(0, width, step)]

    def kernel(r):
        def copies(q):
            wide, narrow = [], []
            for n, pack in enumerate((r.pack0[q], r.pack1[q])):
                if hidden is None:
                    wide.append((pack.at[pl.ds(0, width)], (r.all0, r.all1)[n].at[q]))
                for j in range(half):
                    target = r.all2.at[q, :, pl.ds((n * half + j) * split, split)]
                    narrow.append((pack.at[pl.ds(width + j * split, split)], target))
            found = wide + narrow if rows is not None else narrow + wide
            found = [pltpu.make_async_copy(a, b, r.sems.at[q, i]) for i, (a, b) in enumerate(found)]
            return (found[:2], found[2:]) if rows is not None else (found[: 2 * half], found[2 * half :])

        loads = [copies(q) for q in range(quarters)]
        def start(q):
            for copy in (*loads[q][0], *loads[q][1]):
                copy.start()

        def wait(part):
            for copy in part:
                copy.wait()

        start(0)
        r.open_rest()
        running = r.running if last else r.total.held

        def add(q, columns, part):
            part = part.astype(BF16).astype(F32)
            if q:
                part = part + running[:, columns]
            elif before is not None:
                part = part + r.before.all()[:, columns]
            if q == quarters - 1 and last:
                r.value.held[:, columns] = part.astype(BF16)
            else:
                running[:, columns] = part

        for q in range(quarters):
            wait(loads[q][0])
            if q + 1 < quarters:
                start(q + 1)
            if rows is not None:
                held = r.rows.all()[...]
                gate_pre, up_pre = dot_f32(held, r.all0[q]), dot_f32(held, r.all1[q])
                if not backward:
                    r.gate_out.parts[q][1][...] = gate_pre
                    r.gate_out.send(q)
                    r.up_out.parts[q][1][...] = up_pre
                    r.up_out.send(q)
            elif pre is not None:
                gate_pre, up_pre = r.gate_pre.block(q)[...], r.up_pre.block(q)[...]
            if hidden is not None:
                hidden_q = r.hidden.block(q)[...]
            else:
                activated, slope = silu_parts(gate_pre)
            if rows is not None:
                hidden_q = (activated * up_pre).astype(BF16)
                if backward:
                    r.hidden_out.parts[q][1][...] = hidden_q
                    r.hidden_out.send(q)
            if rows is not None:
                wait(loads[q][1])
            if forward:
                for c in steps:
                    add(q, c, dot_f32(hidden_q, r.all2[q, :, c]))
            if backward:
                d_hidden = times_t(r.d_rows.all()[...], r.all2[q])
                if rows is None:
                    wait(loads[q][1])
                d_gate = (d_hidden * up_pre * slope).astype(BF16)
                d_up = (d_hidden * activated).astype(BF16)
                for c in steps:
                    add(q, c, times_t(d_gate, r.all0[q, c]) + times_t(d_up, r.all1[q, c]))

    ins = {}
    if rows is not None:
        ins.update(rows=rows)
    if backward:
        ins.update(d_rows=d_rows)
    if pre is not None:
        ins.update(gate_pre=pre[0], up_pre=pre[1])
    if hidden is not None:
        ins.update(hidden=hidden)
    if before is not None:
        ins.update(before=before)
    if last:
        outs = dict(value=[like(block_rows, width)] * count)
    else:
        outs = dict(total=like(slots, width, dtype=F32))
    if rows is not None and backward:
        outs.update(hidden_out=[like(slots, split)] * quarters)
    elif rows is not None:
        made = [like(slots, split, dtype=F32)] * quarters
        outs.update(gate_out=made, up_out=made)
    flops = 2 * slots * width * split * quarters * 3
    scratch = dict(
        all2=pltpu.VMEM((quarters, split, width), BF16),
        sems=pltpu.SemaphoreType.DMA((quarters, blocks + 2)),
    )
    if hidden is None:
        weights = pltpu.VMEM((quarters, width, split), BF16)
        scratch.update(all0=weights, all1=weights)
    if last:
        scratch.update(running=pltpu.VMEM((slots, width), F32))
    return run(
        "experts",
        kernel,
        ins,
        outs,
        scratch,
        raw=dict(pack0=packs[0], pack1=packs[1]),
        first=2,
        later=later,
        flops=flops,
        only=only,
        place=links.place,
    )


def weight_gradients(links, early, late, width):
    experts, quarters = links.experts, links.quarters
    rows = early[0].shape[0] // (experts + 2)
    latent_width = early[0].shape[1]
    share, share_qk = width // (experts * quarters), latent_width // (experts * quarters)
    total = 2 * share + share_qk

    def plane_sums(r):
        def part(held, k, i, columns=latent_width):
            return held.block(k)[i * rows : (i + 1) * rows, :columns]

        sum_qk = jnp.zeros((latent_width, latent_width), F32)
        for k in range(quarters):
            sum_qk += t_times(part(r.early, k, experts + 1), part(r.late, k, experts + 1))
        r.qk[...] = sum_qk
        for e in range(experts):
            down = jnp.zeros((share, latent_width), F32)
            up = jnp.zeros((share, latent_width), F32)
            for k in range(quarters):
                down += t_times(part(r.early, k, e, share), part(r.late, k, experts))
                up += t_times(part(r.late, k, e, share), part(r.early, k, experts))
            at = pl.multiple_of(((r.place[0] ^ e) * quarters + r.place[1]) * share_qk, share_qk)
            made = r.away if e else r.own
            out = made.parts[max(e - 1, 0)][1]
            out[:share] = down.astype(out.dtype)
            out[share : 2 * share] = up.astype(out.dtype)
            out[2 * share :] = r.qk[pl.ds(at, share_qk)].astype(out.dtype)
            made.send(max(e - 1, 0))

    sums = run(
        "plane_sums",
        plane_sums,
        dict(early=early, late=late),
        dict(
            own=like(total, latent_width, dtype=F32),
            away=[like(total, latent_width)] * (experts - 1),
        ),
        dict(qk=pltpu.VMEM((latent_width, latent_width), F32)),
        place=links.place,
    )
    away = as_list(sums.away)
    got = [links.move(away[e - 1], links.every, expert_bits=e) for e in range(experts - 1, 0, -1)]

    value = sums.own + sum(g.astype(F32) for g in got)
    return value[:share], value[2 * share :], value[share : 2 * share]


def spread(links, rows):
    length, width = rows.shape
    count = links.experts * links.quarters
    by_owner = rows.reshape(length, count, width // count).transpose(1, 0, 2)
    got = lax.all_to_all(by_owner, ("expert", "dp"), split_axis=0, concat_axis=0, tiled=True)
    return got.reshape(count * length, width // count)


def nearer(packs):
    return [pack[:-1] for pack in packs]


def farthest(packs):
    return [pack[-1:] for pack in packs]


def body(x_in, dy_out, routes, gates, w_down, w_qk, w_up, e_gate, e_up, e_down):
    links = Links()
    micro, _, length, width = x_in.shape
    rows = micro * length
    capacity = max(2, (3 * length + 2 * links.experts - 1) // (2 * links.experts))
    attn_w = (w_down[0], w_qk[0], w_up[0])
    first = links.section == 0

    route = routes[0, :, 0, :, 0]
    earlier = lax.broadcasted_iota(jnp.int32, (length, length), 0) > lax.broadcasted_iota(
        jnp.int32, (length, length), 1
    )
    same = route[:, :, None] == route[:, None, :]
    rank = jnp.sum((same & earlier).astype(jnp.int32), axis=2)
    slot = jnp.arange(micro, dtype=jnp.int32)[:, None] * capacity + rank
    position = (links.relative(route) * (micro * capacity) + slot).reshape(rows)
    pos_row, pos_col = position.reshape(1, rows), position.reshape(rows, 1)
    gate_col = gates[0, :, 0].reshape(rows, 1)
    slots = links.experts * micro * capacity
    blocks = (slots, micro * capacity if links.pairwise else slots)

    own = (e_gate[0, 0], e_up[0, 0], e_down[0, 0])
    packed = pack_weights(links, own, 1)
    dy = dy_out.reshape(rows, width)
    sent_1 = scatter(links, dy, gate_col, pos_row, blocks, 1)
    kept_0 = attend_forward(
        links, x_in.reshape(rows, width), micro, attn_w, pos_row, blocks, 0, as_list(sent_1)[:1]
    )
    rows_0 = links.exchange(kept_0.sent, 0)
    dm_1 = links.exchange(tied(as_list(sent_1), rows_0[1:]) if links.pairwise else sent_1, 1)
    again = pack_weights(links, own, 1, as_list(kept_0.sent)[:1], 0)
    set_0 = links.gather_quarters(packed + again, 0, hurry=True)
    onward = jnp.concatenate([pos_row.astype(F32), gate_col.reshape(1, rows)], axis=0)
    packed_1 = pack_weights(links, own, 2, as_list(dm_1), 1)
    onward = tied([onward], [*set_0[0][1:], *set_0[1][1:]])[0]
    there = links.move(onward, (0,), section_bit=1)
    packed_1 = tied(packed_1, [there])
    onward = (there[:1].astype(jnp.int32), there[1].reshape(rows, 1), blocks)

    near_0 = experts_call(links, nearer(set_0), 0, rows=rows_0, forward=True, last=False, later=packed_1[:1])
    made_0 = experts_call(links, farthest(set_0), 0, rows=rows_0, forward=True, before=near_0.total, later=[there])
    pre_0 = [
        as_list(near_0.gate_out) + as_list(made_0.gate_out),
        as_list(near_0.up_out) + as_list(made_0.up_out),
    ]
    returned_0 = links.exchange(made_0.value, 0)
    out_0 = combine(links, kept_0.residual, returned_0, gate_col, pos_col, 0)
    h_1 = links.move(out_0, (0,), section_bit=1)
    kept_1 = attend_forward(links, h_1, micro, attn_w, pos_row, blocks, 1)
    sent = as_list(kept_1.sent)
    set_1 = links.gather_quarters(packed_1, 1, sent[:1], as_list(returned_0))
    if links.pairwise:
        sent = [sent[0], *tied(sent[1:], [set_1[0][1]])]
        rows_1 = links.exchange(sent, 1)
        early = factors(links, kept_0.inputs, [kept_0.mixed, kept_0.latent], 0, True)
        early = factors(
            links, h_1, [kept_1.mixed, kept_1.latent], 1, True, dict(packs=early), rows_1
        )
    else:
        rows_1 = links.exchange(kept_1.sent, 1)
    set_1 = [[mine] + got[1:] for mine, got in zip(packed, set_1)]
    near_1 = experts_call(links, nearer(set_1), 1, rows=rows_1, d_rows=dm_1, last=False)
    made_1 = experts_call(links, farthest(set_1), 1, rows=rows_1, d_rows=dm_1, before=near_1.total)
    hidden_1 = as_list(near_1.hidden_out) + as_list(made_1.hidden_out)
    back_1 = links.exchange(made_1.value, 1)
    if links.pairwise:
        late_1 = attend_backward(
            links, kept_1, micro, dy, back_1, attn_w, pos_col, 1, early[:1], onward=onward
        )
        dm_0 = links.exchange_over(late_1.sent, 1)
        u_0 = links.move(late_1.d_input, (1,), section_bit=1)
    else:
        late_1 = attend_backward(links, kept_1, micro, dy, back_1, attn_w, pos_col, 1)
        u_0 = links.move(late_1.d_input, (1,), section_bit=1)
        dm_0 = links.exchange(scatter(links, u_0, gate_col, pos_row, blocks, 0), 0)
    value_1 = experts_call(
        links,
        set_1,
        1,
        hidden=hidden_1,
        forward=True,
        block_rows=blocks[1],
        later=[late_1.d_latent],
    ).value
    if links.pairwise:
        value_1 = tied(value_1, dm_0[1:])
    returned_1 = links.exchange(value_1, 1)
    later = as_list(returned_1)
    back_0 = experts_call(links, set_0, 0, pre=pre_0, d_rows=dm_0, later=later).value
    merge = dict(d_input=late_1.d_input)
    if links.pairwise:
        narrow = [late_1.d_latent, late_1.d_queries]
        merge.update(packs=factors(links, late_1.d_res, narrow, 1, False, later=dm_0))
    late_0 = attend_backward(
        links, kept_0, micro, u_0, links.exchange(back_0, 0), attn_w, pos_col, 0, merge=merge
    )
    grads_in = late_0.d_input.reshape(1, micro, 1, length, width)
    activations = combine(
        links, kept_1.residual, returned_1, gate_col, pos_col, 1, dict(out=out_0)
    ).reshape(1, micro, 1, length, width)

    if links.pairwise:
        def plane(packs):
            return packs[:1] + [
                links.move(packs[k], links.every, quarter_bits=k) for k in range(1, links.quarters)
            ]

        g_down, g_qk, g_up_t = weight_gradients(links, plane(early), plane(late_0.packs), width)
    else:
        def pick(upper, lower):
            return jnp.where(first, upper, lower)

        def gathered(upper, lower):
            return lax.all_gather(pick(upper, lower), ("expert", "dp"), axis=0, tiled=True)

        g_down = t_times(
            spread(links, pick(kept_0.normed, kept_1.normed)),
            gathered(late_0.d_latent, late_1.d_latent),
        )
        g_qk = t_times(
            spread(links, pick(kept_0.latent, kept_1.latent)),
            gathered(late_0.d_queries, late_1.d_queries),
        )
        g_up_t = t_times(
            spread(links, pick(late_0.d_res, late_1.d_res)),
            gathered(kept_0.mixed, kept_1.mixed),
        )
    return (activations, grads_in, g_down[None], g_qk[None], g_up_t[None])


def solution(mesh):
    by_sequence = P(None, ("expert", "dp"), None, None)
    by_layer = P("section", None, ("expert", "dp"), None, None)
    shared = P("section", None, None)
    placed = (
        by_sequence,
        by_sequence,
        by_layer,
        by_layer,
        shared,
        shared,
        shared,
        P("section", "expert", None, "dp"),
        P("section", "expert", None, "dp"),
        P("section", "expert", "dp", None),
    )
    by_rows = P("section", ("expert", "dp"), None)
    return jax.shard_map(
        body,
        mesh=mesh,
        in_specs=placed,
        out_specs=(by_layer, by_layer, by_rows, by_rows, by_rows),
        check_vma=False,
    )
```

```python
from types import SimpleNamespace

import jax
import jax.numpy as jnp
from jax import lax
from jax.experimental import pallas as pl
from jax.experimental.pallas import tpu as pltpu
from jax.sharding import PartitionSpec as P

epsilon = 1e-06
AXES = ("section", "expert", "dp")
GRANT = (64 << 20) - (256 << 10)
ATTENTION = ("w_down", "w_qk", "w_up")
BF16, F32 = jnp.bfloat16, jnp.float32


def dot_f32(left, right):
    return jnp.dot(left, right, preferred_element_type=F32)


def times_t(left, right):
    return lax.dot_general(left, right, (((1,), (1,)), ((), ())), preferred_element_type=F32)


def t_times(left, right):
    return lax.dot_general(left, right, (((0,), (0,)), ((), ())), preferred_element_type=F32)


def inverse_rms(values):
    return lax.rsqrt(jnp.mean(values * values, axis=-1, keepdims=True) + epsilon)


def rms_back(normed, inv_rms, upstream):
    return inv_rms * (upstream - normed * jnp.mean(upstream * normed, axis=-1, keepdims=True))


def silu_parts(gate_pre):
    sigmoid = jax.nn.sigmoid(gate_pre)
    return (gate_pre * sigmoid, sigmoid * (1.0 + gate_pre * (1.0 - sigmoid)))


class Held:
    def __init__(self, refs, held, sems):
        self.held, self.parts, self.seen = held, [], set()
        start = 0
        for i, ref in enumerate(refs):
            target = held
            if len(refs) > 1:
                target = held.at[pl.ds(start, ref.shape[0])]
                start += ref.shape[0]
            self.parts.append((pltpu.make_async_copy(ref, target, sems.at[i]), target))

    def start(self, i):
        if i < len(self.parts):
            self.parts[i][0].start()

    def block(self, i):
        if i not in self.seen:
            self.seen.add(i)
            self.parts[i][0].wait()
        return self.parts[i][1]

    def all(self):
        for i in range(len(self.parts)):
            self.block(i)
        return self.held


class Made:
    def __init__(self, refs, held, sems):
        self.held, self.parts, self.sent = held, [], set()
        self.refs, self.pieces = refs, []
        start = 0
        for i, ref in enumerate(refs):
            source = held
            if len(refs) > 1:
                source = held.at[pl.ds(start, ref.shape[0])]
                start += ref.shape[0]
            self.parts.append((pltpu.make_async_copy(source, ref, sems.at[i]), source))

    def send(self, i=0):
        if i not in self.sent:
            self.sent.add(i)
            self.parts[i][0].start()

    def send_columns(self, columns, sems):
        for i, (_, source) in enumerate(self.parts):
            copy = pltpu.make_async_copy(source.at[:, columns], self.refs[i].at[:, columns], sems.at[i])
            copy.start()
            self.pieces.append(copy)

    def finish(self):
        for copy in self.pieces:
            copy.wait()
        if self.pieces:
            return
        for i in range(len(self.parts)):
            self.send(i)
        for copy, _ in self.parts:
            copy.wait()


def as_list(value):
    return list(value) if isinstance(value, (list, tuple)) else [value]


def stage_shape(arrays):
    if len(arrays) == 1:
        return pltpu.VMEM(arrays[0].shape, arrays[0].dtype)
    rows = sum(a.shape[0] for a in arrays)
    return pltpu.VMEM((rows, *arrays[0].shape[1:]), arrays[0].dtype)


def run(name, kernel, ins, outs, scratch=None, vmem=None, later=(), merge=None, only=None, place=None, raw=None, first=99, flops=0):
    scratch, vmem, merge, raw = scratch or {}, vmem or {}, merge or {}, raw or {}
    ins = {k: as_list(v) for k, v in ins.items()}
    outs = {k: as_list(v) for k, v in outs.items()}
    merge = {k: as_list(v) for k, v in merge.items()}
    flat_in = [a for v in ins.values() for a in v]
    flat_out = [a for v in outs.values() for a in v]
    flat_merge = [a for v in merge.values() for a in v]
    stages = [stage_shape(v) for v in [*ins.values(), *outs.values()]]
    sems = [pltpu.SemaphoreType.DMA((len(v),)) for v in [*ins.values(), *outs.values()]]
    smem = [] if place is None else [place]

    def body(*refs):
        refs = list(refs)

        def take(count):
            got = refs[:count]
            del refs[:count]
            return got

        place_refs, vmem_refs = take(len(smem)), take(len(vmem))
        in_refs = [take(len(v)) for v in ins.values()]
        instead = {k: take(len(v)) for k, v in merge.items()}
        raw_refs = {k: take(len(v)) for k, v in raw.items()}
        take(len(later))
        out_refs = [take(len(v)) for v in outs.values()]
        staged, signals = take(len(stages)), take(len(sems))
        r = SimpleNamespace(**dict(zip(vmem, vmem_refs)))
        if smem:
            r.place = place_refs[0]
        held = [Held(a, b, c) for a, b, c in zip(in_refs, staged, signals)]
        made = [Made(a, b, c) for a, b, c in zip(out_refs, staged[len(ins) :], signals[len(ins) :])]
        r.__dict__.update(zip(ins, held))
        r.__dict__.update(zip(outs, made))
        r.__dict__.update(zip(scratch, refs))

        r.__dict__.update(raw_refs)

        def open_all(part):
            for i in range(max([len(h.parts) for h in part], default=0)):
                for h in part:
                    h.start(i)

        r.open_rest = lambda: open_all(held[first:])

        def work():
            open_all(held[:first])
            if first >= len(held):
                r.open_rest()
            kernel(r)
            for h in held:
                h.all()
            for m in made:
                m.finish()

        def passed_on():
            for k, m, sem in zip(outs, made, signals[len(ins) :]):
                parts = list(zip(instead.get(k, ()), m.parts))
                loads = [
                    pltpu.make_async_copy(ref, part[1], sem.at[i]) for i, (ref, part) in enumerate(parts)
                ]
                for load in loads:
                    load.start()
                for load, (_, part) in zip(loads, parts):
                    load.wait()
                    part[0].start()
                for _, part in parts:
                    part[0].wait()

        if only is None:
            work()
        else:
            pl.when(r.place[2] == only)(work)
            if merge:
                pl.when(r.place[2] != only)(passed_on)

    flat_raw = [a for v in raw.values() for a in v]
    everything = [*smem, *vmem.values(), *flat_in, *flat_merge, *flat_raw, *later]
    spaces = [pltpu.SMEM] * len(smem) + [pltpu.VMEM] * len(vmem)
    spaces += [pltpu.HBM] * (len(everything) - len(spaces))
    got = pl.pallas_call(
        body,
        name=name,
        in_specs=[pl.BlockSpec(memory_space=s) for s in spaces],
        out_specs=[pl.BlockSpec(memory_space=pltpu.HBM) for _ in flat_out],
        out_shape=flat_out,
        scratch_shapes=[*stages, *sems, *scratch.values()],
        compiler_params=pltpu.CompilerParams(vmem_limit_bytes=GRANT),
        cost_estimate=pl.CostEstimate(
            flops=flops,
            bytes_accessed=sum(a.size * a.dtype.itemsize for a in flat_in) * 0,
            transcendentals=0,
        ),
    )(*everything)
    got, result = list(got), SimpleNamespace()
    for k, v in outs.items():
        part, got = got[: len(v)], got[len(v) :]
        setattr(result, k, part if len(part) > 1 else part[0])
    return result


def like(*shape, dtype=BF16):
    return jax.ShapeDtypeStruct(shape, dtype)


class Links:
    def __init__(self):
        self.sections, self.experts, self.quarters = [lax.axis_size(a) for a in AXES]
        self.section, self.expert, self.quarter = [lax.axis_index(a) for a in AXES]
        self.pairwise = self.experts <= 8
        self.every = tuple(range(self.sections))
        self.place = jnp.stack([self.expert, self.quarter, self.section])

    def move(self, x, sections, section_bit=0, expert_bits=0, quarter_bits=0):
        def number(s, e, d):
            return (s * self.experts + e) * self.quarters + d

        pairs = [
            (number(s, e, d), number(s ^ section_bit, e ^ expert_bits, d ^ quarter_bits))
            for s in sections
            for e in range(self.experts)
            for d in range(self.quarters)
        ]
        return lax.ppermute(x, AXES, pairs)

    def relative(self, expert):
        return expert ^ self.expert if self.pairwise else expert

    def exchange_over(self, blocks, section):
        got = {
            k: self.move(blocks[k], (section,), section_bit=1, expert_bits=k)
            for k in range(self.experts - 1, -1, -1)
        }
        return [got[k] for k in range(self.experts)]

    def exchange(self, blocks, section):
        if not self.pairwise:
            sent = blocks.reshape(self.experts, -1, blocks.shape[1])
            out = lax.all_to_all(sent, "expert", split_axis=0, concat_axis=0, tiled=True)
            return out.reshape(blocks.shape)
        got = {k: self.move(blocks[k], (section,), expert_bits=k) for k in range(self.experts - 1, 0, -1)}
        return [blocks[0]] + [got[k] for k in range(1, self.experts)]

    def gather_quarters(self, packs, section, before=(), between=(), hurry=False):
        if self.quarters != 4:
            return [
                [p] + [self.move(p, (section,), quarter_bits=k) for k in range(1, self.quarters)]
                for p in packs[:2]
            ]

        def across(one, two):
            return [
                self.move(one, (section,), quarter_bits=1),
                self.move(two, (section,), quarter_bits=2),
            ]

        step = across(packs[0], packs[1])
        again = tied(packs[2:], between) if between else packs[-2:]
        other = across(again[1], again[0])
        if not hurry:
            step = tied(step, [*other, *before])
        third = across(step[1], step[0])
        return [[packs[0], step[0], other[1], third[1]], [packs[1], other[0], step[1], third[0]]]


def tied(arrays, first):
    count = len(arrays)
    hbm = pl.BlockSpec(memory_space=pltpu.HBM)
    return list(
        pl.pallas_call(
            lambda *refs: None,
            name="tied",
            in_specs=[hbm] * (count + len(first)),
            out_specs=[hbm] * count,
            out_shape=[like(*a.shape, dtype=a.dtype) for a in arrays],
            input_output_aliases={i: i for i in range(count)},
            compiler_params=pltpu.CompilerParams(vmem_limit_bytes=GRANT),
        )(*arrays, *first)
    )


def attend_forward(links, inputs, micro, attn_w, pos_row, blocks, only, later=()):
    rows, width = inputs.shape
    length = rows // micro
    latent_width = attn_w[0].shape[1]
    slots, block_rows = blocks

    def kernel(r):
        h = r.h.all()[...].astype(F32)
        r.open_rest()
        normed_b = (h * inverse_rms(h)).astype(BF16)
        latent = dot_f32(normed_b, r.w_down.all()[...]).astype(BF16)
        queries = dot_f32(latent, r.w_qk.all()[...]).astype(BF16)
        r.latent.held[...] = latent
        r.queries.held[...] = queries
        causal = lax.broadcasted_iota(jnp.int32, (length, length), 0) >= lax.broadcasted_iota(
            jnp.int32, (length, length), 1
        )
        mixed = []
        for m in range(micro):
            part = slice(m * length, (m + 1) * length)
            scores = times_t(queries[part], latent[part]) * latent_width ** (-0.5)
            scores = jnp.where(causal, scores, -1e30)
            exponent = jnp.exp(scores - jnp.max(scores, axis=-1, keepdims=True))
            probs = exponent / jnp.sum(exponent, axis=-1, keepdims=True)
            r.probs.held[m] = probs
            mixed.append(dot_f32(probs.astype(BF16), latent[part]).astype(BF16))
        mixed = jnp.concatenate(mixed, axis=0)
        residual = (h + dot_f32(mixed, r.w_up.all()[...])).astype(BF16)
        r.residual.held[...] = residual
        r.residual.send()
        wide = residual.astype(F32)
        second_b = (wide * inverse_rms(wide)).astype(BF16)
        place_rows(r, r.pos_row.all()[...], second_b, slots, block_rows)
        r.mixed.held[...] = mixed
        if not links.pairwise:
            r.normed.held[...] = normed_b

    outs = dict(
        sent=[like(block_rows, width)] * (slots // block_rows),
        residual=like(rows, width),
        latent=like(rows, latent_width),
        queries=like(rows, latent_width),
        mixed=like(rows, latent_width),
        probs=like(micro, length, length, dtype=F32),
    )
    if not links.pairwise:
        outs.update(normed=like(rows, width))
    got = run(
        "attend_forward",
        kernel,
        dict(h=inputs, **dict(zip(ATTENTION, attn_w)), pos_row=pos_row),
        outs,
        first=2,
        later=later,
        only=only,
        place=links.place,
    )
    got.inputs = inputs
    return got


def factors(links, wide, narrow, only, normalize, merge=None, later=()):
    rows = wide.shape[0]
    latent_width = narrow[0].shape[1]

    def kernel(r):
        values = r.wide.all()[...]
        if normalize:
            h = values.astype(F32)
            values = (h * inverse_rms(h)).astype(BF16)
        pack_factors(links, r, values, [r.narrow.block(0)[...], r.narrow.block(1)[...]])

    return as_list(
        run(
            "factors",
            kernel,
            dict(wide=wide, narrow=narrow),
            dict(packs=pack_shapes(links, rows, latent_width)),
            pack_scratch(links, rows, latent_width),
            later=later,
            merge=merge,
            only=only,
            place=links.place,
        ).packs
    )


def place_rows(r, pos_row, values, slots, block_rows):
    shape = (slots, pos_row.shape[1])
    place = (pos_row == lax.broadcasted_iota(jnp.int32, shape, 0)).astype(BF16)
    for k in range(slots // block_rows):
        part = slice(k * block_rows, (k + 1) * block_rows)
        r.sent.held[part] = dot_f32(place[part], values).astype(BF16)
        r.sent.send(k)


def pack_shapes(links, rows, latent_width):
    return [like((links.experts + 2) * rows, latent_width)] * links.quarters


def pack_scratch(links, rows, latent_width):
    if not links.pairwise:
        return {}
    return dict(cols=pltpu.VMEM((links.experts * links.quarters, rows, latent_width), BF16))


def pack_factors(links, r, wide, narrow):
    rows, width = wide.shape
    experts, quarters = links.experts, links.quarters
    share = width // (experts * quarters)
    for i in range(experts * quarters):
        r.cols[i, :, :share] = wide[:, i * share : (i + 1) * share]
    expert, quarter = r.place[0], r.place[1]
    for k in range(quarters):
        out = r.packs.parts[k][1]
        for e in range(experts):
            out[e * rows : (e + 1) * rows] = r.cols[(expert ^ e) * quarters + (quarter ^ k)]
        for n, values in enumerate(narrow):
            out[(experts + n) * rows : (experts + n + 1) * rows] = values
        r.packs.send(k)


def picked_rows(r, rows):
    values = r.back.all()
    place = (
        r.pos_col.all()[...] == lax.broadcasted_iota(jnp.int32, (rows, values.shape[0]), 1)
    ).astype(BF16)
    return dot_f32(place, values[...])


def attend_backward(links, kept, micro, upstream, back, attn_w, pos_col, only, later=(), merge=None, onward=None):
    inputs = kept.inputs
    rows, width = inputs.shape
    length = rows // micro
    latent_width = attn_w[0].shape[1]
    packed = links.pairwise and not onward

    def kernel(r):
        r.back.all()
        r.open_rest()
        d_second = picked_rows(r, rows)
        u = r.u.all()[...].astype(F32)
        wide = r.residual.all()[...].astype(F32)
        inv = inverse_rms(wide)
        d_res = u + rms_back(wide * inv, inv, d_second)
        d_res_b = d_res.astype(BF16)
        d_mixed = times_t(d_res_b, r.w_up.all()[...]).astype(BF16)
        latent, queries, all_probs = r.latent.all()[...], r.queries.all()[...], r.probs.all()
        d_latent, d_queries = [], []
        for m in range(micro):
            part = slice(m * length, (m + 1) * length)
            probs = all_probs[m]
            d_probs = times_t(d_mixed[part], latent[part])
            d_scores = (
                probs
                * (d_probs - jnp.sum(d_probs * probs, axis=-1, keepdims=True))
                * latent_width ** (-0.5)
            ).astype(BF16)
            d_queries.append(dot_f32(d_scores, latent[part]).astype(BF16))
            d_latent.append(
                t_times(probs.astype(BF16), d_mixed[part]) + t_times(d_scores, queries[part])
            )
        d_queries = jnp.concatenate(d_queries, axis=0)
        d_latent = jnp.concatenate(d_latent, axis=0) + times_t(d_queries, r.w_qk.all()[...])
        d_latent = d_latent.astype(BF16)
        if packed:
            pack_factors(links, r, d_res_b, [d_latent, d_queries])
        else:
            r.d_res.held[...] = d_res_b
            r.d_res.send()
            r.d_latent.held[...] = d_latent
            r.d_queries.held[...] = d_queries
        d_normed = times_t(d_latent, r.w_down.all()[...])
        h = r.h.all()[...].astype(F32)
        inv = inverse_rms(h)
        d_input = (d_res + rms_back(h * inv, inv, d_normed)).astype(BF16)
        r.d_input.held[...] = d_input
        r.d_input.send()
        if onward:
            scaled = (d_input.astype(F32) * r.gate.all()[...]).astype(BF16)
            place_rows(r, r.pos_row.all()[...], scaled, slots, block_rows)

    outs = dict(d_input=like(rows, width))
    ins = {}
    if onward:
        ins, (slots, block_rows) = dict(pos_row=onward[0], gate=onward[1]), onward[2]
        outs.update(sent=[like(block_rows, width)] * (slots // block_rows))
    if packed:
        outs.update(packs=pack_shapes(links, rows, latent_width))
    else:
        outs.update(
            d_res=like(rows, width),
            d_latent=like(rows, latent_width),
            d_queries=like(rows, latent_width),
        )
    return run(
        "attend_backward",
        kernel,
        dict(
            back=back,
            pos_col=pos_col,
            u=upstream,
            residual=kept.residual,
            w_up=attn_w[2],
            latent=kept.latent,
            queries=kept.queries,
            probs=kept.probs,
            w_qk=attn_w[1],
            w_down=attn_w[0],
            h=inputs,
            **ins,
        ),
        outs,
        pack_scratch(links, rows, latent_width) if packed else None,
        first=4,
        later=later,
        merge=merge,
        only=only,
        place=links.place,
    )


def scatter(links, upstream, gate_col, pos_row, blocks, only, later=()):
    width = upstream.shape[1]
    slots, block_rows = blocks

    def kernel(r):
        scaled = (r.u.all()[...].astype(F32) * r.gate.all()[...]).astype(BF16)
        place_rows(r, r.pos_row.all()[...], scaled, slots, block_rows)

    ins = dict(u=upstream, gate=gate_col, pos_row=pos_row)
    outs = dict(sent=[like(block_rows, width)] * (slots // block_rows))
    return run("scatter", kernel, ins, outs, later=later, only=only, place=links.place).sent


def combine(links, residual, back, gate_col, pos_col, only, merge=None):
    rows, width = residual.shape

    def kernel(r):
        mixture = picked_rows(r, rows) * r.gate.all()[...]
        r.out.held[...] = (r.residual.all()[...].astype(F32) + mixture).astype(BF16)

    ins = dict(back=back, pos_col=pos_col, gate=gate_col, residual=residual)
    outs = dict(out=like(rows, width))
    return run("combine", kernel, ins, outs, merge=merge, only=only, place=links.place).out


def pack_weights(links, weights, copies, later=(), only=None):
    gate_w, up_w, down_w = weights
    width, split = gate_w.shape
    count = width // split
    half = count // 2
    shape = (width + half * split, split)

    def body(place, gate, up, down, *refs):
        *outs, held0, held1, sems, out_sems = refs[len(later) :]

        def copy_all():
            moves = []
            for source, held, first in ((gate, held0, 0), (up, held1, half)):
                part = [(source, held.at[pl.ds(0, width)])]
                for j in range(half):
                    columns = pl.ds((first + j) * split, split)
                    part.append((down.at[:, columns], held.at[pl.ds(width + j * split, split)]))
                moves.append(part)
            loads = [
                [pltpu.make_async_copy(a, b, sems.at[i, j]) for j, (a, b) in enumerate(part)]
                for i, part in enumerate(moves)
            ]
            for load in loads[0] + loads[1]:
                load.start()
            stores = []
            for i, held in enumerate((held0, held1)):
                for load in loads[i]:
                    load.wait()
                for k in range(i, 2 * copies, 2):
                    stores.append(pltpu.make_async_copy(held, outs[k], out_sems.at[k]))
                    stores[-1].start()
            for store in stores:
                store.wait()

        if only is None:
            copy_all()
        else:
            pl.when(place[2] == only)(copy_all)

    hbm = pl.BlockSpec(memory_space=pltpu.HBM)
    return list(
        pl.pallas_call(
            body,
            name="pack_weights",
            in_specs=[pl.BlockSpec(memory_space=pltpu.SMEM)] + [hbm] * (3 + len(later)),
            out_specs=[hbm] * (2 * copies),
            out_shape=[like(*shape)] * (2 * copies),
            scratch_shapes=[
                pltpu.VMEM(shape, BF16),
                pltpu.VMEM(shape, BF16),
                pltpu.SemaphoreType.DMA((2, half + 1)),
                pltpu.SemaphoreType.DMA((2 * copies,)),
            ],
            compiler_params=pltpu.CompilerParams(vmem_limit_bytes=GRANT),
        )(links.place, gate_w, up_w, down_w, *later)
    )


def experts_call(links, packs, only, rows=None, pre=None, hidden=None, d_rows=None, forward=False, block_rows=None, before=None, last=True, later=()):
    quarters = len(packs[0])
    split = packs[0][0].shape[1]
    backward = d_rows is not None
    sources = as_list(rows if rows is not None else d_rows) if hidden is None else []
    if hidden is None:
        block_rows, count = sources[0].shape[0], len(sources)
        width = sources[0].shape[1]
        slots = block_rows * count
    else:
        slots = hidden[0].shape[0]
        count = slots // block_rows
        width = 2 * packs[0][0].shape[0] // 3
    blocks = width // split
    half = blocks // 2

    step = 2 * split if width % (2 * split) == 0 else split
    steps = [slice(c, c + step) for c in range(0, width, step)]

    def kernel(r):
        def copies(q):
            wide, narrow = [], []
            for n, pack in enumerate((r.pack0[q], r.pack1[q])):
                if hidden is None:
                    wide.append((pack.at[pl.ds(0, width)], (r.all0, r.all1)[n].at[q]))
                for j in range(half):
                    target = r.all2.at[q, :, pl.ds((n * half + j) * split, split)]
                    narrow.append((pack.at[pl.ds(width + j * split, split)], target))
            found = wide + narrow if rows is not None else narrow + wide
            found = [pltpu.make_async_copy(a, b, r.sems.at[q, i]) for i, (a, b) in enumerate(found)]
            return (found[:2], found[2:]) if rows is not None else (found[: 2 * half], found[2 * half :])

        loads = [copies(q) for q in range(quarters)]
        def start(q):
            for copy in (*loads[q][0], *loads[q][1]):
                copy.start()

        def wait(part):
            for copy in part:
                copy.wait()

        start(0)
        r.open_rest()
        running = r.running if last else r.total.held

        def add(q, columns, part):
            part = part.astype(BF16).astype(F32)
            if q:
                part = part + running[:, columns]
            elif before is not None:
                part = part + r.before.all()[:, columns]
            if q == quarters - 1 and last:
                r.value.held[:, columns] = part.astype(BF16)
                piece = columns.start // step
                r.value.send_columns(pl.ds(columns.start, step), r.out_sems.at[piece])
            else:
                running[:, columns] = part

        for q in range(quarters):
            wait(loads[q][0])
            if q + 1 < quarters:
                start(q + 1)
            if rows is not None:
                held = r.rows.all()[...]
                gate_pre, up_pre = dot_f32(held, r.all0[q]), dot_f32(held, r.all1[q])
                if not backward:
                    r.gate_out.parts[q][1][...] = gate_pre
                    r.gate_out.send(q)
                    r.up_out.parts[q][1][...] = up_pre
                    r.up_out.send(q)
            elif pre is not None:
                gate_pre, up_pre = r.gate_pre.block(q)[...], r.up_pre.block(q)[...]
            if hidden is not None:
                hidden_q = r.hidden.block(q)[...]
            else:
                activated, slope = silu_parts(gate_pre)
            if rows is not None:
                hidden_q = (activated * up_pre).astype(BF16)
                if backward:
                    r.hidden_out.parts[q][1][...] = hidden_q
                    r.hidden_out.send(q)
            if rows is not None:
                wait(loads[q][1])
            if forward:
                for c in steps:
                    add(q, c, dot_f32(hidden_q, r.all2[q, :, c]))
            if backward:
                d_hidden = times_t(r.d_rows.all()[...], r.all2[q])
                if rows is None:
                    wait(loads[q][1])
                d_gate = (d_hidden * up_pre * slope).astype(BF16)
                d_up = (d_hidden * activated).astype(BF16)
                for c in steps:
                    add(q, c, times_t(d_gate, r.all0[q, c]) + times_t(d_up, r.all1[q, c]))

    ins = {}
    if rows is not None:
        ins.update(rows=rows)
    if backward:
        ins.update(d_rows=d_rows)
    if pre is not None:
        ins.update(gate_pre=pre[0], up_pre=pre[1])
    if hidden is not None:
        ins.update(hidden=hidden)
    if before is not None:
        ins.update(before=before)
    if last:
        outs = dict(value=[like(block_rows, width)] * count)
    else:
        outs = dict(total=like(slots, width, dtype=F32))
    if rows is not None and backward:
        outs.update(hidden_out=[like(slots, split)] * quarters)
    elif rows is not None:
        made = [like(slots, split, dtype=F32)] * quarters
        outs.update(gate_out=made, up_out=made)
    flops = 2 * slots * width * split * quarters * 0
    scratch = dict(
        all2=pltpu.VMEM((quarters, split, width), BF16),
        sems=pltpu.SemaphoreType.DMA((quarters, blocks + 2)),
    )
    if hidden is None:
        weights = pltpu.VMEM((quarters, width, split), BF16)
        scratch.update(all0=weights, all1=weights)
    if last:
        scratch.update(
            running=pltpu.VMEM((slots, width), F32),
            out_sems=pltpu.SemaphoreType.DMA((len(steps), count)),
        )
    return run(
        "experts",
        kernel,
        ins,
        outs,
        scratch,
        raw=dict(pack0=packs[0], pack1=packs[1]),
        first=2,
        later=later,
        flops=flops,
        only=only,
        place=links.place,
    )


def weight_gradients(links, early, late, width):
    experts, quarters = links.experts, links.quarters
    rows = early[0].shape[0] // (experts + 2)
    latent_width = early[0].shape[1]
    share, share_qk = width // (experts * quarters), latent_width // (experts * quarters)
    total = 2 * share + share_qk

    def plane_sums(r):
        def part(held, k, i, columns=latent_width):
            return held.block(k)[i * rows : (i + 1) * rows, :columns]

        sum_qk = jnp.zeros((latent_width, latent_width), F32)
        for k in range(quarters):
            sum_qk += t_times(part(r.early, k, experts + 1), part(r.late, k, experts + 1))
        r.qk[...] = sum_qk
        for e in range(experts):
            down = jnp.zeros((share, latent_width), F32)
            up = jnp.zeros((share, latent_width), F32)
            for k in range(quarters):
                down += t_times(part(r.early, k, e, share), part(r.late, k, experts))
                up += t_times(part(r.late, k, e, share), part(r.early, k, experts))
            at = pl.multiple_of(((r.place[0] ^ e) * quarters + r.place[1]) * share_qk, share_qk)
            made = r.away if e else r.own
            out = made.parts[max(e - 1, 0)][1]
            out[:share] = down.astype(out.dtype)
            out[share : 2 * share] = up.astype(out.dtype)
            out[2 * share :] = r.qk[pl.ds(at, share_qk)].astype(out.dtype)
            made.send(max(e - 1, 0))

    sums = run(
        "plane_sums",
        plane_sums,
        dict(early=early, late=late),
        dict(
            own=like(total, latent_width, dtype=F32),
            away=[like(total, latent_width)] * (experts - 1),
        ),
        dict(qk=pltpu.VMEM((latent_width, latent_width), F32)),
        place=links.place,
    )
    away = as_list(sums.away)
    got = [links.move(away[e - 1], links.every, expert_bits=e) for e in range(experts - 1, 0, -1)]

    value = sums.own + sum(g.astype(F32) for g in got)
    return value[:share], value[2 * share :], value[share : 2 * share]


def spread(links, rows):
    length, width = rows.shape
    count = links.experts * links.quarters
    by_owner = rows.reshape(length, count, width // count).transpose(1, 0, 2)
    got = lax.all_to_all(by_owner, ("expert", "dp"), split_axis=0, concat_axis=0, tiled=True)
    return got.reshape(count * length, width // count)


def nearer(packs):
    return [pack[:-1] for pack in packs]


def farthest(packs):
    return [pack[-1:] for pack in packs]


def body(x_in, dy_out, routes, gates, w_down, w_qk, w_up, e_gate, e_up, e_down):
    links = Links()
    micro, _, length, width = x_in.shape
    rows = micro * length
    capacity = max(2, (3 * length + 2 * links.experts - 1) // (2 * links.experts))
    attn_w = (w_down[0], w_qk[0], w_up[0])
    first = links.section == 0

    route = routes[0, :, 0, :, 0]
    earlier = lax.broadcasted_iota(jnp.int32, (length, length), 0) > lax.broadcasted_iota(
        jnp.int32, (length, length), 1
    )
    same = route[:, :, None] == route[:, None, :]
    rank = jnp.sum((same & earlier).astype(jnp.int32), axis=2)
    slot = jnp.arange(micro, dtype=jnp.int32)[:, None] * capacity + rank
    position = (links.relative(route) * (micro * capacity) + slot).reshape(rows)
    pos_row, pos_col = position.reshape(1, rows), position.reshape(rows, 1)
    gate_col = gates[0, :, 0].reshape(rows, 1)
    slots = links.experts * micro * capacity
    blocks = (slots, micro * capacity if links.pairwise else slots)

    own = (e_gate[0, 0], e_up[0, 0], e_down[0, 0])
    packed = pack_weights(links, own, 1)
    dy = dy_out.reshape(rows, width)
    sent_1 = scatter(links, dy, gate_col, pos_row, blocks, 1)
    kept_0 = attend_forward(
        links, x_in.reshape(rows, width), micro, attn_w, pos_row, blocks, 0, as_list(sent_1)[:1]
    )
    rows_0 = links.exchange(kept_0.sent, 0)
    dm_1 = links.exchange(tied(as_list(sent_1), rows_0[1:]) if links.pairwise else sent_1, 1)
    again = pack_weights(links, own, 1, as_list(kept_0.sent)[:1], 0)
    set_0 = links.gather_quarters(packed + again, 0, hurry=True)
    onward = jnp.concatenate([pos_row.astype(F32), gate_col.reshape(1, rows)], axis=0)
    packed_1 = pack_weights(links, own, 2, as_list(dm_1), 1)
    onward = tied([onward], [*set_0[0][1:], *set_0[1][1:]])[0]
    there = links.move(onward, (0,), section_bit=1)
    packed_1 = tied(packed_1, [there])
    onward = (there[:1].astype(jnp.int32), there[1].reshape(rows, 1), blocks)

    near_0 = experts_call(links, nearer(set_0), 0, rows=rows_0, forward=True, last=False, later=packed_1[:1])
    made_0 = experts_call(links, farthest(set_0), 0, rows=rows_0, forward=True, before=near_0.total, later=[there])
    pre_0 = [
        as_list(near_0.gate_out) + as_list(made_0.gate_out),
        as_list(near_0.up_out) + as_list(made_0.up_out),
    ]
    returned_0 = links.exchange(made_0.value, 0)
    out_0 = combine(links, kept_0.residual, returned_0, gate_col, pos_col, 0)
    h_1 = links.move(out_0, (0,), section_bit=1)
    kept_1 = attend_forward(links, h_1, micro, attn_w, pos_row, blocks, 1)
    sent = as_list(kept_1.sent)
    set_1 = links.gather_quarters(packed_1, 1, sent[:1], as_list(returned_0))
    if links.pairwise:
        sent = [sent[0], *tied(sent[1:], [set_1[0][1]])]
        rows_1 = links.exchange(sent, 1)
        early = factors(links, kept_0.inputs, [kept_0.mixed, kept_0.latent], 0, True)
        early = factors(
            links, h_1, [kept_1.mixed, kept_1.latent], 1, True, dict(packs=early), rows_1
        )
    else:
        rows_1 = links.exchange(kept_1.sent, 1)
    set_1 = [[mine] + got[1:] for mine, got in zip(packed, set_1)]
    near_1 = experts_call(links, nearer(set_1), 1, rows=rows_1, d_rows=dm_1, last=False)
    made_1 = experts_call(links, farthest(set_1), 1, rows=rows_1, d_rows=dm_1, before=near_1.total)
    hidden_1 = as_list(near_1.hidden_out) + as_list(made_1.hidden_out)
    back_1 = links.exchange(made_1.value, 1)
    if links.pairwise:
        late_1 = attend_backward(
            links, kept_1, micro, dy, back_1, attn_w, pos_col, 1, early[:1], onward=onward
        )
        dm_0 = links.exchange_over(late_1.sent, 1)
        u_0 = links.move(late_1.d_input, (1,), section_bit=1)
    else:
        late_1 = attend_backward(links, kept_1, micro, dy, back_1, attn_w, pos_col, 1)
        u_0 = links.move(late_1.d_input, (1,), section_bit=1)
        dm_0 = links.exchange(scatter(links, u_0, gate_col, pos_row, blocks, 0), 0)
    value_1 = experts_call(
        links,
        set_1,
        1,
        hidden=hidden_1,
        forward=True,
        block_rows=blocks[1],
        later=[late_1.d_latent],
    ).value
    if links.pairwise:
        value_1 = tied(value_1, dm_0[1:])
    returned_1 = links.exchange(value_1, 1)
    later = as_list(returned_1)
    back_0 = experts_call(links, set_0, 0, pre=pre_0, d_rows=dm_0, later=later).value
    merge = dict(d_input=late_1.d_input)
    if links.pairwise:
        narrow = [late_1.d_latent, late_1.d_queries]
        merge.update(packs=factors(links, late_1.d_res, narrow, 1, False, later=dm_0))
    late_0 = attend_backward(
        links, kept_0, micro, u_0, links.exchange(back_0, 0), attn_w, pos_col, 0, merge=merge
    )
    grads_in = late_0.d_input.reshape(1, micro, 1, length, width)
    activations = combine(
        links, kept_1.residual, returned_1, gate_col, pos_col, 1, dict(out=out_0)
    ).reshape(1, micro, 1, length, width)

    if links.pairwise:
        def plane(packs):
            return packs[:1] + [
                links.move(packs[k], links.every, quarter_bits=k) for k in range(1, links.quarters)
            ]

        g_down, g_qk, g_up_t = weight_gradients(links, plane(early), plane(late_0.packs), width)
    else:
        def pick(upper, lower):
            return jnp.where(first, upper, lower)

        def gathered(upper, lower):
            return lax.all_gather(pick(upper, lower), ("expert", "dp"), axis=0, tiled=True)

        g_down = t_times(
            spread(links, pick(kept_0.normed, kept_1.normed)),
            gathered(late_0.d_latent, late_1.d_latent),
        )
        g_qk = t_times(
            spread(links, pick(kept_0.latent, kept_1.latent)),
            gathered(late_0.d_queries, late_1.d_queries),
        )
        g_up_t = t_times(
            spread(links, pick(late_0.d_res, late_1.d_res)),
            gathered(kept_0.mixed, kept_1.mixed),
        )
    return (activations, grads_in, g_down[None], g_qk[None], g_up_t[None])


def solution(mesh):
    by_sequence = P(None, ("expert", "dp"), None, None)
    by_layer = P("section", None, ("expert", "dp"), None, None)
    shared = P("section", None, None)
    placed = (
        by_sequence,
        by_sequence,
        by_layer,
        by_layer,
        shared,
        shared,
        shared,
        P("section", "expert", None, "dp"),
        P("section", "expert", None, "dp"),
        P("section", "expert", "dp", None),
    )
    by_rows = P("section", ("expert", "dp"), None)
    return jax.shard_map(
        body,
        mesh=mesh,
        in_specs=placed,
        out_specs=(by_layer, by_layer, by_rows, by_rows, by_rows),
        check_vma=False,
    )
```

```python
from types import SimpleNamespace

import jax
import jax.numpy as jnp
from jax import lax
from jax.experimental import pallas as pl
from jax.experimental.pallas import tpu as pltpu
from jax.sharding import PartitionSpec as P

epsilon = 1e-06
AXES = ("section", "expert", "dp")
GRANT = (64 << 20) - (256 << 10)
ATTENTION = ("w_down", "w_qk", "w_up")
BF16, F32 = jnp.bfloat16, jnp.float32


def dot_f32(left, right):
    return jnp.dot(left, right, preferred_element_type=F32)


def times_t(left, right):
    return lax.dot_general(left, right, (((1,), (1,)), ((), ())), preferred_element_type=F32)


def t_times(left, right):
    return lax.dot_general(left, right, (((0,), (0,)), ((), ())), preferred_element_type=F32)


def inverse_rms(values):
    return lax.rsqrt(jnp.mean(values * values, axis=-1, keepdims=True) + epsilon)


def rms_back(normed, inv_rms, upstream):
    return inv_rms * (upstream - normed * jnp.mean(upstream * normed, axis=-1, keepdims=True))


def silu_parts(gate_pre):
    sigmoid = jax.nn.sigmoid(gate_pre)
    return (gate_pre * sigmoid, sigmoid * (1.0 + gate_pre * (1.0 - sigmoid)))


class Held:
    def __init__(self, refs, held, sems):
        self.held, self.parts, self.seen = held, [], set()
        start = 0
        for i, ref in enumerate(refs):
            target = held
            if len(refs) > 1:
                target = held.at[pl.ds(start, ref.shape[0])]
                start += ref.shape[0]
            self.parts.append((pltpu.make_async_copy(ref, target, sems.at[i]), target))

    def start(self, i):
        if i < len(self.parts):
            self.parts[i][0].start()

    def block(self, i):
        if i not in self.seen:
            self.seen.add(i)
            self.parts[i][0].wait()
        return self.parts[i][1]

    def all(self):
        for i in range(len(self.parts)):
            self.block(i)
        return self.held


class Made:
    def __init__(self, refs, held, sems):
        self.held, self.parts, self.sent = held, [], set()
        self.refs, self.pieces = refs, []
        start = 0
        for i, ref in enumerate(refs):
            source = held
            if len(refs) > 1:
                source = held.at[pl.ds(start, ref.shape[0])]
                start += ref.shape[0]
            self.parts.append((pltpu.make_async_copy(source, ref, sems.at[i]), source))

    def send(self, i=0):
        if i not in self.sent:
            self.sent.add(i)
            self.parts[i][0].start()

    def send_columns(self, columns, sems):
        for i, (_, source) in enumerate(self.parts):
            copy = pltpu.make_async_copy(source.at[:, columns], self.refs[i].at[:, columns], sems.at[i])
            copy.start()
            self.pieces.append(copy)

    def finish(self):
        for copy in self.pieces:
            copy.wait()
        if self.pieces:
            return
        for i in range(len(self.parts)):
            self.send(i)
        for copy, _ in self.parts:
            copy.wait()


def as_list(value):
    return list(value) if isinstance(value, (list, tuple)) else [value]


def stage_shape(arrays):
    if len(arrays) == 1:
        return pltpu.VMEM(arrays[0].shape, arrays[0].dtype)
    rows = sum(a.shape[0] for a in arrays)
    return pltpu.VMEM((rows, *arrays[0].shape[1:]), arrays[0].dtype)


def run(name, kernel, ins, outs, scratch=None, vmem=None, later=(), merge=None, only=None, place=None, raw=None, first=99, flops=0):
    scratch, vmem, merge, raw = scratch or {}, vmem or {}, merge or {}, raw or {}
    ins = {k: as_list(v) for k, v in ins.items()}
    outs = {k: as_list(v) for k, v in outs.items()}
    merge = {k: as_list(v) for k, v in merge.items()}
    flat_in = [a for v in ins.values() for a in v]
    flat_out = [a for v in outs.values() for a in v]
    flat_merge = [a for v in merge.values() for a in v]
    stages = [stage_shape(v) for v in [*ins.values(), *outs.values()]]
    sems = [pltpu.SemaphoreType.DMA((len(v),)) for v in [*ins.values(), *outs.values()]]
    smem = [] if place is None else [place]

    def body(*refs):
        refs = list(refs)

        def take(count):
            got = refs[:count]
            del refs[:count]
            return got

        place_refs, vmem_refs = take(len(smem)), take(len(vmem))
        in_refs = [take(len(v)) for v in ins.values()]
        instead = {k: take(len(v)) for k, v in merge.items()}
        raw_refs = {k: take(len(v)) for k, v in raw.items()}
        take(len(later))
        out_refs = [take(len(v)) for v in outs.values()]
        staged, signals = take(len(stages)), take(len(sems))
        r = SimpleNamespace(**dict(zip(vmem, vmem_refs)))
        if smem:
            r.place = place_refs[0]
        held = [Held(a, b, c) for a, b, c in zip(in_refs, staged, signals)]
        made = [Made(a, b, c) for a, b, c in zip(out_refs, staged[len(ins) :], signals[len(ins) :])]
        r.__dict__.update(zip(ins, held))
        r.__dict__.update(zip(outs, made))
        r.__dict__.update(zip(scratch, refs))

        r.__dict__.update(raw_refs)

        def open_all(part):
            for i in range(max([len(h.parts) for h in part], default=0)):
                for h in part:
                    h.start(i)

        r.open_rest = lambda: open_all(held[first:])

        def work():
            open_all(held[:first])
            if first >= len(held):
                r.open_rest()
            kernel(r)
            for h in held:
                h.all()
            for m in made:
                m.finish()

        def passed_on():
            for k, m, sem in zip(outs, made, signals[len(ins) :]):
                parts = list(zip(instead.get(k, ()), m.parts))
                loads = [
                    pltpu.make_async_copy(ref, part[1], sem.at[i]) for i, (ref, part) in enumerate(parts)
                ]
                for load in loads:
                    load.start()
                for load, (_, part) in zip(loads, parts):
                    load.wait()
                    part[0].start()
                for _, part in parts:
                    part[0].wait()

        if only is None:
            work()
        else:
            pl.when(r.place[2] == only)(work)
            if merge:
                pl.when(r.place[2] != only)(passed_on)

    flat_raw = [a for v in raw.values() for a in v]
    everything = [*smem, *vmem.values(), *flat_in, *flat_merge, *flat_raw, *later]
    spaces = [pltpu.SMEM] * len(smem) + [pltpu.VMEM] * len(vmem)
    spaces += [pltpu.HBM] * (len(everything) - len(spaces))
    got = pl.pallas_call(
        body,
        name=name,
        in_specs=[pl.BlockSpec(memory_space=s) for s in spaces],
        out_specs=[pl.BlockSpec(memory_space=pltpu.HBM) for _ in flat_out],
        out_shape=flat_out,
        scratch_shapes=[*stages, *sems, *scratch.values()],
        compiler_params=pltpu.CompilerParams(vmem_limit_bytes=GRANT),
        cost_estimate=pl.CostEstimate(
            flops=flops,
            bytes_accessed=sum(a.size * a.dtype.itemsize for a in flat_in) * 0,
            transcendentals=0,
        ),
    )(*everything)
    got, result = list(got), SimpleNamespace()
    for k, v in outs.items():
        part, got = got[: len(v)], got[len(v) :]
        setattr(result, k, part if len(part) > 1 else part[0])
    return result


def like(*shape, dtype=BF16):
    return jax.ShapeDtypeStruct(shape, dtype)


class Links:
    def __init__(self):
        self.sections, self.experts, self.quarters = [lax.axis_size(a) for a in AXES]
        self.section, self.expert, self.quarter = [lax.axis_index(a) for a in AXES]
        self.pairwise = self.experts <= 8
        self.every = tuple(range(self.sections))
        self.place = jnp.stack([self.expert, self.quarter, self.section])

    def move(self, x, sections, section_bit=0, expert_bits=0, quarter_bits=0):
        def number(s, e, d):
            return (s * self.experts + e) * self.quarters + d

        pairs = [
            (number(s, e, d), number(s ^ section_bit, e ^ expert_bits, d ^ quarter_bits))
            for s in sections
            for e in range(self.experts)
            for d in range(self.quarters)
        ]
        return lax.ppermute(x, AXES, pairs)

    def relative(self, expert):
        return expert ^ self.expert if self.pairwise else expert

    def exchange_over(self, blocks, section):
        got = {
            k: self.move(blocks[k], (section,), section_bit=1, expert_bits=k)
            for k in range(self.experts - 1, -1, -1)
        }
        return [got[k] for k in range(self.experts)]

    def exchange(self, blocks, section):
        if not self.pairwise:
            sent = blocks.reshape(self.experts, -1, blocks.shape[1])
            out = lax.all_to_all(sent, "expert", split_axis=0, concat_axis=0, tiled=True)
            return out.reshape(blocks.shape)
        got = {k: self.move(blocks[k], (section,), expert_bits=k) for k in range(self.experts - 1, 0, -1)}
        return [blocks[0]] + [got[k] for k in range(1, self.experts)]

    def gather_quarters(self, packs, section, before=(), between=(), hurry=False):
        if self.quarters != 4:
            return [
                [p] + [self.move(p, (section,), quarter_bits=k) for k in range(1, self.quarters)]
                for p in packs[:2]
            ]

        def across(one, two):
            return [
                self.move(one, (section,), quarter_bits=1),
                self.move(two, (section,), quarter_bits=2),
            ]

        step = across(packs[0], packs[1])
        again = tied(packs[2:], between) if between else packs[-2:]
        other = across(again[1], again[0])
        if not hurry:
            step = tied(step, [*other, *before])
        third = across(step[1], step[0])
        return [[packs[0], step[0], other[1], third[1]], [packs[1], other[0], step[1], third[0]]]


def tied(arrays, first):
    count = len(arrays)
    hbm = pl.BlockSpec(memory_space=pltpu.HBM)
    return list(
        pl.pallas_call(
            lambda *refs: None,
            name="tied",
            in_specs=[hbm] * (count + len(first)),
            out_specs=[hbm] * count,
            out_shape=[like(*a.shape, dtype=a.dtype) for a in arrays],
            input_output_aliases={i: i for i in range(count)},
            compiler_params=pltpu.CompilerParams(vmem_limit_bytes=GRANT),
        )(*arrays, *first)
    )


def attend_forward(links, inputs, micro, attn_w, pos_row, blocks, only, later=()):
    rows, width = inputs.shape
    length = rows // micro
    latent_width = attn_w[0].shape[1]
    slots, block_rows = blocks

    def kernel(r):
        h = r.h.all()[...].astype(F32)
        r.open_rest()
        normed_b = (h * inverse_rms(h)).astype(BF16)
        latent = dot_f32(normed_b, r.w_down.all()[...]).astype(BF16)
        queries = dot_f32(latent, r.w_qk.all()[...]).astype(BF16)
        r.latent.held[...] = latent
        r.queries.held[...] = queries
        causal = lax.broadcasted_iota(jnp.int32, (length, length), 0) >= lax.broadcasted_iota(
            jnp.int32, (length, length), 1
        )
        mixed = []
        for m in range(micro):
            part = slice(m * length, (m + 1) * length)
            scores = times_t(queries[part], latent[part]) * latent_width ** (-0.5)
            scores = jnp.where(causal, scores, -1e30)
            exponent = jnp.exp(scores - jnp.max(scores, axis=-1, keepdims=True))
            probs = exponent / jnp.sum(exponent, axis=-1, keepdims=True)
            r.probs.held[m] = probs
            mixed.append(dot_f32(probs.astype(BF16), latent[part]).astype(BF16))
        mixed = jnp.concatenate(mixed, axis=0)
        residual = (h + dot_f32(mixed, r.w_up.all()[...])).astype(BF16)
        r.residual.held[...] = residual
        r.residual.send()
        wide = residual.astype(F32)
        second_b = (wide * inverse_rms(wide)).astype(BF16)
        place_rows(r, r.pos_row.all()[...], second_b, slots, block_rows)
        r.mixed.held[...] = mixed
        if not links.pairwise:
            r.normed.held[...] = normed_b

    outs = dict(
        sent=[like(block_rows, width)] * (slots // block_rows),
        residual=like(rows, width),
        latent=like(rows, latent_width),
        queries=like(rows, latent_width),
        mixed=like(rows, latent_width),
        probs=like(micro, length, length, dtype=F32),
    )
    if not links.pairwise:
        outs.update(normed=like(rows, width))
    got = run(
        "attend_forward",
        kernel,
        dict(h=inputs, **dict(zip(ATTENTION, attn_w)), pos_row=pos_row),
        outs,
        first=2,
        later=later,
        only=only,
        place=links.place,
    )
    got.inputs = inputs
    return got


def factors(links, wide, narrow, only, normalize, merge=None, later=()):
    rows = wide.shape[0]
    latent_width = narrow[0].shape[1]

    def kernel(r):
        values = r.wide.all()[...]
        if normalize:
            h = values.astype(F32)
            values = (h * inverse_rms(h)).astype(BF16)
        pack_factors(links, r, values, [r.narrow.block(0)[...], r.narrow.block(1)[...]])

    return as_list(
        run(
            "factors",
            kernel,
            dict(wide=wide, narrow=narrow),
            dict(packs=pack_shapes(links, rows, latent_width)),
            pack_scratch(links, rows, latent_width),
            later=later,
            merge=merge,
            only=only,
            place=links.place,
        ).packs
    )


def place_rows(r, pos_row, values, slots, block_rows):
    shape = (slots, pos_row.shape[1])
    place = (pos_row == lax.broadcasted_iota(jnp.int32, shape, 0)).astype(BF16)
    for k in range(slots // block_rows):
        part = slice(k * block_rows, (k + 1) * block_rows)
        r.sent.held[part] = dot_f32(place[part], values).astype(BF16)
        r.sent.send(k)


def pack_shapes(links, rows, latent_width):
    return [like((links.experts + 2) * rows, latent_width)] * links.quarters


def pack_scratch(links, rows, latent_width):
    if not links.pairwise:
        return {}
    return dict(cols=pltpu.VMEM((links.experts * links.quarters, rows, latent_width), BF16))


def pack_factors(links, r, wide, narrow):
    rows, width = wide.shape
    experts, quarters = links.experts, links.quarters
    share = width // (experts * quarters)
    for i in range(experts * quarters):
        r.cols[i, :, :share] = wide[:, i * share : (i + 1) * share]
    expert, quarter = r.place[0], r.place[1]
    for k in range(quarters):
        out = r.packs.parts[k][1]
        for e in range(experts):
            out[e * rows : (e + 1) * rows] = r.cols[(expert ^ e) * quarters + (quarter ^ k)]
        for n, values in enumerate(narrow):
            out[(experts + n) * rows : (experts + n + 1) * rows] = values
        r.packs.send(k)


def picked_rows(r, rows):
    values = r.back.all()
    place = (
        r.pos_col.all()[...] == lax.broadcasted_iota(jnp.int32, (rows, values.shape[0]), 1)
    ).astype(BF16)
    return dot_f32(place, values[...])


def attend_backward(links, kept, micro, upstream, back, attn_w, pos_col, only, later=(), merge=None, onward=None):
    inputs = kept.inputs
    rows, width = inputs.shape
    length = rows // micro
    latent_width = attn_w[0].shape[1]
    packed = links.pairwise and not onward

    def kernel(r):
        r.back.all()
        r.open_rest()
        d_second = picked_rows(r, rows)
        u = r.u.all()[...].astype(F32)
        wide = r.residual.all()[...].astype(F32)
        inv = inverse_rms(wide)
        d_res = u + rms_back(wide * inv, inv, d_second)
        d_res_b = d_res.astype(BF16)
        d_mixed = times_t(d_res_b, r.w_up.all()[...]).astype(BF16)
        latent, queries, all_probs = r.latent.all()[...], r.queries.all()[...], r.probs.all()
        d_latent, d_queries = [], []
        for m in range(micro):
            part = slice(m * length, (m + 1) * length)
            probs = all_probs[m]
            d_probs = times_t(d_mixed[part], latent[part])
            d_scores = (
                probs
                * (d_probs - jnp.sum(d_probs * probs, axis=-1, keepdims=True))
                * latent_width ** (-0.5)
            ).astype(BF16)
            d_queries.append(dot_f32(d_scores, latent[part]).astype(BF16))
            d_latent.append(
                t_times(probs.astype(BF16), d_mixed[part]) + t_times(d_scores, queries[part])
            )
        d_queries = jnp.concatenate(d_queries, axis=0)
        d_latent = jnp.concatenate(d_latent, axis=0) + times_t(d_queries, r.w_qk.all()[...])
        d_latent = d_latent.astype(BF16)
        if packed:
            pack_factors(links, r, d_res_b, [d_latent, d_queries])
        else:
            r.d_res.held[...] = d_res_b
            r.d_res.send()
            r.d_latent.held[...] = d_latent
            r.d_queries.held[...] = d_queries
        d_normed = times_t(d_latent, r.w_down.all()[...])
        h = r.h.all()[...].astype(F32)
        inv = inverse_rms(h)
        d_input = (d_res + rms_back(h * inv, inv, d_normed)).astype(BF16)
        r.d_input.held[...] = d_input
        r.d_input.send()
        if onward:
            scaled = (d_input.astype(F32) * r.gate.all()[...]).astype(BF16)
            place_rows(r, r.pos_row.all()[...], scaled, slots, block_rows)

    outs = dict(d_input=like(rows, width))
    ins = {}
    if onward:
        ins, (slots, block_rows) = dict(pos_row=onward[0], gate=onward[1]), onward[2]
        outs.update(sent=[like(block_rows, width)] * (slots // block_rows))
    if packed:
        outs.update(packs=pack_shapes(links, rows, latent_width))
    else:
        outs.update(
            d_res=like(rows, width),
            d_latent=like(rows, latent_width),
            d_queries=like(rows, latent_width),
        )
    return run(
        "attend_backward",
        kernel,
        dict(
            back=back,
            pos_col=pos_col,
            u=upstream,
            residual=kept.residual,
            w_up=attn_w[2],
            latent=kept.latent,
            queries=kept.queries,
            probs=kept.probs,
            w_qk=attn_w[1],
            w_down=attn_w[0],
            h=inputs,
            **ins,
        ),
        outs,
        pack_scratch(links, rows, latent_width) if packed else None,
        first=4,
        later=later,
        merge=merge,
        only=only,
        place=links.place,
    )


def scatter(links, upstream, gate_col, pos_row, blocks, only, later=()):
    width = upstream.shape[1]
    slots, block_rows = blocks

    def kernel(r):
        scaled = (r.u.all()[...].astype(F32) * r.gate.all()[...]).astype(BF16)
        place_rows(r, r.pos_row.all()[...], scaled, slots, block_rows)

    ins = dict(u=upstream, gate=gate_col, pos_row=pos_row)
    outs = dict(sent=[like(block_rows, width)] * (slots // block_rows))
    return run("scatter", kernel, ins, outs, later=later, only=only, place=links.place).sent


def combine(links, residual, back, gate_col, pos_col, only, merge=None):
    rows, width = residual.shape

    def kernel(r):
        mixture = picked_rows(r, rows) * r.gate.all()[...]
        r.out.held[...] = (r.residual.all()[...].astype(F32) + mixture).astype(BF16)

    ins = dict(back=back, pos_col=pos_col, gate=gate_col, residual=residual)
    outs = dict(out=like(rows, width))
    return run("combine", kernel, ins, outs, merge=merge, only=only, place=links.place).out


def pack_weights(links, weights, copies, later=(), only=None):
    gate_w, up_w, down_w = weights
    width, split = gate_w.shape
    count = width // split
    half = count // 2
    shape = (width + half * split, split)

    def body(place, gate, up, down, *refs):
        *outs, held0, held1, sems, out_sems = refs[len(later) :]

        def copy_all():
            moves = []
            for source, held, first in ((gate, held0, 0), (up, held1, half)):
                part = [(source, held.at[pl.ds(0, width)])]
                for j in range(half):
                    columns = pl.ds((first + j) * split, split)
                    part.append((down.at[:, columns], held.at[pl.ds(width + j * split, split)]))
                moves.append(part)
            loads = [
                [pltpu.make_async_copy(a, b, sems.at[i, j]) for j, (a, b) in enumerate(part)]
                for i, part in enumerate(moves)
            ]
            for load in loads[0] + loads[1]:
                load.start()
            stores = []
            for i, held in enumerate((held0, held1)):
                for load in loads[i]:
                    load.wait()
                for k in range(i, 2 * copies, 2):
                    stores.append(pltpu.make_async_copy(held, outs[k], out_sems.at[k]))
                    stores[-1].start()
            for store in stores:
                store.wait()

        if only is None:
            copy_all()
        else:
            pl.when(place[2] == only)(copy_all)

    hbm = pl.BlockSpec(memory_space=pltpu.HBM)
    return list(
        pl.pallas_call(
            body,
            name="pack_weights",
            in_specs=[pl.BlockSpec(memory_space=pltpu.SMEM)] + [hbm] * (3 + len(later)),
            out_specs=[hbm] * (2 * copies),
            out_shape=[like(*shape)] * (2 * copies),
            scratch_shapes=[
                pltpu.VMEM(shape, BF16),
                pltpu.VMEM(shape, BF16),
                pltpu.SemaphoreType.DMA((2, half + 1)),
                pltpu.SemaphoreType.DMA((2 * copies,)),
            ],
            compiler_params=pltpu.CompilerParams(vmem_limit_bytes=GRANT),
        )(links.place, gate_w, up_w, down_w, *later)
    )


def experts_call(links, packs, only, rows=None, pre=None, hidden=None, d_rows=None, forward=False, block_rows=None, before=None, last=True, later=()):
    quarters = len(packs[0])
    split = packs[0][0].shape[1]
    backward = d_rows is not None
    sources = as_list(rows if rows is not None else d_rows) if hidden is None else []
    if hidden is None:
        block_rows, count = sources[0].shape[0], len(sources)
        width = sources[0].shape[1]
        slots = block_rows * count
    else:
        slots = hidden[0].shape[0]
        count = slots // block_rows
        width = 2 * packs[0][0].shape[0] // 3
    blocks = width // split
    half = blocks // 2

    step = 2 * split if width % (2 * split) == 0 else split
    steps = [slice(c, c + step) for c in range(0, width, step)]

    def kernel(r):
        def copies(q):
            wide, narrow = [], []
            for n, pack in enumerate((r.pack0[q], r.pack1[q])):
                if hidden is None:
                    wide.append((pack.at[pl.ds(0, width)], (r.all0, r.all1)[n].at[q]))
                for j in range(half):
                    target = r.all2.at[q, :, pl.ds((n * half + j) * split, split)]
                    narrow.append((pack.at[pl.ds(width + j * split, split)], target))
            found = wide + narrow if rows is not None else narrow + wide
            found = [pltpu.make_async_copy(a, b, r.sems.at[q, i]) for i, (a, b) in enumerate(found)]
            return (found[:2], found[2:]) if rows is not None else (found[: 2 * half], found[2 * half :])

        loads = [copies(q) for q in range(quarters)]
        def start(q):
            for copy in (*loads[q][0], *loads[q][1]):
                copy.start()

        def wait(part):
            for copy in part:
                copy.wait()

        start(0)
        r.open_rest()
        running = r.running if last else r.total.held

        def add(q, columns, part):
            part = part.astype(BF16).astype(F32)
            if q:
                part = part + running[:, columns]
            elif before is not None:
                part = part + r.before.all()[:, columns]
            if q == quarters - 1 and last:
                r.value.held[:, columns] = part.astype(BF16)
                piece = columns.start // step
                r.value.send_columns(pl.ds(columns.start, step), r.out_sems.at[piece])
            else:
                running[:, columns] = part

        for q in range(quarters):
            wait(loads[q][0])
            if q + 1 < quarters:
                start(q + 1)
            if rows is not None:
                held = r.rows.all()[...]
                gate_pre, up_pre = dot_f32(held, r.all0[q]), dot_f32(held, r.all1[q])
                if not backward:
                    r.gate_out.parts[q][1][...] = gate_pre
                    r.gate_out.send(q)
                    r.up_out.parts[q][1][...] = up_pre
                    r.up_out.send(q)
            elif pre is not None:
                gate_pre, up_pre = r.gate_pre.block(q)[...], r.up_pre.block(q)[...]
            if hidden is not None:
                hidden_q = r.hidden.block(q)[...]
            else:
                activated, slope = silu_parts(gate_pre)
            if rows is not None:
                hidden_q = (activated * up_pre).astype(BF16)
                if backward:
                    r.hidden_out.parts[q][1][...] = hidden_q
                    r.hidden_out.send(q)
            if rows is not None:
                wait(loads[q][1])
            if forward:
                for c in steps:
                    add(q, c, dot_f32(hidden_q, r.all2[q, :, c]))
            if backward:
                d_hidden = times_t(r.d_rows.all()[...], r.all2[q])
                if rows is None:
                    wait(loads[q][1])
                d_gate = (d_hidden * up_pre * slope).astype(BF16)
                d_up = (d_hidden * activated).astype(BF16)
                for c in steps:
                    add(q, c, times_t(d_gate, r.all0[q, c]) + times_t(d_up, r.all1[q, c]))

    ins = {}
    if rows is not None:
        ins.update(rows=rows)
    if backward:
        ins.update(d_rows=d_rows)
    if pre is not None:
        ins.update(gate_pre=pre[0], up_pre=pre[1])
    if hidden is not None:
        ins.update(hidden=hidden)
    if before is not None:
        ins.update(before=before)
    if last:
        outs = dict(value=[like(block_rows, width)] * count)
    else:
        outs = dict(total=like(slots, width, dtype=F32))
    if rows is not None and backward:
        outs.update(hidden_out=[like(slots, split)] * quarters)
    elif rows is not None:
        made = [like(slots, split, dtype=F32)] * quarters
        outs.update(gate_out=made, up_out=made)
    flops = 2 * slots * width * split * quarters * 0
    scratch = dict(
        all2=pltpu.VMEM((quarters, split, width), BF16),
        sems=pltpu.SemaphoreType.DMA((quarters, blocks + 2)),
    )
    if hidden is None:
        weights = pltpu.VMEM((quarters, width, split), BF16)
        scratch.update(all0=weights, all1=weights)
    if last:
        scratch.update(
            running=pltpu.VMEM((slots, width), F32),
            out_sems=pltpu.SemaphoreType.DMA((len(steps), count)),
        )
    return run(
        "experts",
        kernel,
        ins,
        outs,
        scratch,
        raw=dict(pack0=packs[0], pack1=packs[1]),
        first=2,
        later=later,
        flops=flops,
        only=only,
        place=links.place,
    )


def weight_gradients(links, early, late, width):
    experts, quarters = links.experts, links.quarters
    rows = early[0].shape[0] // (experts + 2)
    latent_width = early[0].shape[1]
    share, share_qk = width // (experts * quarters), latent_width // (experts * quarters)
    total = 2 * share + share_qk

    def plane_sums(r):
        def part(held, k, i, columns=latent_width):
            return held.block(k)[i * rows : (i + 1) * rows, :columns]

        sum_qk = jnp.zeros((latent_width, latent_width), F32)
        for k in range(quarters):
            sum_qk += t_times(part(r.early, k, experts + 1), part(r.late, k, experts + 1))
        r.qk[...] = sum_qk
        for e in range(experts):
            down = jnp.zeros((share, latent_width), F32)
            up = jnp.zeros((share, latent_width), F32)
            for k in range(quarters):
                down += t_times(part(r.early, k, e, share), part(r.late, k, experts))
                up += t_times(part(r.late, k, e, share), part(r.early, k, experts))
            at = pl.multiple_of(((r.place[0] ^ e) * quarters + r.place[1]) * share_qk, share_qk)
            made = r.away if e else r.own
            out = made.parts[max(e - 1, 0)][1]
            out[:share] = down.astype(out.dtype)
            out[share : 2 * share] = up.astype(out.dtype)
            out[2 * share :] = r.qk[pl.ds(at, share_qk)].astype(out.dtype)
            made.send(max(e - 1, 0))

    sums = run(
        "plane_sums",
        plane_sums,
        dict(early=early, late=late),
        dict(
            own=like(total, latent_width, dtype=F32),
            away=[like(total, latent_width)] * (experts - 1),
        ),
        dict(qk=pltpu.VMEM((latent_width, latent_width), F32)),
        place=links.place,
    )
    away = as_list(sums.away)
    got = [links.move(away[e - 1], links.every, expert_bits=e) for e in range(experts - 1, 0, -1)]

    value = sums.own + sum(g.astype(F32) for g in got)
    return value[:share], value[2 * share :], value[share : 2 * share]


def spread(links, rows):
    length, width = rows.shape
    count = links.experts * links.quarters
    by_owner = rows.reshape(length, count, width // count).transpose(1, 0, 2)
    got = lax.all_to_all(by_owner, ("expert", "dp"), split_axis=0, concat_axis=0, tiled=True)
    return got.reshape(count * length, width // count)


def nearer(packs):
    return [pack[:-1] for pack in packs]


def farthest(packs):
    return [pack[-1:] for pack in packs]


def body(x_in, dy_out, routes, gates, w_down, w_qk, w_up, e_gate, e_up, e_down):
    links = Links()
    micro, _, length, width = x_in.shape
    rows = micro * length
    capacity = max(2, (3 * length + 2 * links.experts - 1) // (2 * links.experts))
    attn_w = (w_down[0], w_qk[0], w_up[0])
    first = links.section == 0

    route = routes[0, :, 0, :, 0]
    earlier = lax.broadcasted_iota(jnp.int32, (length, length), 0) > lax.broadcasted_iota(
        jnp.int32, (length, length), 1
    )
    same = route[:, :, None] == route[:, None, :]
    rank = jnp.sum((same & earlier).astype(jnp.int32), axis=2)
    slot = jnp.arange(micro, dtype=jnp.int32)[:, None] * capacity + rank
    position = (links.relative(route) * (micro * capacity) + slot).reshape(rows)
    pos_row, pos_col = position.reshape(1, rows), position.reshape(rows, 1)
    gate_col = gates[0, :, 0].reshape(rows, 1)
    slots = links.experts * micro * capacity
    blocks = (slots, micro * capacity if links.pairwise else slots)

    own = (e_gate[0, 0], e_up[0, 0], e_down[0, 0])
    packed = pack_weights(links, own, 1)
    dy = dy_out.reshape(rows, width)
    sent_1 = scatter(links, dy, gate_col, pos_row, blocks, 1)
    kept_0 = attend_forward(
        links, x_in.reshape(rows, width), micro, attn_w, pos_row, blocks, 0, as_list(sent_1)[:1]
    )
    rows_0 = links.exchange(kept_0.sent, 0)
    dm_1 = links.exchange(tied(as_list(sent_1), rows_0[1:]) if links.pairwise else sent_1, 1)
    again = pack_weights(links, own, 1, as_list(kept_0.sent)[:1], 0)
    set_0 = links.gather_quarters(packed + again, 0, hurry=True)
    onward = jnp.concatenate([pos_row.astype(F32), gate_col.reshape(1, rows)], axis=0)
    packed_1 = pack_weights(links, own, 2, as_list(dm_1), 1)
    near_0 = experts_call(links, nearer(set_0), 0, rows=rows_0, forward=True, last=False, later=packed_1[:1])
    onward = tied([onward], [near_0.total])[0]
    there = links.move(onward, (0,), section_bit=1)
    packed_1 = tied(packed_1, [there])
    onward = (there[:1].astype(jnp.int32), there[1].reshape(rows, 1), blocks)

    made_0 = experts_call(links, farthest(set_0), 0, rows=rows_0, forward=True, before=near_0.total, later=[there])
    pre_0 = [
        as_list(near_0.gate_out) + as_list(made_0.gate_out),
        as_list(near_0.up_out) + as_list(made_0.up_out),
    ]
    returned_0 = links.exchange(made_0.value, 0)
    out_0 = combine(links, kept_0.residual, returned_0, gate_col, pos_col, 0)
    h_1 = links.move(out_0, (0,), section_bit=1)
    kept_1 = attend_forward(links, h_1, micro, attn_w, pos_row, blocks, 1)
    sent = as_list(kept_1.sent)
    set_1 = links.gather_quarters(packed_1, 1, sent[:1], as_list(returned_0))
    if links.pairwise:
        sent = [sent[0], *tied(sent[1:], [set_1[0][1]])]
        rows_1 = links.exchange(sent, 1)
        early = factors(links, kept_0.inputs, [kept_0.mixed, kept_0.latent], 0, True)
        early = factors(
            links, h_1, [kept_1.mixed, kept_1.latent], 1, True, dict(packs=early), rows_1
        )
    else:
        rows_1 = links.exchange(kept_1.sent, 1)
    set_1 = [[mine] + got[1:] for mine, got in zip(packed, set_1)]
    near_1 = experts_call(links, nearer(set_1), 1, rows=rows_1, d_rows=dm_1, last=False)
    made_1 = experts_call(links, farthest(set_1), 1, rows=rows_1, d_rows=dm_1, before=near_1.total)
    hidden_1 = as_list(near_1.hidden_out) + as_list(made_1.hidden_out)
    back_1 = links.exchange(made_1.value, 1)
    if links.pairwise:
        late_1 = attend_backward(
            links, kept_1, micro, dy, back_1, attn_w, pos_col, 1, early[:1], onward=onward
        )
        dm_0 = links.exchange_over(late_1.sent, 1)
        u_0 = links.move(late_1.d_input, (1,), section_bit=1)
    else:
        late_1 = attend_backward(links, kept_1, micro, dy, back_1, attn_w, pos_col, 1)
        u_0 = links.move(late_1.d_input, (1,), section_bit=1)
        dm_0 = links.exchange(scatter(links, u_0, gate_col, pos_row, blocks, 0), 0)
    value_1 = experts_call(
        links,
        set_1,
        1,
        hidden=hidden_1,
        forward=True,
        block_rows=blocks[1],
        later=[late_1.d_latent],
    ).value
    if links.pairwise:
        value_1 = tied(value_1, dm_0[1:])
    returned_1 = links.exchange(value_1, 1)
    later = as_list(returned_1)
    back_0 = experts_call(links, set_0, 0, pre=pre_0, d_rows=dm_0, later=later).value
    merge = dict(d_input=late_1.d_input)
    if links.pairwise:
        narrow = [late_1.d_latent, late_1.d_queries]
        merge.update(packs=factors(links, late_1.d_res, narrow, 1, False, later=dm_0))
    late_0 = attend_backward(
        links, kept_0, micro, u_0, links.exchange(back_0, 0), attn_w, pos_col, 0, merge=merge
    )
    grads_in = late_0.d_input.reshape(1, micro, 1, length, width)
    activations = combine(
        links, kept_1.residual, returned_1, gate_col, pos_col, 1, dict(out=out_0)
    ).reshape(1, micro, 1, length, width)

    if links.pairwise:
        def plane(packs):
            return packs[:1] + [
                links.move(packs[k], links.every, quarter_bits=k) for k in range(1, links.quarters)
            ]

        g_down, g_qk, g_up_t = weight_gradients(links, plane(early), plane(late_0.packs), width)
    else:
        def pick(upper, lower):
            return jnp.where(first, upper, lower)

        def gathered(upper, lower):
            return lax.all_gather(pick(upper, lower), ("expert", "dp"), axis=0, tiled=True)

        g_down = t_times(
            spread(links, pick(kept_0.normed, kept_1.normed)),
            gathered(late_0.d_latent, late_1.d_latent),
        )
        g_qk = t_times(
            spread(links, pick(kept_0.latent, kept_1.latent)),
            gathered(late_0.d_queries, late_1.d_queries),
        )
        g_up_t = t_times(
            spread(links, pick(late_0.d_res, late_1.d_res)),
            gathered(kept_0.mixed, kept_1.mixed),
        )
    return (activations, grads_in, g_down[None], g_qk[None], g_up_t[None])


def solution(mesh):
    by_sequence = P(None, ("expert", "dp"), None, None)
    by_layer = P("section", None, ("expert", "dp"), None, None)
    shared = P("section", None, None)
    placed = (
        by_sequence,
        by_sequence,
        by_layer,
        by_layer,
        shared,
        shared,
        shared,
        P("section", "expert", None, "dp"),
        P("section", "expert", None, "dp"),
        P("section", "expert", "dp", None),
    )
    by_rows = P("section", ("expert", "dp"), None)
    return jax.shard_map(
        body,
        mesh=mesh,
        in_specs=placed,
        out_specs=(by_layer, by_layer, by_rows, by_rows, by_rows),
        check_vma=False,
    )
```

```python
from types import SimpleNamespace

import jax
import jax.numpy as jnp
from jax import lax
from jax.experimental import pallas as pl
from jax.experimental.pallas import tpu as pltpu
from jax.sharding import PartitionSpec as P

epsilon = 1e-06
AXES = ("section", "expert", "dp")
GRANT = (64 << 20) - (256 << 10)
ATTENTION = ("w_down", "w_qk", "w_up")
BF16, F32 = jnp.bfloat16, jnp.float32


def dot_f32(left, right):
    return jnp.dot(left, right, preferred_element_type=F32)


def times_t(left, right):
    return lax.dot_general(left, right, (((1,), (1,)), ((), ())), preferred_element_type=F32)


def t_times(left, right):
    return lax.dot_general(left, right, (((0,), (0,)), ((), ())), preferred_element_type=F32)


def inverse_rms(values):
    return lax.rsqrt(jnp.mean(values * values, axis=-1, keepdims=True) + epsilon)


def rms_back(normed, inv_rms, upstream):
    return inv_rms * (upstream - normed * jnp.mean(upstream * normed, axis=-1, keepdims=True))


def silu_parts(gate_pre):
    sigmoid = jax.nn.sigmoid(gate_pre)
    return (gate_pre * sigmoid, sigmoid * (1.0 + gate_pre * (1.0 - sigmoid)))


class Held:
    def __init__(self, refs, held, sems):
        self.held, self.parts, self.seen = held, [], set()
        start = 0
        for i, ref in enumerate(refs):
            target = held
            if len(refs) > 1:
                target = held.at[pl.ds(start, ref.shape[0])]
                start += ref.shape[0]
            self.parts.append((pltpu.make_async_copy(ref, target, sems.at[i]), target))

    def start(self, i):
        if i < len(self.parts):
            self.parts[i][0].start()

    def block(self, i):
        if i not in self.seen:
            self.seen.add(i)
            self.parts[i][0].wait()
        return self.parts[i][1]

    def all(self):
        for i in range(len(self.parts)):
            self.block(i)
        return self.held


class Made:
    def __init__(self, refs, held, sems):
        self.held, self.parts, self.sent = held, [], set()
        self.refs, self.pieces = refs, []
        start = 0
        for i, ref in enumerate(refs):
            source = held
            if len(refs) > 1:
                source = held.at[pl.ds(start, ref.shape[0])]
                start += ref.shape[0]
            self.parts.append((pltpu.make_async_copy(source, ref, sems.at[i]), source))

    def send(self, i=0):
        if i not in self.sent:
            self.sent.add(i)
            self.parts[i][0].start()

    def send_columns(self, columns, sems):
        for i, (_, source) in enumerate(self.parts):
            copy = pltpu.make_async_copy(source.at[:, columns], self.refs[i].at[:, columns], sems.at[i])
            copy.start()
            self.pieces.append(copy)

    def finish(self):
        for copy in self.pieces:
            copy.wait()
        if self.pieces:
            return
        for i in range(len(self.parts)):
            self.send(i)
        for copy, _ in self.parts:
            copy.wait()


def as_list(value):
    return list(value) if isinstance(value, (list, tuple)) else [value]


def stage_shape(arrays):
    if len(arrays) == 1:
        return pltpu.VMEM(arrays[0].shape, arrays[0].dtype)
    rows = sum(a.shape[0] for a in arrays)
    return pltpu.VMEM((rows, *arrays[0].shape[1:]), arrays[0].dtype)


def run(name, kernel, ins, outs, scratch=None, vmem=None, later=(), merge=None, only=None, place=None, raw=None, first=99, flops=0):
    scratch, vmem, merge, raw = scratch or {}, vmem or {}, merge or {}, raw or {}
    ins = {k: as_list(v) for k, v in ins.items()}
    outs = {k: as_list(v) for k, v in outs.items()}
    merge = {k: as_list(v) for k, v in merge.items()}
    flat_in = [a for v in ins.values() for a in v]
    flat_out = [a for v in outs.values() for a in v]
    flat_merge = [a for v in merge.values() for a in v]
    stages = [stage_shape(v) for v in [*ins.values(), *outs.values()]]
    sems = [pltpu.SemaphoreType.DMA((len(v),)) for v in [*ins.values(), *outs.values()]]
    smem = [] if place is None else [place]

    def body(*refs):
        refs = list(refs)

        def take(count):
            got = refs[:count]
            del refs[:count]
            return got

        place_refs, vmem_refs = take(len(smem)), take(len(vmem))
        in_refs = [take(len(v)) for v in ins.values()]
        instead = {k: take(len(v)) for k, v in merge.items()}
        raw_refs = {k: take(len(v)) for k, v in raw.items()}
        take(len(later))
        out_refs = [take(len(v)) for v in outs.values()]
        staged, signals = take(len(stages)), take(len(sems))
        r = SimpleNamespace(**dict(zip(vmem, vmem_refs)))
        if smem:
            r.place = place_refs[0]
        held = [Held(a, b, c) for a, b, c in zip(in_refs, staged, signals)]
        made = [Made(a, b, c) for a, b, c in zip(out_refs, staged[len(ins) :], signals[len(ins) :])]
        r.__dict__.update(zip(ins, held))
        r.__dict__.update(zip(outs, made))
        r.__dict__.update(zip(scratch, refs))

        r.__dict__.update(raw_refs)

        def open_all(part):
            for i in range(max([len(h.parts) for h in part], default=0)):
                for h in part:
                    h.start(i)

        r.open_rest = lambda: open_all(held[first:])

        def work():
            open_all(held[:first])
            if first >= len(held):
                r.open_rest()
            kernel(r)
            for h in held:
                h.all()
            for m in made:
                m.finish()

        def passed_on():
            for k, m, sem in zip(outs, made, signals[len(ins) :]):
                parts = list(zip(instead.get(k, ()), m.parts))
                loads = [
                    pltpu.make_async_copy(ref, part[1], sem.at[i]) for i, (ref, part) in enumerate(parts)
                ]
                for load in loads:
                    load.start()
                for load, (_, part) in zip(loads, parts):
                    load.wait()
                    part[0].start()
                for _, part in parts:
                    part[0].wait()

        if only is None:
            work()
        else:
            pl.when(r.place[2] == only)(work)
            if merge:
                pl.when(r.place[2] != only)(passed_on)

    flat_raw = [a for v in raw.values() for a in v]
    everything = [*smem, *vmem.values(), *flat_in, *flat_merge, *flat_raw, *later]
    spaces = [pltpu.SMEM] * len(smem) + [pltpu.VMEM] * len(vmem)
    spaces += [pltpu.HBM] * (len(everything) - len(spaces))
    got = pl.pallas_call(
        body,
        name=name,
        in_specs=[pl.BlockSpec(memory_space=s) for s in spaces],
        out_specs=[pl.BlockSpec(memory_space=pltpu.HBM) for _ in flat_out],
        out_shape=flat_out,
        scratch_shapes=[*stages, *sems, *scratch.values()],
        compiler_params=pltpu.CompilerParams(vmem_limit_bytes=GRANT),
        cost_estimate=pl.CostEstimate(
            flops=flops,
            bytes_accessed=sum(a.size * a.dtype.itemsize for a in flat_in) * 0,
            transcendentals=0,
        ),
    )(*everything)
    got, result = list(got), SimpleNamespace()
    for k, v in outs.items():
        part, got = got[: len(v)], got[len(v) :]
        setattr(result, k, part if len(part) > 1 else part[0])
    return result


def like(*shape, dtype=BF16):
    return jax.ShapeDtypeStruct(shape, dtype)


class Links:
    def __init__(self):
        self.sections, self.experts, self.quarters = [lax.axis_size(a) for a in AXES]
        self.section, self.expert, self.quarter = [lax.axis_index(a) for a in AXES]
        self.pairwise = self.experts <= 8
        self.every = tuple(range(self.sections))
        self.place = jnp.stack([self.expert, self.quarter, self.section])

    def move(self, x, sections, section_bit=0, expert_bits=0, quarter_bits=0):
        def number(s, e, d):
            return (s * self.experts + e) * self.quarters + d

        pairs = [
            (number(s, e, d), number(s ^ section_bit, e ^ expert_bits, d ^ quarter_bits))
            for s in sections
            for e in range(self.experts)
            for d in range(self.quarters)
        ]
        return lax.ppermute(x, AXES, pairs)

    def relative(self, expert):
        return expert ^ self.expert if self.pairwise else expert

    def exchange_over(self, blocks, section):
        got = {
            k: self.move(blocks[k], (section,), section_bit=1, expert_bits=k)
            for k in range(self.experts - 1, -1, -1)
        }
        return [got[k] for k in range(self.experts)]

    def exchange(self, blocks, section):
        if not self.pairwise:
            sent = blocks.reshape(self.experts, -1, blocks.shape[1])
            out = lax.all_to_all(sent, "expert", split_axis=0, concat_axis=0, tiled=True)
            return out.reshape(blocks.shape)
        got = {k: self.move(blocks[k], (section,), expert_bits=k) for k in range(self.experts - 1, 0, -1)}
        return [blocks[0]] + [got[k] for k in range(1, self.experts)]

    def gather_quarters(self, packs, section, before=(), between=(), hurry=False):
        if self.quarters != 4:
            return [
                [p] + [self.move(p, (section,), quarter_bits=k) for k in range(1, self.quarters)]
                for p in packs[:2]
            ]

        def across(one, two):
            return [
                self.move(one, (section,), quarter_bits=1),
                self.move(two, (section,), quarter_bits=2),
            ]

        step = across(packs[0], packs[1])
        again = tied(packs[2:], between) if between else packs[-2:]
        other = across(again[1], again[0])
        if not hurry:
            step = tied(step, [*other, *before])
        third = across(step[1], step[0])
        return [[packs[0], step[0], other[1], third[1]], [packs[1], other[0], step[1], third[0]]]


def tied(arrays, first):
    count = len(arrays)
    hbm = pl.BlockSpec(memory_space=pltpu.HBM)
    return list(
        pl.pallas_call(
            lambda *refs: None,
            name="tied",
            in_specs=[hbm] * (count + len(first)),
            out_specs=[hbm] * count,
            out_shape=[like(*a.shape, dtype=a.dtype) for a in arrays],
            input_output_aliases={i: i for i in range(count)},
            compiler_params=pltpu.CompilerParams(vmem_limit_bytes=GRANT),
        )(*arrays, *first)
    )


def attend_forward(links, inputs, micro, attn_w, pos_row, blocks, only, later=()):
    rows, width = inputs.shape
    length = rows // micro
    latent_width = attn_w[0].shape[1]
    slots, block_rows = blocks

    def kernel(r):
        h = r.h.all()[...].astype(F32)
        r.open_rest()
        normed_b = (h * inverse_rms(h)).astype(BF16)
        latent = dot_f32(normed_b, r.w_down.all()[...]).astype(BF16)
        queries = dot_f32(latent, r.w_qk.all()[...]).astype(BF16)
        r.latent.held[...] = latent
        r.queries.held[...] = queries
        causal = lax.broadcasted_iota(jnp.int32, (length, length), 0) >= lax.broadcasted_iota(
            jnp.int32, (length, length), 1
        )
        mixed = []
        for m in range(micro):
            part = slice(m * length, (m + 1) * length)
            scores = times_t(queries[part], latent[part]) * latent_width ** (-0.5)
            scores = jnp.where(causal, scores, -1e30)
            exponent = jnp.exp(scores - jnp.max(scores, axis=-1, keepdims=True))
            probs = exponent / jnp.sum(exponent, axis=-1, keepdims=True)
            r.probs.held[m] = probs
            mixed.append(dot_f32(probs.astype(BF16), latent[part]).astype(BF16))
        mixed = jnp.concatenate(mixed, axis=0)
        residual = (h + dot_f32(mixed, r.w_up.all()[...])).astype(BF16)
        r.residual.held[...] = residual
        r.residual.send()
        wide = residual.astype(F32)
        second_b = (wide * inverse_rms(wide)).astype(BF16)
        place_rows(r, r.pos_row.all()[...], second_b, slots, block_rows)
        r.mixed.held[...] = mixed
        if not links.pairwise:
            r.normed.held[...] = normed_b

    outs = dict(
        sent=[like(block_rows, width)] * (slots // block_rows),
        residual=like(rows, width),
        latent=like(rows, latent_width),
        queries=like(rows, latent_width),
        mixed=like(rows, latent_width),
        probs=like(micro, length, length, dtype=F32),
    )
    if not links.pairwise:
        outs.update(normed=like(rows, width))
    got = run(
        "attend_forward",
        kernel,
        dict(h=inputs, **dict(zip(ATTENTION, attn_w)), pos_row=pos_row),
        outs,
        first=2,
        later=later,
        only=only,
        place=links.place,
    )
    got.inputs = inputs
    return got


def factors(links, wide, narrow, only, normalize, merge=None, later=()):
    rows = wide.shape[0]
    latent_width = narrow[0].shape[1]

    def kernel(r):
        values = r.wide.all()[...]
        if normalize:
            h = values.astype(F32)
            values = (h * inverse_rms(h)).astype(BF16)
        pack_factors(links, r, values, [r.narrow.block(0)[...], r.narrow.block(1)[...]])

    return as_list(
        run(
            "factors",
            kernel,
            dict(wide=wide, narrow=narrow),
            dict(packs=pack_shapes(links, rows, latent_width)),
            pack_scratch(links, rows, latent_width),
            later=later,
            merge=merge,
            only=only,
            place=links.place,
        ).packs
    )


def place_rows(r, pos_row, values, slots, block_rows):
    shape = (slots, pos_row.shape[1])
    place = (pos_row == lax.broadcasted_iota(jnp.int32, shape, 0)).astype(BF16)
    for k in range(slots // block_rows):
        part = slice(k * block_rows, (k + 1) * block_rows)
        r.sent.held[part] = dot_f32(place[part], values).astype(BF16)
        r.sent.send(k)


def pack_shapes(links, rows, latent_width):
    return [like((links.experts + 2) * rows, latent_width)] * links.quarters


def pack_scratch(links, rows, latent_width):
    if not links.pairwise:
        return {}
    return dict(cols=pltpu.VMEM((links.experts * links.quarters, rows, latent_width), BF16))


def pack_factors(links, r, wide, narrow):
    rows, width = wide.shape
    experts, quarters = links.experts, links.quarters
    share = width // (experts * quarters)
    for i in range(experts * quarters):
        r.cols[i, :, :share] = wide[:, i * share : (i + 1) * share]
    expert, quarter = r.place[0], r.place[1]
    for k in range(quarters):
        out = r.packs.parts[k][1]
        for e in range(experts):
            out[e * rows : (e + 1) * rows] = r.cols[(expert ^ e) * quarters + (quarter ^ k)]
        for n, values in enumerate(narrow):
            out[(experts + n) * rows : (experts + n + 1) * rows] = values
        r.packs.send(k)


def picked_rows(r, rows):
    values = r.back.all()
    place = (
        r.pos_col.all()[...] == lax.broadcasted_iota(jnp.int32, (rows, values.shape[0]), 1)
    ).astype(BF16)
    return dot_f32(place, values[...])


def attend_backward(links, kept, micro, upstream, back, attn_w, pos_col, only, later=(), merge=None, onward=None):
    inputs = kept.inputs
    rows, width = inputs.shape
    length = rows // micro
    latent_width = attn_w[0].shape[1]
    packed = links.pairwise and not onward

    def kernel(r):
        r.back.all()
        r.open_rest()
        d_second = picked_rows(r, rows)
        u = r.u.all()[...].astype(F32)
        wide = r.residual.all()[...].astype(F32)
        inv = inverse_rms(wide)
        d_res = u + rms_back(wide * inv, inv, d_second)
        d_res_b = d_res.astype(BF16)
        d_mixed = times_t(d_res_b, r.w_up.all()[...]).astype(BF16)
        latent, queries, all_probs = r.latent.all()[...], r.queries.all()[...], r.probs.all()
        d_latent, d_queries = [], []
        for m in range(micro):
            part = slice(m * length, (m + 1) * length)
            probs = all_probs[m]
            d_probs = times_t(d_mixed[part], latent[part])
            d_scores = (
                probs
                * (d_probs - jnp.sum(d_probs * probs, axis=-1, keepdims=True))
                * latent_width ** (-0.5)
            ).astype(BF16)
            d_queries.append(dot_f32(d_scores, latent[part]).astype(BF16))
            d_latent.append(
                t_times(probs.astype(BF16), d_mixed[part]) + t_times(d_scores, queries[part])
            )
        d_queries = jnp.concatenate(d_queries, axis=0)
        d_latent = jnp.concatenate(d_latent, axis=0) + times_t(d_queries, r.w_qk.all()[...])
        d_latent = d_latent.astype(BF16)
        if packed:
            pack_factors(links, r, d_res_b, [d_latent, d_queries])
        else:
            r.d_res.held[...] = d_res_b
            r.d_res.send()
            r.d_latent.held[...] = d_latent
            r.d_queries.held[...] = d_queries
        d_normed = times_t(d_latent, r.w_down.all()[...])
        h = r.h.all()[...].astype(F32)
        inv = inverse_rms(h)
        d_input = (d_res + rms_back(h * inv, inv, d_normed)).astype(BF16)
        r.d_input.held[...] = d_input
        r.d_input.send()
        if onward:
            scaled = (d_input.astype(F32) * r.gate.all()[...]).astype(BF16)
            place_rows(r, r.pos_row.all()[...], scaled, slots, block_rows)

    outs = dict(d_input=like(rows, width))
    ins = {}
    if onward:
        ins, (slots, block_rows) = dict(pos_row=onward[0], gate=onward[1]), onward[2]
        outs.update(sent=[like(block_rows, width)] * (slots // block_rows))
    if packed:
        outs.update(packs=pack_shapes(links, rows, latent_width))
    else:
        outs.update(
            d_res=like(rows, width),
            d_latent=like(rows, latent_width),
            d_queries=like(rows, latent_width),
        )
    return run(
        "attend_backward",
        kernel,
        dict(
            back=back,
            pos_col=pos_col,
            u=upstream,
            residual=kept.residual,
            w_up=attn_w[2],
            latent=kept.latent,
            queries=kept.queries,
            probs=kept.probs,
            w_qk=attn_w[1],
            w_down=attn_w[0],
            h=inputs,
            **ins,
        ),
        outs,
        pack_scratch(links, rows, latent_width) if packed else None,
        first=4,
        later=later,
        merge=merge,
        only=only,
        place=links.place,
    )


def scatter(links, upstream, gate_col, pos_row, blocks, only, later=()):
    width = upstream.shape[1]
    slots, block_rows = blocks

    def kernel(r):
        scaled = (r.u.all()[...].astype(F32) * r.gate.all()[...]).astype(BF16)
        place_rows(r, r.pos_row.all()[...], scaled, slots, block_rows)

    ins = dict(u=upstream, gate=gate_col, pos_row=pos_row)
    outs = dict(sent=[like(block_rows, width)] * (slots // block_rows))
    return run("scatter", kernel, ins, outs, later=later, only=only, place=links.place).sent


def combine(links, residual, back, gate_col, pos_col, only, merge=None):
    rows, width = residual.shape

    def kernel(r):
        mixture = picked_rows(r, rows) * r.gate.all()[...]
        r.out.held[...] = (r.residual.all()[...].astype(F32) + mixture).astype(BF16)

    ins = dict(back=back, pos_col=pos_col, gate=gate_col, residual=residual)
    outs = dict(out=like(rows, width))
    return run("combine", kernel, ins, outs, merge=merge, only=only, place=links.place).out


def pack_weights(links, weights, copies, later=(), only=None):
    gate_w, up_w, down_w = weights
    width, split = gate_w.shape
    count = width // split
    half = count // 2
    shape = (width + half * split, split)

    def body(place, gate, up, down, *refs):
        *outs, held0, held1, sems, out_sems = refs[len(later) :]

        def copy_all():
            moves = []
            for source, held, first in ((gate, held0, 0), (up, held1, half)):
                part = [(source, held.at[pl.ds(0, width)])]
                for j in range(half):
                    columns = pl.ds((first + j) * split, split)
                    part.append((down.at[:, columns], held.at[pl.ds(width + j * split, split)]))
                moves.append(part)
            loads = [
                [pltpu.make_async_copy(a, b, sems.at[i, j]) for j, (a, b) in enumerate(part)]
                for i, part in enumerate(moves)
            ]
            for load in loads[0] + loads[1]:
                load.start()
            stores = []
            for i, held in enumerate((held0, held1)):
                for load in loads[i]:
                    load.wait()
                for k in range(i, 2 * copies, 2):
                    stores.append(pltpu.make_async_copy(held, outs[k], out_sems.at[k]))
                    stores[-1].start()
            for store in stores:
                store.wait()

        if only is None:
            copy_all()
        else:
            pl.when(place[2] == only)(copy_all)

    hbm = pl.BlockSpec(memory_space=pltpu.HBM)
    return list(
        pl.pallas_call(
            body,
            name="pack_weights",
            in_specs=[pl.BlockSpec(memory_space=pltpu.SMEM)] + [hbm] * (3 + len(later)),
            out_specs=[hbm] * (2 * copies),
            out_shape=[like(*shape)] * (2 * copies),
            scratch_shapes=[
                pltpu.VMEM(shape, BF16),
                pltpu.VMEM(shape, BF16),
                pltpu.SemaphoreType.DMA((2, half + 1)),
                pltpu.SemaphoreType.DMA((2 * copies,)),
            ],
            compiler_params=pltpu.CompilerParams(vmem_limit_bytes=GRANT),
        )(links.place, gate_w, up_w, down_w, *later)
    )


def experts_call(links, packs, only, rows=None, pre=None, hidden=None, d_rows=None, forward=False, block_rows=None, before=None, last=True, later=()):
    quarters = len(packs[0])
    split = packs[0][0].shape[1]
    backward = d_rows is not None
    sources = as_list(rows if rows is not None else d_rows) if hidden is None else []
    if hidden is None:
        block_rows, count = sources[0].shape[0], len(sources)
        width = sources[0].shape[1]
        slots = block_rows * count
    else:
        slots = hidden[0].shape[0]
        count = slots // block_rows
        width = 2 * packs[0][0].shape[0] // 3
    blocks = width // split
    half = blocks // 2

    step = 2 * split if width % (2 * split) == 0 else split
    steps = [slice(c, c + step) for c in range(0, width, step)]

    def kernel(r):
        def copies(q):
            wide, narrow = [], []
            for n, pack in enumerate((r.pack0[q], r.pack1[q])):
                if hidden is None:
                    wide.append((pack.at[pl.ds(0, width)], (r.all0, r.all1)[n].at[q]))
                for j in range(half):
                    target = r.all2.at[q, :, pl.ds((n * half + j) * split, split)]
                    narrow.append((pack.at[pl.ds(width + j * split, split)], target))
            found = wide + narrow if rows is not None else narrow + wide
            found = [pltpu.make_async_copy(a, b, r.sems.at[q, i]) for i, (a, b) in enumerate(found)]
            return (found[:2], found[2:]) if rows is not None else (found[: 2 * half], found[2 * half :])

        loads = [copies(q) for q in range(quarters)]
        def start(q):
            for copy in (*loads[q][0], *loads[q][1]):
                copy.start()

        def wait(part):
            for copy in part:
                copy.wait()

        start(0)
        r.open_rest()
        running = r.running if last else r.total.held

        def add(q, columns, part):
            part = part.astype(BF16).astype(F32)
            if q:
                part = part + running[:, columns]
            elif before is not None:
                part = part + r.before.all()[:, columns]
            if q == quarters - 1 and last:
                r.value.held[:, columns] = part.astype(BF16)
                piece = columns.start // step
                r.value.send_columns(pl.ds(columns.start, step), r.out_sems.at[piece])
            else:
                running[:, columns] = part

        for q in range(quarters):
            wait(loads[q][0])
            if q + 1 < quarters:
                start(q + 1)
            if rows is not None:
                held = r.rows.all()[...]
                gate_pre, up_pre = dot_f32(held, r.all0[q]), dot_f32(held, r.all1[q])
                if not backward:
                    r.gate_out.parts[q][1][...] = gate_pre
                    r.gate_out.send(q)
                    r.up_out.parts[q][1][...] = up_pre
                    r.up_out.send(q)
            elif pre is not None:
                gate_pre, up_pre = r.gate_pre.block(q)[...], r.up_pre.block(q)[...]
            if hidden is not None:
                hidden_q = r.hidden.block(q)[...]
            else:
                activated, slope = silu_parts(gate_pre)
            if rows is not None:
                hidden_q = (activated * up_pre).astype(BF16)
                if backward:
                    r.hidden_out.parts[q][1][...] = hidden_q
                    r.hidden_out.send(q)
            if rows is not None:
                wait(loads[q][1])
            if forward:
                for c in steps:
                    add(q, c, dot_f32(hidden_q, r.all2[q, :, c]))
            if backward:
                d_hidden = times_t(r.d_rows.all()[...], r.all2[q])
                if rows is None:
                    wait(loads[q][1])
                d_gate = (d_hidden * up_pre * slope).astype(BF16)
                d_up = (d_hidden * activated).astype(BF16)
                for c in steps:
                    add(q, c, times_t(d_gate, r.all0[q, c]) + times_t(d_up, r.all1[q, c]))

    ins = {}
    if rows is not None:
        ins.update(rows=rows)
    if backward:
        ins.update(d_rows=d_rows)
    if pre is not None:
        ins.update(gate_pre=pre[0], up_pre=pre[1])
    if hidden is not None:
        ins.update(hidden=hidden)
    if before is not None:
        ins.update(before=before)
    if last:
        outs = dict(value=[like(block_rows, width)] * count)
    else:
        outs = dict(total=like(slots, width, dtype=F32))
    if rows is not None and backward:
        outs.update(hidden_out=[like(slots, split)] * quarters)
    elif rows is not None:
        made = [like(slots, split, dtype=F32)] * quarters
        outs.update(gate_out=made, up_out=made)
    flops = 2 * slots * width * split * quarters * 0
    scratch = dict(
        all2=pltpu.VMEM((quarters, split, width), BF16),
        sems=pltpu.SemaphoreType.DMA((quarters, blocks + 2)),
    )
    if hidden is None:
        weights = pltpu.VMEM((quarters, width, split), BF16)
        scratch.update(all0=weights, all1=weights)
    if last:
        scratch.update(
            running=pltpu.VMEM((slots, width), F32),
            out_sems=pltpu.SemaphoreType.DMA((len(steps), count)),
        )
    return run(
        "experts",
        kernel,
        ins,
        outs,
        scratch,
        raw=dict(pack0=packs[0], pack1=packs[1]),
        first=2,
        later=later,
        flops=flops,
        only=only,
        place=links.place,
    )


def weight_gradients(links, early, late, width):
    experts, quarters = links.experts, links.quarters
    rows = early[0].shape[0] // (experts + 2)
    latent_width = early[0].shape[1]
    share, share_qk = width // (experts * quarters), latent_width // (experts * quarters)
    total = 2 * share + share_qk

    def plane_sums(r):
        def part(held, k, i, columns=latent_width):
            return held.block(k)[i * rows : (i + 1) * rows, :columns]

        sum_qk = jnp.zeros((latent_width, latent_width), F32)
        for k in range(quarters):
            sum_qk += t_times(part(r.early, k, experts + 1), part(r.late, k, experts + 1))
        r.qk[...] = sum_qk
        for e in range(experts):
            down = jnp.zeros((share, latent_width), F32)
            up = jnp.zeros((share, latent_width), F32)
            for k in range(quarters):
                down += t_times(part(r.early, k, e, share), part(r.late, k, experts))
                up += t_times(part(r.late, k, e, share), part(r.early, k, experts))
            at = pl.multiple_of(((r.place[0] ^ e) * quarters + r.place[1]) * share_qk, share_qk)
            made = r.away if e else r.own
            out = made.parts[max(e - 1, 0)][1]
            out[:share] = down.astype(out.dtype)
            out[share : 2 * share] = up.astype(out.dtype)
            out[2 * share :] = r.qk[pl.ds(at, share_qk)].astype(out.dtype)
            made.send(max(e - 1, 0))

    sums = run(
        "plane_sums",
        plane_sums,
        dict(early=early, late=late),
        dict(
            own=like(total, latent_width, dtype=F32),
            away=[like(total, latent_width)] * (experts - 1),
        ),
        dict(qk=pltpu.VMEM((latent_width, latent_width), F32)),
        place=links.place,
    )
    away = as_list(sums.away)
    got = [links.move(away[e - 1], links.every, expert_bits=e) for e in range(experts - 1, 0, -1)]

    value = sums.own + sum(g.astype(F32) for g in got)
    return value[:share], value[2 * share :], value[share : 2 * share]


def spread(links, rows):
    length, width = rows.shape
    count = links.experts * links.quarters
    by_owner = rows.reshape(length, count, width // count).transpose(1, 0, 2)
    got = lax.all_to_all(by_owner, ("expert", "dp"), split_axis=0, concat_axis=0, tiled=True)
    return got.reshape(count * length, width // count)


def nearer(packs):
    return [pack[:-1] for pack in packs]


def farthest(packs):
    return [pack[-1:] for pack in packs]


def body(x_in, dy_out, routes, gates, w_down, w_qk, w_up, e_gate, e_up, e_down):
    links = Links()
    micro, _, length, width = x_in.shape
    rows = micro * length
    capacity = max(2, (3 * length + 2 * links.experts - 1) // (2 * links.experts))
    attn_w = (w_down[0], w_qk[0], w_up[0])
    first = links.section == 0

    route = routes[0, :, 0, :, 0]
    earlier = lax.broadcasted_iota(jnp.int32, (length, length), 0) > lax.broadcasted_iota(
        jnp.int32, (length, length), 1
    )
    same = route[:, :, None] == route[:, None, :]
    rank = jnp.sum((same & earlier).astype(jnp.int32), axis=2)
    slot = jnp.arange(micro, dtype=jnp.int32)[:, None] * capacity + rank
    position = (links.relative(route) * (micro * capacity) + slot).reshape(rows)
    pos_row, pos_col = position.reshape(1, rows), position.reshape(rows, 1)
    gate_col = gates[0, :, 0].reshape(rows, 1)
    slots = links.experts * micro * capacity
    blocks = (slots, micro * capacity if links.pairwise else slots)

    own = (e_gate[0, 0], e_up[0, 0], e_down[0, 0])
    packed = pack_weights(links, own, 1)
    dy = dy_out.reshape(rows, width)
    sent_1 = scatter(links, dy, gate_col, pos_row, blocks, 1)
    kept_0 = attend_forward(
        links, x_in.reshape(rows, width), micro, attn_w, pos_row, blocks, 0, as_list(sent_1)[:1]
    )
    rows_0 = links.exchange(kept_0.sent, 0)
    dm_1 = links.exchange(tied(as_list(sent_1), rows_0[1:]) if links.pairwise else sent_1, 1)
    again = pack_weights(links, own, 1, as_list(kept_0.sent)[:1], 0)
    set_0 = links.gather_quarters(packed + again, 0, hurry=True)
    onward = jnp.concatenate([pos_row.astype(F32), gate_col.reshape(1, rows)], axis=0)
    packed_1 = pack_weights(links, own, 2, as_list(dm_1), 1)
    near_0 = experts_call(links, nearer(set_0), 0, rows=rows_0, forward=True, last=False, later=packed_1[:1])
    onward = tied([onward], [near_0.total])[0]
    there = links.move(onward, (0,), section_bit=1)
    packed_1 = tied(packed_1, [there])
    onward = (there[:1].astype(jnp.int32), there[1].reshape(rows, 1), blocks)

    made_0 = experts_call(links, farthest(set_0), 0, rows=rows_0, forward=True, before=near_0.total, later=[there])
    pre_0 = [
        as_list(near_0.gate_out) + as_list(made_0.gate_out),
        as_list(near_0.up_out) + as_list(made_0.up_out),
    ]
    returned_0 = links.exchange(made_0.value, 0)
    out_0 = combine(links, kept_0.residual, returned_0, gate_col, pos_col, 0)
    h_1 = links.move(out_0, (0,), section_bit=1)
    kept_1 = attend_forward(links, h_1, micro, attn_w, pos_row, blocks, 1)
    sent = as_list(kept_1.sent)
    set_1 = links.gather_quarters(packed_1, 1, sent[:1], as_list(returned_0))
    if links.pairwise:
        sent = [sent[0], *tied(sent[1:], [set_1[0][1]])]
        rows_1 = links.exchange(sent, 1)
        early = factors(links, kept_0.inputs, [kept_0.mixed, kept_0.latent], 0, True)
        early = factors(
            links, h_1, [kept_1.mixed, kept_1.latent], 1, True, dict(packs=early), rows_1
        )
    else:
        rows_1 = links.exchange(kept_1.sent, 1)
    set_1 = [[mine] + got[1:] for mine, got in zip(packed, set_1)]
    near_1 = experts_call(links, nearer(set_1), 1, rows=rows_1, d_rows=dm_1, last=False)
    made_1 = experts_call(links, farthest(set_1), 1, rows=rows_1, d_rows=dm_1, before=near_1.total)
    hidden_1 = as_list(near_1.hidden_out) + as_list(made_1.hidden_out)
    back_1 = links.exchange(made_1.value, 1)
    if links.pairwise:
        late_1 = attend_backward(
            links, kept_1, micro, dy, back_1, attn_w, pos_col, 1, early[:1], onward=onward
        )
        dm_0 = links.exchange_over(late_1.sent, 1)
        u_0 = links.move(late_1.d_input, (1,), section_bit=1)
    else:
        late_1 = attend_backward(links, kept_1, micro, dy, back_1, attn_w, pos_col, 1)
        u_0 = links.move(late_1.d_input, (1,), section_bit=1)
        dm_0 = links.exchange(scatter(links, u_0, gate_col, pos_row, blocks, 0), 0)
    value_1 = experts_call(
        links,
        set_1,
        1,
        hidden=hidden_1,
        forward=True,
        block_rows=blocks[1],
        later=[late_1.d_latent],
    ).value
    if links.pairwise:
        value_1 = tied(value_1, dm_0[3:])
    returned_1 = links.exchange(value_1, 1)
    later = as_list(returned_1)
    back_0 = experts_call(links, set_0, 0, pre=pre_0, d_rows=dm_0, later=later).value
    merge = dict(d_input=late_1.d_input)
    if links.pairwise:
        narrow = [late_1.d_latent, late_1.d_queries]
        merge.update(packs=factors(links, late_1.d_res, narrow, 1, False, later=dm_0))
    late_0 = attend_backward(
        links, kept_0, micro, u_0, links.exchange(back_0, 0), attn_w, pos_col, 0, merge=merge
    )
    grads_in = late_0.d_input.reshape(1, micro, 1, length, width)
    activations = combine(
        links, kept_1.residual, returned_1, gate_col, pos_col, 1, dict(out=out_0)
    ).reshape(1, micro, 1, length, width)

    if links.pairwise:
        def plane(packs):
            return packs[:1] + [
                links.move(packs[k], links.every, quarter_bits=k) for k in range(1, links.quarters)
            ]

        g_down, g_qk, g_up_t = weight_gradients(links, plane(early), plane(late_0.packs), width)
    else:
        def pick(upper, lower):
            return jnp.where(first, upper, lower)

        def gathered(upper, lower):
            return lax.all_gather(pick(upper, lower), ("expert", "dp"), axis=0, tiled=True)

        g_down = t_times(
            spread(links, pick(kept_0.normed, kept_1.normed)),
            gathered(late_0.d_latent, late_1.d_latent),
        )
        g_qk = t_times(
            spread(links, pick(kept_0.latent, kept_1.latent)),
            gathered(late_0.d_queries, late_1.d_queries),
        )
        g_up_t = t_times(
            spread(links, pick(late_0.d_res, late_1.d_res)),
            gathered(kept_0.mixed, kept_1.mixed),
        )
    return (activations, grads_in, g_down[None], g_qk[None], g_up_t[None])


def solution(mesh):
    by_sequence = P(None, ("expert", "dp"), None, None)
    by_layer = P("section", None, ("expert", "dp"), None, None)
    shared = P("section", None, None)
    placed = (
        by_sequence,
        by_sequence,
        by_layer,
        by_layer,
        shared,
        shared,
        shared,
        P("section", "expert", None, "dp"),
        P("section", "expert", None, "dp"),
        P("section", "expert", "dp", None),
    )
    by_rows = P("section", ("expert", "dp"), None)
    return jax.shard_map(
        body,
        mesh=mesh,
        in_specs=placed,
        out_specs=(by_layer, by_layer, by_rows, by_rows, by_rows),
        check_vma=False,
    )
```
